32 devices in a mesh: seq: 16 (over z, y, x), head: 2 (over core).
Axes of the slice: x: 2, y: 2, z: 4, core: 2. Of those that a mesh axis runs over, the one named last changes fastest.
Arguments:
- layer_input: bfloat16 [4, 2, 1024, 768], P(None, None, 'seq'), may hold values from -6 to 6
- block_sizes: int32 [4], replicated, may hold values from 4 to 16, as said below
- mixing_gain: float32 [768], replicated, may hold values from 0.5 to 1.5
- mixing_shift: float32 [768], replicated, may hold values from -2 to 2
- w_heads: bfloat16 [3, 768, 768], P(None, None, 'head'), may hold values from -0.21875 to 0.21875
- w_output: bfloat16 [768, 768], P('head'), may hold values from -6 to 6
- feed_gain: float32 [768], replicated, may hold values from 0.5 to 1.5
- feed_shift: float32 [768], replicated, may hold values from -2 to 2
- w_up: bfloat16 [768, 3072], P(None, 'head'), may hold values from -0.21875 to 0.21875
- bias_up: float32 [3072], P('head'), may hold values from -3 to 3
- w_down: bfloat16 [3072, 768], P('head'), may hold values from -0.109375 to 0.109375
- bias_down: float32 [768], replicated, may hold values from -2 to 2
- cotangent: bfloat16 [4, 2, 1024, 768], P(None, None, 'seq'), may hold values from -6 to 6
Outputs:
- layer_output: bfloat16 [4, 2, 1024, 768], P(None, None, 'seq')
- input_grad: float32 [4, 2, 1024, 768], P(None, None, 'seq')
- grad_heads: float32 [3, 768, 768], P(None, None, 'head')
- grad_output: float32 [768, 768], P('head')
- grad_up: float32 [768, 3072], P(None, 'head')
- grad_bias_up: float32 [3072], P('head')
- grad_down: float32 [3072, 768], P('head')
- grad_bias_down: float32 [768], replicated
- grad_mixing_gain: float32 [768], replicated
- grad_mixing_shift: float32 [768], replicated
- grad_feed_gain: float32 [768], replicated
- grad_feed_shift: float32 [768], replicated
The draws below stay inside these ranges and needn't reach their ends.
Inputs may be any that keep to these rules, and one draw needn't show every extreme that they name: `block_sizes`: each example's block size is 4, 8 or 16, and every draw holds all three.
All inputs are finite; a program needn't handle non-finite values.
Results may differ from the reference program's by a relative error of at most 0.02.
Values may be sent and summed in bfloat16 or wider, within the bound.
A program may use at most 256 MiB of HBM per device.

```python
import math
import jax
import jax.numpy as jnp
from jax import lax

D = 768
HEADS = 12
HD = 64
FF = 3072
MICRO = 4
LENGTH = 1024


def draw_block_sizes(key, part):
    key = jax.random.fold_in(key, 7)
    extra_key, order_key = jax.random.split(key)
    extra = jax.random.randint(extra_key, (MICRO - 3,), 0, 3).astype(jnp.int32)
    powers = jnp.concatenate([jnp.arange(3, dtype=jnp.int32), extra])
    powers = jax.random.permutation(order_key, powers)
    return jnp.where(powers == 0, 4, jnp.where(powers == 1, 8, 16)).astype(jnp.int32)


def shard_levels(key, extent, shards, smallest, largest):
    level = 1.0
    for position, blocks in shards:
        draws = jax.random.uniform(jax.random.fold_in(jax.random.fold_in(key, 6), position), (blocks,), jnp.float32, smallest / len(shards), largest / len(shards))
        level = level * jnp.repeat(jnp.exp(draws), extent[position] // blocks).reshape((-1,) + (1,) * (len(extent) - 1 - position))
    return level


def normal_values(key, extent, scale, bound, pieces=(), held_as=jnp.bfloat16):
    gain = shard_levels(key, extent, pieces, -0.22, 0.18) if pieces else 1.0
    drawn = jax.random.normal(key, extent, jnp.float32) * scale * gain
    return jnp.minimum(jnp.maximum(drawn, -bound), bound).astype(held_as)


def setup_inputs(seed: int = 0) -> dict:
    splits = jax.random.split(jax.random.key(seed), 14)
    return {
        "layer_input": normal_values(splits[0], (MICRO, 2, LENGTH, D), 1.0, 6.0, ((2, 16),)),
        "block_sizes": draw_block_sizes(jax.random.fold_in(splits[13], 71), 0),
        "mixing_gain": jnp.clip(1.0 + 0.1 * jax.random.normal(splits[2], (D,), jnp.float32), 0.5, 1.5),
        "mixing_shift": normal_values(splits[3], (D,), 0.3, 2.0, (), jnp.float32),
        "w_heads": normal_values(splits[4], (3, D, D), D ** -0.5, 0.21875, ((2, 2),)),
        "w_output": normal_values(splits[5], (D, D), 1.2, 6.0, ((0, 2),)),
        "feed_gain": jnp.clip(1.0 + 0.1 * jax.random.normal(splits[6], (D,), jnp.float32), 0.5, 1.5),
        "feed_shift": normal_values(splits[7], (D,), 0.3, 2.0, (), jnp.float32),
        "w_up": normal_values(splits[8], (D, FF), D ** -0.5, 0.21875, ((1, 2),)),
        "bias_up": normal_values(splits[9], (FF,), 0.5, 3.0, ((0, 2),), jnp.float32),
        "w_down": normal_values(splits[10], (FF, D), FF ** -0.5, 0.109375, ((0, 2),)),
        "bias_down": normal_values(splits[11], (D,), 0.3, 2.0, (), jnp.float32),
        "cotangent": normal_values(splits[12], (MICRO, 2, LENGTH, D), 1.0, 6.0, ((2, 16),)),
    }


@jax.custom_vjp
def low(v):
    return lax.optimization_barrier(v.astype(jnp.bfloat16)).astype(jnp.float32)

@jax.custom_vjp
def low_back(v):
    return v

def low_keep(v):
    return (low(v), None)

def low_pass(kept, grad):
    return (grad,)

def back_keep(v):
    return (v, None)

def back_low(kept, grad):
    return (low(grad),)
low.defvjp(low_keep, low_pass)
low_back.defvjp(back_keep, back_low)
neg_large = -1e+30
norm_eps = 1e-05
rotary_base = 10000.0
highest = lax.Precision.HIGHEST

def layer_norm(inputs, norm_gain, norm_shift):
    center = lax.optimization_barrier(jnp.mean(inputs, axis=-1, keepdims=True))
    offsets = inputs - center
    spread = lax.optimization_barrier(jnp.mean(offsets * offsets, axis=-1, keepdims=True))
    return offsets * lax.rsqrt(spread + norm_eps) * norm_gain + norm_shift

def gelu_tanh(pre_values):
    return jax.nn.gelu(pre_values, approximate=True)

def rotary_tables(positions, head_size):
    halves = head_size // 2
    frequency = jnp.exp(jnp.arange(halves, dtype=jnp.float32) * (-math.log(rotary_base) / halves))
    angles = positions.astype(jnp.float32)[:, None] * frequency[None, :]
    return (jnp.cos(angles), jnp.sin(angles))

def rotate(vectors, cos_table, sin_table):
    halves = vectors.shape[-1] // 2
    front_half = vectors[..., :halves]
    back_half = vectors[..., halves:]
    cos_wide = cos_table[:, None, :]
    sin_wide = sin_table[:, None, :]
    return jnp.concatenate([front_half * cos_wide - back_half * sin_wide, back_half * cos_wide + front_half * sin_wide], axis=-1)

def attend_rows(query_part, query_blocks, query_clean, keys_rot, values_all, key_blocks, key_clean):
    score_scale = 1.0 / math.sqrt(HD)
    scores = low_back(jnp.einsum('qhd,khd->hqk', query_part, keys_rot, precision=highest) * score_scale)
    clean_ok = key_clean[None, :] & (key_blocks[None, :] <= query_blocks[:, None])
    noisy_ok = jnp.where(key_clean[None, :], key_blocks[None, :] < query_blocks[:, None], key_blocks[None, :] == query_blocks[:, None])
    allowed = jnp.where(query_clean[:, None], clean_ok, noisy_ok)
    masked = jnp.where(allowed[None], scores, neg_large)
    log_totals = jax.nn.logsumexp(masked, axis=-1, keepdims=True)
    softmaxed = low(jnp.exp(masked - log_totals))
    return jnp.einsum('hqk,khd->qhd', softmaxed, values_all, precision=highest)

def forward(layer_input, mixing_gain, mixing_shift, w_heads, w_output, feed_gain, feed_shift, w_up, bias_up, w_down, bias_down, block_sizes):
    seq_len = layer_input.shape[2]
    positions = jnp.arange(seq_len, dtype=jnp.int32)
    row_positions = jnp.concatenate([positions, positions])
    row_clean = jnp.arange(2 * seq_len, dtype=jnp.int32) >= seq_len
    cos_table, sin_table = rotary_tables(row_positions, HD)
    block_total = 2 * seq_len // 512
    results = []
    for micro_index in range(layer_input.shape[0]):
        inputs = layer_input[micro_index].reshape(2 * seq_len, D)
        normed_one = low(layer_norm(inputs, mixing_gain, mixing_shift))
        projected = jnp.einsum('rd,kdc->krc', normed_one, w_heads, precision=highest)
        query_pre = low_back(projected[0]).reshape(2 * seq_len, HEADS, HD)
        key_pre = low_back(projected[1]).reshape(2 * seq_len, HEADS, HD)
        values_all = low_back(low(projected[2])).reshape(2 * seq_len, HEADS, HD)
        queries = low(rotate(query_pre, cos_table, sin_table))
        keys_rot = low(rotate(key_pre, cos_table, sin_table))
        row_blocks = row_positions // block_sizes[micro_index]

        def query_block(parts):
            query_part, block_part, clean_part = parts
            return attend_rows(query_part, block_part, clean_part, keys_rot, values_all, row_blocks, row_clean)
        attended = lax.map(jax.checkpoint(query_block), (queries.reshape(block_total, 512, HEADS, HD), row_blocks.reshape(block_total, 512), row_clean.reshape(block_total, 512)))
        attended = low_back(low(attended.reshape(2 * seq_len, D)))
        mixed = low_back(jnp.dot(attended, w_output, precision=highest, preferred_element_type=jnp.float32))
        middle = inputs + mixed
        normed_two = low(layer_norm(middle, feed_gain, feed_shift))
        hidden_pre = low_back(jnp.dot(normed_two, w_up, precision=highest, preferred_element_type=jnp.float32) + bias_up)
        hidden = low(gelu_tanh(hidden_pre))
        result = middle + jnp.dot(hidden, w_down, precision=highest, preferred_element_type=jnp.float32) + bias_down
        results.append(result.reshape(2, seq_len, D))
    return jnp.stack(results)

def reference(layer_input, block_sizes, mixing_gain, mixing_shift, w_heads, w_output, feed_gain, feed_shift, w_up, bias_up, w_down, bias_down, cotangent):

    def forward_fixed(input_f, gain_one, shift_one, heads_f, output_f, gain_two, shift_two, up_f, bias_up_f, down_f, bias_down_f):
        return forward(input_f, gain_one, shift_one, heads_f, output_f, gain_two, shift_two, up_f, bias_up_f, down_f, bias_down_f, block_sizes)
    result, pull = jax.vjp(forward_fixed, layer_input.astype(jnp.float32), mixing_gain.astype(jnp.float32), mixing_shift.astype(jnp.float32), w_heads.astype(jnp.float32), w_output.astype(jnp.float32), feed_gain.astype(jnp.float32), feed_shift.astype(jnp.float32), w_up.astype(jnp.float32), bias_up.astype(jnp.float32), w_down.astype(jnp.float32), bias_down.astype(jnp.float32))
    grads = pull(cotangent.astype(jnp.float32))
    return (result.astype(jnp.bfloat16), grads[0], grads[3], grads[4], grads[7], grads[8], grads[9], grads[10], grads[1], grads[2], grads[5], grads[6])
```

```python
import functools
import math

import jax
import jax.numpy as jnp
from jax import lax
from jax.experimental import pallas as pl
from jax.experimental.pallas import tpu as pltpu
from jax.sharding import PartitionSpec as P

HD = 64
LANES = 128
NEG = -1e30
EPS = 1e-05
ROTARY_BASE = 10000.0
GELU_A = math.sqrt(2.0 / math.pi)
GELU_B = 0.044715
MESH = pl.DeviceIdType.MESH
F32 = jnp.float32
BF16 = jnp.bfloat16
WIDE = 256
VMEM_BYTES = 66_000_000


def nn(a, b):
    return lax.dot_general(a, b, (((1,), (0,)), ((), ())), preferred_element_type=F32)


def nt(a, b):
    return lax.dot_general(a, b, (((1,), (1,)), ((), ())), preferred_element_type=F32)


def tn(a, b):
    return lax.dot_general(a, b, (((0,), (0,)), ((), ())), preferred_element_type=F32)


def lane_swap(a):
    lane = lax.broadcasted_iota(jnp.int32, a.shape, 1)
    ahead = pltpu.roll(a, LANES - HD // 2, 1)
    behind = pltpu.roll(a, HD // 2, 1)
    return jnp.where(lane % HD < HD // 2, ahead, behind)


def stack_heads(a):
    lane = lax.broadcasted_iota(jnp.int32, a.shape, 1)
    zero = jnp.zeros_like(a)
    return jnp.concatenate([jnp.where(lane < HD, a, zero), jnp.where(lane >= HD, a, zero)], axis=0)


def merge_heads(a):
    half = a.shape[1] // 2
    sub = lax.broadcasted_iota(jnp.int32, (a.shape[0], half), 0)
    return jnp.where(sub < HD, a[:, :half], a[:, half:])


def fused(dims, *refs):
    n, groups, span, width, head_width, hidden = dims
    (
        x_in, c_in, wh_in, wo_in, wu_in, wd_in, blocks, gain_one, shift_one, gain_two, shift_two,
        bias_up, bias_down, cos_t, sin_t,
        y_out, ig_out, down_out, up_out, heads_out, wout_out, small_out,
        wh, wo, wu, wd, xb, dyb, n1, n2, qs, dos, kv, kvn, dkv, rkv, dkvn, lses, deltas, att, att_f,
        middle, hid, gpre, send_h, recv_h, grad_mid, dq_t,
        acc, arr, small, small_r,
        w_sem, x_send, x_recv, c_send, c_recv, kv_send, kv_recv, h_send, h_recv, g_send, g_recv,
        y_send, y_recv, i_send, i_recv, ar_send, ar_recv, ar_free, sm_send, sm_recv, out_sem,
    ) = refs
    inner = n // groups
    pairs = head_width // LANES
    chunk = 2 * span
    rows = groups * chunk
    stack = 2 * chunk
    key_ranks = min(inner, max(1, WIDE // span))
    key_blocks = inner // key_ranks
    half_rows = rows // 2
    col_tiles = width // LANES
    bits = int(math.log2(n))
    scale = 1.0 / math.sqrt(HD)

    me = lax.axis_index("seq")
    core = lax.axis_index("head")
    group = me // inner
    rank = me % inner

    def peer(seq_index):
        return (seq_index, core)

    sibling = (me, 1 - core)

    def group_peer(step):
        return (group + step) % groups

    def plane_peer(step):
        return (rank + step) % inner

    def remote(src, dst, ssem, rsem, where):
        return pltpu.make_async_remote_copy(
            src_ref=src, dst_ref=dst, send_sem=ssem, recv_sem=rsem, device_id=where, device_id_type=MESH
        )

    barrier = pltpu.get_barrier_semaphore()
    for step in range(1, groups):
        pl.semaphore_signal(barrier, inc=1, device_id=peer(group_peer(step) * inner + rank), device_id_type=MESH)
    for step in range(1, inner):
        pl.semaphore_signal(barrier, inc=1, device_id=peer(group * inner + plane_peer(step)), device_id_type=MESH)
    pl.semaphore_signal(barrier, inc=1, device_id=sibling, device_id_type=MESH)
    weight_copies = [
        pltpu.make_async_copy(wh_in, wh, w_sem.at[0]),
        pltpu.make_async_copy(wo_in, wo, w_sem.at[1]),
        pltpu.make_async_copy(wu_in, wu, w_sem.at[2]),
        pltpu.make_async_copy(wd_in, wd, w_sem.at[3]),
    ]
    own_x = pltpu.make_async_copy(x_in.at[group], xb.at[group], w_sem.at[4])
    own_c = pltpu.make_async_copy(c_in.at[group], dyb.at[group], w_sem.at[5])
    own_x.start()
    weight_copies[0].start()
    pl.semaphore_wait(barrier, groups + inner - 1)

    x_copies, c_copies = [], []
    for step in range(1, groups):
        to = group_peer(step)
        x_copies.append(remote(x_in.at[to], xb.at[group], x_send.at[step], x_recv.at[step], peer(to * inner + rank)))
        c_copies.append(remote(c_in.at[to], dyb.at[group], c_send.at[step], c_recv.at[step], peer(to * inner + rank)))
    for copy in x_copies:
        copy.start()
    for copy in c_copies:
        copy.start()
    for copy in weight_copies[1:]:
        copy.start()
    own_c.start()

    size_b = blocks[group]
    lane_q = lax.broadcasted_iota(jnp.int32, (1, stack), 1)
    in_chunk = lane_q % chunk
    clean_q = in_chunk >= span
    start_q = (in_chunk % span) & (-size_b)
    limit_q = start_q + jnp.where(clean_q, size_b, 0)

    def norm_stats(x):
        center = jnp.mean(x, axis=-1, keepdims=True)
        off = x - center
        inv = lax.rsqrt(jnp.mean(off * off, axis=-1, keepdims=True) + EPS)
        return off * inv, inv

    kv_copies = []

    def project(index):
        x = xb[index].astype(F32)
        hat, _ = norm_stats(x)
        normed = (hat * gain_one[...] + shift_one[...]).astype(BF16)
        n1[pl.ds(pl.multiple_of(index * chunk, chunk), chunk), :] = normed
        slot = index * inner + rank
        cos = cos_t[index]
        sin = sin_t[index]
        cos2 = jnp.concatenate([cos, cos], axis=0)
        sin2 = jnp.concatenate([sin, sin], axis=0)
        at_q = pl.ds(pl.multiple_of(index * stack, stack), stack)
        for kind in range(3):
            out = nn(normed, wh[kind])
            for p in range(pairs):
                part = out[:, p * LANES:(p + 1) * LANES]
                if kind < 2:
                    part = part * cos2 + lane_swap(part) * sin2
                if kind == 0:
                    part = part * scale
                low = part.astype(BF16)
                if kind == 0:
                    qs[p, at_q, :] = stack_heads(low)
                else:
                    where = (kind - 1) * pairs + p
                    kvn[index, where] = low[:span]
                    kv[slot, where] = low[span:]

    for step in range(groups):
        index = group_peer(groups - step) if step else group
        if step == 0:
            own_x.wait()
            weight_copies[0].wait()
        else:
            x_copies[step - 1].wait_recv()
        project(index)
        slot = index * inner + rank
        for near in range(1, inner):
            copy = remote(
                kv.at[slot], kv.at[slot], kv_send.at[index, near], kv_recv.at[index, near],
                peer(group * inner + plane_peer(near)),
            )
            copy.start()

    def kv_wait(index):
        for near in range(1, inner):
            source = index * inner + plane_peer(inner - near)
            remote(
                kv.at[source], kv.at[source], kv_send.at[index, near], kv_recv.at[index, near],
                peer(group * inner + plane_peer(near)),
            ).wait()

    def clean_mask(index, first_rank, count, shape):
        key = lax.broadcasted_iota(jnp.int32, shape, 0) + first_rank * span
        return key < limit_q + rank * span

    def noisy_mask(shape):
        key = lax.broadcasted_iota(jnp.int32, shape, 0) & (-size_b)
        return (key == start_q) & jnp.logical_not(clean_q)

    def head_send(piece, value, which):
        send_h[which % 3, piece * half_rows:(piece + 1) * half_rows, :] = value.astype(BF16)
        copy = head_copy(piece, which)
        copy.start()

    def head_copy(piece, which):
        at = pl.ds(piece * half_rows, half_rows)
        return remote(
            send_h.at[which % 3, at], recv_h.at[which % 3, at], h_send.at[which, piece], h_recv.at[which, piece], sibling
        )

    for index in range(groups):
        kv_wait(index)

        def attend(p, carry, index=index):
            q = qs[p, index * stack:(index + 1) * stack, :]
            pieces = []
            top = None
            for g in range(index + 1):
                keys = kv[g * inner:(g + 1) * inner, p].reshape(inner * span, LANES)
                s = nt(keys, q)
                if g == index:
                    s = jnp.where(clean_mask(index, 0, inner, s.shape), s, NEG)
                pieces.append(s)
                best = jnp.max(s, axis=0, keepdims=True)
                top = best if top is None else jnp.maximum(top, best)
            s = nt(kvn[index, p], q)
            s = jnp.where(noisy_mask(s.shape), s, NEG)
            top = jnp.maximum(top, jnp.max(s, axis=0, keepdims=True))
            e = jnp.exp(s - top)
            total = jnp.sum(e, axis=0, keepdims=True)
            out = tn(kvn[index, pairs + p], e.astype(BF16))
            for g in range(index + 1):
                e = jnp.exp(pieces[g] - top)
                total = total + jnp.sum(e, axis=0, keepdims=True)
                vals = kv[g * inner:(g + 1) * inner, pairs + p].reshape(inner * span, LANES)
                out = out + tn(vals, e.astype(BF16))
            lses[p, :, index * stack:(index + 1) * stack] = top + jnp.log(total)
            rows_out = jnp.transpose(merge_heads(out / total))
            att_f[p, index * chunk:(index + 1) * chunk, :] = rows_out
            at = pl.ds(pl.multiple_of(p * LANES, LANES), LANES)
            att[index * chunk:(index + 1) * chunk, at] = rows_out.astype(BF16)
            return carry

        lax.fori_loop(0, pairs, attend, 0)
        if index == 0:
            weight_copies[1].wait()
        if index % (groups // 2) == groups // 2 - 1:
            piece = index // (groups // 2)
            head_send(piece, nn(att[piece * half_rows:(piece + 1) * half_rows, :], wo[...]), 0)

    def chunk_rows(z):
        return pl.ds(pl.multiple_of(z * chunk, chunk), chunk)

    def second_norm(z, carry):
        at = chunk_rows(z)
        mid = xb[z].astype(F32) + (send_h[0, at, :].astype(F32) + recv_h[0, at, :].astype(F32))
        middle[at, :] = mid
        hat, _ = norm_stats(mid)
        n2[at, :] = (hat * gain_two[...] + shift_two[...]).astype(BF16)
        return carry

    for piece in range(2):
        head_copy(piece, 0).wait()
        lax.fori_loop(piece * groups // 2, (piece + 1) * groups // 2, second_norm, 0)

    weight_copies[2].wait()
    weight_copies[3].wait()
    own_c.wait()
    for copy in c_copies:
        copy.wait_recv()

    up_bias_rows = hidden // WIDE
    small[...] = jnp.zeros_like(small)

    def feed(i, carry):
        cols = pl.ds(pl.multiple_of(i * WIDE, WIDE), WIDE)
        bias = bias_up[pl.ds(i, 1), :]
        sums = jnp.zeros((1, WIDE), F32)
        for part in range(2):
            lo = part * half_rows
            v = nn(n2[lo:lo + half_rows, :], wu[:, cols]) + bias
            dy = dyb[part * groups // 2:(part + 1) * groups // 2].reshape(half_rows, width)
            back = nt(dy, wd[cols, :])
            sq = v * v
            t = jnp.tanh(GELU_A * v * (1.0 + GELU_B * sq))
            half = 0.5 * (1.0 + t)
            hid[lo:lo + half_rows, cols] = (v * half).astype(BF16)
            slope = half + 0.5 * v * (1.0 - t * t) * (GELU_A * (1.0 + 3.0 * GELU_B * sq))
            low = (back * slope).astype(BF16)
            gpre[lo:lo + half_rows, cols] = low
            sums = sums + jnp.sum(low.astype(F32), axis=0, keepdims=True)
        small[pl.ds(i, 1), :] = sums
        dy = dyb[...].reshape(rows, width)
        down = tn(hid[:, cols], dy)
        for c in range(col_tiles):
            at = pl.ds(pl.multiple_of(c * hidden + i * WIDE, WIDE), WIDE)
            acc[0, at, :] = down[:, c * LANES:(c + 1) * LANES].astype(BF16)
        up = tn(n2[...], gpre[:, cols])
        for c in range(WIDE // LANES):
            at = pl.ds(pl.multiple_of((i * (WIDE // LANES) + c) * width, width), width)
            acc[1, at, :] = up[:, c * LANES:(c + 1) * LANES].astype(BF16)
        return carry

    lax.fori_loop(0, up_bias_rows, feed, 0)

    acc_rows = acc.shape[1]
    seg = acc_rows // n
    seg_a = max(16, (seg * 5 // 12 + 8) // 16 * 16)
    seg_sizes = [seg_a, seg_a, seg - 2 * seg_a]
    low_bits = int(math.log2(inner))
    orders = [
        list(range(bits)),
        [1, 0] + list(range(2, bits)),
        list(range(low_bits, bits)) + list(range(low_bits)),
    ]

    def bit_of(bit):
        return (me // (1 << bit)) % 2

    def partner(bit):
        return peer(me + (1 - 2 * bit_of(bit)) * (1 << bit))

    def sum_job(job, part):
        base = n * sum(seg_sizes[:part])
        s = seg_sizes[part]
        order = orders[part]
        lo = 0
        size = n

        def at(ref, first, count):
            return ref.at[job, pl.ds(pl.multiple_of(base + first * s, 16), count * s)]

        for k, bit in enumerate(order):
            half = size // 2
            mine = lo + bit_of(bit) * half
            other = lo + (1 - bit_of(bit)) * half
            copy = remote(
                at(acc, other, half), at(arr, n - size, half),
                ar_send.at[job, part, k], ar_recv.at[job, part, k], partner(bit),
            )
            copy.start()
            yield
            copy.wait()
            pl.semaphore_signal(ar_free.at[job, part, k], inc=1, device_id=partner(bit), device_id_type=MESH)
            step_rows = s

            def add(i, carry, mine=mine, size=size):
                to = pl.ds(pl.multiple_of(base + mine * s + i * step_rows, 16), step_rows)
                frm = pl.ds(pl.multiple_of(base + (n - size) * s + i * step_rows, 16), step_rows)
                acc[job, to, :] = (acc[job, to, :].astype(F32) + arr[job, frm, :].astype(F32)).astype(BF16)
                return carry

            lax.fori_loop(0, half, add, 0)
            lo, size = mine, half
        for k, bit in reversed(list(enumerate(order))):
            pl.semaphore_wait(ar_free.at[job, part, k], 1)
            copy = remote(
                at(acc, lo, size), at(acc, lo, size),
                ar_send.at[job, part, bits + k], ar_recv.at[job, part, bits + k], partner(bit),
            )
            copy.start()
            yield
            copy.wait()
            lo = lo - bit_of(bit) * size
            size = size * 2

    def tick(jobs):
        for job in jobs:
            next(job, None)

    feed_jobs = [sum_job(job, part) for part in range(3) for job in range(2)]
    tick(feed_jobs)

    for piece in range(2):
        lo = piece * half_rows
        head_send(piece, nt(gpre[lo:lo + half_rows, :], wu[...]), 1)
    for piece in range(2):
        lo = piece * half_rows
        head_send(piece, nn(hid[lo:lo + half_rows, :], wd[...]), 2)

    def norm_back(hat, inv, gain, upstream):
        scaled = upstream * gain
        first = jnp.mean(scaled, axis=-1, keepdims=True)
        second = jnp.mean(scaled * hat, axis=-1, keepdims=True)
        return inv * (scaled - first - hat * second)

    def second_back(z, carry):
        gain_sum, shift_sum, bias_sum = carry
        at = chunk_rows(z)
        upstream = send_h[1, at, :].astype(F32) + recv_h[1, at, :].astype(F32)
        hat, inv = norm_stats(middle[at, :])
        dy = dyb[z].astype(F32)
        total = dy + norm_back(hat, inv, gain_two[...], upstream)
        grad_mid[at, :] = total
        n2[at, :] = total.astype(BF16)
        gain_sum = gain_sum + jnp.sum(upstream * hat, axis=0, keepdims=True)
        shift_sum = shift_sum + jnp.sum(upstream, axis=0, keepdims=True)
        bias_sum = bias_sum + jnp.sum(dy, axis=0, keepdims=True)
        return gain_sum, shift_sum, bias_sum

    zero_row = jnp.zeros((1, width), F32)
    sums = (zero_row, zero_row, zero_row)
    for piece in range(2):
        head_copy(piece, 1).wait()
        sums = lax.fori_loop(piece * groups // 2, (piece + 1) * groups // 2, second_back, sums)

    def keep_small(which, row):
        for c in range(width // WIDE):
            at = up_bias_rows + which * (width // WIDE) + c
            small[at:at + 1, :] = row[:, c * WIDE:(c + 1) * WIDE]

    keep_small(0, sums[2])
    keep_small(3, sums[0])
    keep_small(4, sums[1])

    def attended_back(z, carry):
        at = chunk_rows(z)
        back = nt(n2[at, :], wo[...])
        at_q = pl.ds(pl.multiple_of(z * stack, stack), stack)
        for p in range(pairs):
            low = back[:, p * LANES:(p + 1) * LANES].astype(BF16)
            dos[p, at_q, :] = stack_heads(low)
            prod = jnp.transpose(low.astype(F32) * att_f[p, at, :])
            d0 = jnp.sum(prod[:HD], axis=0, keepdims=True)
            d1 = jnp.sum(prod[HD:], axis=0, keepdims=True)
            deltas[p, :, at_q] = jnp.concatenate([d0, d1], axis=1)
        return carry

    lax.fori_loop(0, groups, attended_back, 0)
    tick(feed_jobs)

    def noisy_back(p, carry):
        for index in range(groups):
            at = slice(index * stack, (index + 1) * stack)
            q = qs[p, at, :]
            do = dos[p, at, :]
            keys = kvn[index, p]
            s = nt(keys, q)
            s = jnp.where(noisy_mask(s.shape), s, NEG)
            e = jnp.exp(s - lses[p, :, at])
            dp = nt(kvn[index, pairs + p], do)
            ds = (e * (dp - deltas[p, :, at])).astype(BF16)
            dkvn[index, pairs + p] = nn(e.astype(BF16), do)
            dkvn[index, p] = nn(ds, q)
            dq_t[p, :, at] = tn(keys, ds)
        return carry

    lax.fori_loop(0, pairs, noisy_back, 0)

    def grad_copy(index, near):
        dest = plane_peer(near)
        return remote(
            dkv.at[index * inner + dest], rkv.at[index, near - 1], g_send.at[index, near], g_recv.at[index, near],
            peer(group * inner + dest),
        )

    for index in range(groups):
        for block in range(key_blocks):
            first = index * inner + block * key_ranks

            def clean_back(p, carry, index=index, block=block, first=first):
                at = slice(index * stack, groups * stack)
                q = qs[p, at, :]
                do = dos[p, at, :]
                keys = kv[first:first + key_ranks, p].reshape(key_ranks * span, LANES)
                vals = kv[first:first + key_ranks, pairs + p].reshape(key_ranks * span, LANES)
                s = nt(keys, q)
                own = s[:, :stack]
                own = jnp.where(clean_mask(index, block * key_ranks, key_ranks, own.shape), own, NEG)
                if index < groups - 1:
                    s = jnp.concatenate([own, s[:, stack:]], axis=1)
                else:
                    s = own
                e = jnp.exp(s - lses[p, :, at])
                dp = nt(vals, do)
                ds = (e * (dp - deltas[p, :, at])).astype(BF16)
                dv = nn(e.astype(BF16), do).astype(BF16)
                dk = nn(ds, q).astype(BF16)
                dkv[first:first + key_ranks, p] = dk.reshape(key_ranks, span, LANES)
                dkv[first:first + key_ranks, pairs + p] = dv.reshape(key_ranks, span, LANES)
                dq_t[p, :, at] += tn(keys, ds)
                return carry

            lax.fori_loop(0, pairs, clean_back, 0)
        for near in range(1, inner):
            grad_copy(index, near).start()
        tick(feed_jobs)

    def feed_out(z, carry):
        at = chunk_rows(z)
        fed = send_h[2, at, :].astype(F32) + recv_h[2, at, :].astype(F32)
        dyb[z] = (middle[at, :] + fed + bias_down[...]).astype(BF16)
        return carry

    for piece in range(2):
        head_copy(piece, 2).wait()
    lax.fori_loop(0, groups, feed_out, 0)

    def spread(buf, out, ssem, rsem):
        copies = [pltpu.make_async_copy(buf.at[group], out.at[group], ssem.at[0])]
        for step in range(1, groups):
            to = group_peer(step)
            copies.append(remote(buf.at[to], out.at[group], ssem.at[step], rsem.at[step], peer(to * inner + rank)))
        for copy in copies:
            copy.start()
        return copies

    y_copies = spread(dyb, y_out, y_send, y_recv)

    out_base = 3 * pairs * width
    wout = tn(att[...], n2[...])
    for c in range(col_tiles):
        acc[2, out_base + c * head_width:out_base + (c + 1) * head_width, :] = wout[:, c * LANES:(c + 1) * LANES].astype(BF16)

    for index in range(groups):
        for near in range(1, inner):
            grad_copy(index, near).wait()

    def pre_grads(index, carry):
        cos = cos_t[index]
        sin = sin_t[index]
        cos2 = jnp.concatenate([cos, cos], axis=0)
        sin2 = jnp.concatenate([sin, sin], axis=0)
        at = chunk_rows(index)
        at_q = pl.ds(pl.multiple_of(index * stack, stack), stack)
        slot = index * inner + rank
        for p in range(pairs):
            gq = jnp.transpose(merge_heads(dq_t[p, :, at_q])) * scale
            gq = gq * cos2 - lane_swap(gq) * sin2
            gpre[at, p * LANES:(p + 1) * LANES] = gq.astype(BF16)
            for kind in range(2):
                which = kind * pairs + p
                total = dkv[slot, which].astype(F32)
                for near in range(inner - 1):
                    total = total + rkv[index, near, which].astype(F32)
                g = jnp.concatenate([dkvn[index, which], total], axis=0)
                if kind == 0:
                    g = g * cos2 - lane_swap(g) * sin2
                col = (kind + 1) * head_width + p * LANES
                gpre[at, col:col + LANES] = g.astype(BF16)
        return carry

    lax.fori_loop(0, groups, pre_grads, 0)

    for piece in range(2):
        lo = piece * half_rows
        back = nt(gpre[lo:lo + half_rows, :head_width], wh[0])
        back = back + nt(gpre[lo:lo + half_rows, head_width:2 * head_width], wh[1])
        back = back + nt(gpre[lo:lo + half_rows, 2 * head_width:3 * head_width], wh[2])
        head_send(piece, back, 3)

    for kind in range(3):
        part = tn(n1[...], gpre[:, kind * head_width:(kind + 1) * head_width])
        for p in range(pairs):
            at = (kind * pairs + p) * width
            acc[2, at:at + width, :] = part[:, p * LANES:(p + 1) * LANES].astype(BF16)
    tick(feed_jobs)
    head_jobs = [sum_job(2, part) for part in range(3)]
    tick(head_jobs)

    def first_back(z, carry):
        gain_sum, shift_sum = carry
        at = chunk_rows(z)
        upstream = send_h[0, at, :].astype(F32) + recv_h[0, at, :].astype(F32)
        hat, inv = norm_stats(xb[z].astype(F32))
        dyb[z] = (grad_mid[at, :] + norm_back(hat, inv, gain_one[...], upstream)).astype(BF16)
        gain_sum = gain_sum + jnp.sum(upstream * hat, axis=0, keepdims=True)
        shift_sum = shift_sum + jnp.sum(upstream, axis=0, keepdims=True)
        return gain_sum, shift_sum

    for copy in y_copies:
        copy.wait()
    sums = (zero_row, zero_row)
    for piece in range(2):
        head_copy(piece, 3).wait()
        sums = lax.fori_loop(piece * groups // 2, (piece + 1) * groups // 2, first_back, sums)
    ig_copies = spread(dyb, ig_out, i_send, i_recv)
    keep_small(1, sums[0])
    keep_small(2, sums[1])

    def small_job():
        for bit in range(bits):
            copy = remote(small.at[...], small_r.at[bit], sm_send.at[bit], sm_recv.at[bit], partner(bit))
            copy.start()
            yield
            copy.wait()
            small[...] = small[...] + small_r[bit]

    last = [small_job()]
    all_jobs = feed_jobs + head_jobs + last
    for _ in range(2 * bits + 1):
        tick(all_jobs)
    small_out[...] = small[...]

    outs = []
    for c in range(col_tiles):
        at = slice(c * LANES, (c + 1) * LANES)
        outs.append((acc.at[0, pl.ds(c * hidden, hidden)], down_out.at[:, at]))
    for c in range(hidden // LANES):
        at = slice(c * LANES, (c + 1) * LANES)
        outs.append((acc.at[1, pl.ds(c * width, width)], up_out.at[:, at]))
    for kind in range(3):
        for p in range(pairs):
            at = slice(p * LANES, (p + 1) * LANES)
            outs.append((acc.at[2, pl.ds((kind * pairs + p) * width, width)], heads_out.at[kind, :, at]))
    for c in range(col_tiles):
        at = slice(c * LANES, (c + 1) * LANES)
        outs.append((acc.at[2, pl.ds(out_base + c * head_width, head_width)], wout_out.at[:, at]))
    copies = [pltpu.make_async_copy(src, dst, out_sem.at[i]) for i, (src, dst) in enumerate(outs)]
    for copy in copies:
        copy.start()
    for copy in x_copies + c_copies:
        copy.wait_send()
    for copy in ig_copies:
        copy.wait()
    for copy in copies:
        copy.wait()


def local(
    layer_input, block_sizes, mixing_gain, mixing_shift, w_heads, w_output, feed_gain, feed_shift,
    w_up, bias_up, w_down, bias_down, cotangent,
):
    groups, _, span, width = layer_input.shape
    n = lax.axis_size("seq")
    head_width = w_heads.shape[2]
    hidden = w_up.shape[1]
    inner = n // groups
    pairs = head_width // LANES
    chunk = 2 * span
    rows = groups * chunk
    stack = 2 * chunk
    rank = lax.axis_index("seq") % inner
    bits = int(math.log2(n))

    first = (jnp.arange(groups, dtype=jnp.int32) * inner + rank) * span
    positions = (first[:, None] + jnp.arange(span, dtype=jnp.int32)[None, :]).astype(F32)
    lane = jnp.arange(LANES, dtype=jnp.int32)
    half = HD // 2
    frequency = jnp.exp((lane % half).astype(F32) * (-math.log(ROTARY_BASE) / half))
    angles = positions[:, :, None] * frequency[None, None, :]
    cos_t = jnp.cos(angles)
    sin_t = jnp.sin(angles) * jnp.where(lane % HD < half, -1.0, 1.0).astype(F32)

    acc_rows = hidden * width // LANES
    small_rows = (hidden // WIDE + 5 * (width // WIDE) + 7) // 8 * 8
    out_copies = width // LANES + hidden // LANES + 3 * pairs + width // LANES
    anywhere = pl.BlockSpec(memory_space=pl.ANY)
    vmem = pl.BlockSpec(memory_space=pltpu.VMEM)
    dma = pltpu.SemaphoreType.DMA
    scratch = [
        pltpu.VMEM((3, width, head_width), BF16),
        pltpu.VMEM((head_width, width), BF16),
        pltpu.VMEM((width, hidden), BF16),
        pltpu.VMEM((hidden, width), BF16),
        pltpu.VMEM((groups, chunk, width), BF16),
        pltpu.VMEM((groups, chunk, width), BF16),
        pltpu.VMEM((rows, width), BF16),
        pltpu.VMEM((rows, width), BF16),
        pltpu.VMEM((pairs, groups * stack, LANES), BF16),
        pltpu.VMEM((pairs, groups * stack, LANES), BF16),
        pltpu.VMEM((n, 2 * pairs, span, LANES), BF16),
        pltpu.VMEM((groups, 2 * pairs, span, LANES), BF16),
        pltpu.VMEM((n, 2 * pairs, span, LANES), BF16),
        pltpu.VMEM((groups, inner - 1, 2 * pairs, span, LANES), BF16),
        pltpu.VMEM((groups, 2 * pairs, span, LANES), F32),
        pltpu.VMEM((pairs, 1, groups * stack), F32),
        pltpu.VMEM((pairs, 1, groups * stack), F32),
        pltpu.VMEM((rows, head_width), BF16),
        pltpu.VMEM((pairs, rows, LANES), F32),
        pltpu.VMEM((rows, width), F32),
        pltpu.VMEM((rows, hidden), BF16),
        pltpu.VMEM((rows, hidden), BF16),
        pltpu.VMEM((3, rows, width), BF16),
        pltpu.VMEM((3, rows, width), BF16),
        pltpu.VMEM((rows, width), F32),
        pltpu.VMEM((pairs, LANES, groups * stack), F32),
        pltpu.VMEM((3, acc_rows, LANES), BF16),
        pltpu.VMEM((3, acc_rows, LANES), BF16),
        pltpu.VMEM((small_rows, WIDE), F32),
        pltpu.VMEM((bits, small_rows, WIDE), F32),
        dma((6,)),
        dma((groups,)), dma((groups,)), dma((groups,)), dma((groups,)),
        dma((groups, inner)), dma((groups, inner)),
        dma((4, 2)), dma((4, 2)),
        dma((groups, inner)), dma((groups, inner)),
        dma((groups,)), dma((groups,)), dma((groups,)), dma((groups,)),
        dma((3, 3, 2 * bits)), dma((3, 3, 2 * bits)), pltpu.SemaphoreType.REGULAR((3, 3, bits)),
        dma((bits,)), dma((bits,)),
        dma((out_copies,)),
    ]
    out_shape = (
        jax.ShapeDtypeStruct((groups, chunk, width), BF16),
        jax.ShapeDtypeStruct((groups, chunk, width), BF16),
        jax.ShapeDtypeStruct((hidden, width), BF16),
        jax.ShapeDtypeStruct((width, hidden), BF16),
        jax.ShapeDtypeStruct((3, width, head_width), BF16),
        jax.ShapeDtypeStruct((head_width, width), BF16),
        jax.ShapeDtypeStruct((small_rows, WIDE), F32),
    )
    y, ig, down, up, heads, wout, small = pl.pallas_call(
        functools.partial(fused, (n, groups, span, width, head_width, hidden)),
        out_shape=out_shape,
        in_specs=[anywhere] * 6 + [pl.BlockSpec(memory_space=pltpu.SMEM)] + [vmem] * 8,
        out_specs=(anywhere,) * 6 + (vmem,),
        scratch_shapes=scratch,
        compiler_params=pltpu.CompilerParams(
            collective_id=0, has_side_effects=True, vmem_limit_bytes=VMEM_BYTES
        ),
    )(
        layer_input.reshape(groups, chunk, width),
        cotangent.reshape(groups, chunk, width),
        w_heads, w_output, w_up, w_down, block_sizes,
        mixing_gain[None], mixing_shift[None], feed_gain[None], feed_shift[None],
        bias_up.reshape(hidden // WIDE, WIDE), bias_down[None], cos_t, sin_t,
    )
    up_rows = hidden // WIDE
    per = width // WIDE

    def vector(i):
        return small[up_rows + i * per:up_rows + (i + 1) * per].reshape(width)

    full = (groups, 2, span, width)
    return (
        y.reshape(full),
        ig.astype(F32).reshape(full),
        heads.astype(F32),
        wout.astype(F32),
        up.astype(F32),
        small[:up_rows].reshape(hidden),
        down.astype(F32),
        vector(0),
        vector(1),
        vector(2),
        vector(3),
        vector(4),
    )


def solution(mesh):
    in_specs = (
        P(None, None, "seq", None), P(), P(), P(), P(None, None, "head"), P("head", None), P(), P(),
        P(None, "head"), P("head"), P("head", None), P(), P(None, None, "seq", None),
    )
    out_specs = (
        P(None, None, "seq", None), P(None, None, "seq", None), P(None, None, "head"), P("head", None),
        P(None, "head"), P("head"), P("head", None), P(), P(), P(), P(), P(),
    )
    return jax.shard_map(local, mesh=mesh, in_specs=in_specs, out_specs=out_specs, check_vma=False)
```

```python
import functools
import math

import jax
import jax.numpy as jnp
from jax import lax
from jax.experimental import pallas as pl
from jax.experimental.pallas import tpu as pltpu
from jax.sharding import PartitionSpec as P

HD = 64
LANES = 128
NEG = -1e30
EPS = 1e-05
ROTARY_BASE = 10000.0
GELU_A = math.sqrt(2.0 / math.pi)
GELU_B = 0.044715
MESH = pl.DeviceIdType.MESH
F32 = jnp.float32
BF16 = jnp.bfloat16
WIDE = 256
VMEM_BYTES = 66_000_000


def nn(a, b):
    return lax.dot_general(a, b, (((1,), (0,)), ((), ())), preferred_element_type=F32)


def nt(a, b):
    return lax.dot_general(a, b, (((1,), (1,)), ((), ())), preferred_element_type=F32)


def tn(a, b):
    return lax.dot_general(a, b, (((0,), (0,)), ((), ())), preferred_element_type=F32)


def lane_swap(a):
    lane = lax.broadcasted_iota(jnp.int32, a.shape, 1)
    ahead = pltpu.roll(a, LANES - HD // 2, 1)
    behind = pltpu.roll(a, HD // 2, 1)
    return jnp.where(lane % HD < HD // 2, ahead, behind)


def stack_heads(a):
    lane = lax.broadcasted_iota(jnp.int32, a.shape, 1)
    zero = jnp.zeros_like(a)
    return jnp.concatenate([jnp.where(lane < HD, a, zero), jnp.where(lane >= HD, a, zero)], axis=0)


def merge_heads(a):
    half = a.shape[1] // 2
    sub = lax.broadcasted_iota(jnp.int32, (a.shape[0], half), 0)
    return jnp.where(sub < HD, a[:, :half], a[:, half:])


def job_layout(n, width, head_width, hidden):
    whole = [hidden * width // LANES] * 2 + [2 * head_width * width // LANES] * 2
    padded = [-(-count // (16 * n)) * 16 * n for count in whole]
    return padded, [sum(padded[:i]) for i in range(len(padded) + 1)]


def fused(dims, *refs):
    n, groups, span, width, head_width, hidden = dims
    (
        x_in, c_in, wh_in, wo_in, wu_in, wd_in, blocks,
        gain_one_in, shift_one_in, gain_two_in, shift_two_in, bias_up_in, bias_down_in,
        y_out, ig_out, down_out, up_out, heads_out, wout_out, small_out,
        wh, wo, wu, wd, xb, dyb, n1, n2, qs, dos, kv, kvn, dkv, rkv, dkvn, lses, deltas, att, att_f,
        middle, hid, gpre, send_h, recv_h, grad_mid, dq_t,
        acc, arr, small, small_r, cos_t, sin_t, bias_rows, vectors,
        w_sem, x_send, x_recv, c_send, c_recv, xf_send, xf_recv, cf_send, cf_recv, kv_send, kv_recv, h_send, h_recv, g_send, g_recv,
        y_send, y_recv, i_send, i_recv, yf_send, yf_recv, if_send, if_recv, ar_send, ar_recv, ar_free, sm_send, sm_recv, out_sem,
    ) = refs
    inner = n // groups
    job_rows, bases = job_layout(n, width, head_width, hidden)
    pairs = head_width // LANES
    chunk = 2 * span
    rows = groups * chunk
    stack = 2 * chunk
    key_ranks = min(inner, max(1, WIDE // span))
    key_blocks = inner // key_ranks
    half_rows = rows // 2
    col_tiles = width // LANES
    bits = int(math.log2(n))
    scale = 1.0 / math.sqrt(HD)
    up_bias_rows = hidden // WIDE
    gain_one, shift_one, gain_two, shift_two, bias_down = (vectors.at[i:i + 1, :] for i in range(5))

    me = lax.axis_index("seq")
    core = lax.axis_index("head")
    group = me // inner
    rank = me % inner

    def peer(seq_index):
        return (seq_index, core)

    sibling = (me, 1 - core)

    def group_peer(step):
        return (group + step) % groups

    def plane_peer(step):
        return (rank + step) % inner

    def remote(src, dst, ssem, rsem, where):
        return pltpu.make_async_remote_copy(
            src_ref=src, dst_ref=dst, send_sem=ssem, recv_sem=rsem, device_id=where, device_id_type=MESH
        )

    barrier = pltpu.get_barrier_semaphore()
    for step in range(1, groups):
        pl.semaphore_signal(barrier, inc=1, device_id=peer(group_peer(step) * inner + rank), device_id_type=MESH)
    for step in range(1, inner):
        pl.semaphore_signal(barrier, inc=1, device_id=peer(group * inner + plane_peer(step)), device_id_type=MESH)
    pl.semaphore_signal(barrier, inc=1, device_id=sibling, device_id_type=MESH)
    weight_copies = [
        pltpu.make_async_copy(wh_in, wh, w_sem.at[0]),
        pltpu.make_async_copy(wo_in, wo, w_sem.at[1]),
        pltpu.make_async_copy(wu_in, wu, w_sem.at[2]),
        pltpu.make_async_copy(wd_in, wd, w_sem.at[3]),
    ]
    own_x = pltpu.make_async_copy(x_in.at[group], xb.at[group], w_sem.at[4])
    own_c = pltpu.make_async_copy(c_in.at[group], dyb.at[group], w_sem.at[5])
    own_x.start()
    weight_copies[0].start()
    pl.semaphore_wait(barrier, groups + inner - 1)

    x_copies, c_copies, x_passes, c_passes = [], [], [], []
    share = pl.ds(pl.multiple_of(core * span, span), span)
    for step in range(1, groups):
        to = group_peer(step)
        source = group_peer(groups - step)
        where = peer(to * inner + rank)
        x_copies.append(
            remote(x_in.at[to, share], xb.at[group, share], x_send.at[step], x_recv.at[step], where)
        )
        c_copies.append(
            remote(c_in.at[to, share], dyb.at[group, share], c_send.at[step], c_recv.at[step], where)
        )
        x_passes.append(
            remote(xb.at[source, share], xb.at[source, share], xf_send.at[step], xf_recv.at[step], sibling)
        )
        c_passes.append(
            remote(dyb.at[source, share], dyb.at[source, share], cf_send.at[step], cf_recv.at[step], sibling)
        )
    for copy in x_copies:
        copy.start()
    for copy in weight_copies[1:]:
        copy.start()
    own_c.start()

    size_b = blocks[group]
    lane_q = lax.broadcasted_iota(jnp.int32, (1, stack), 1)
    in_chunk = lane_q % chunk
    clean_q = in_chunk >= span
    start_q = (in_chunk % span) & (-size_b)
    limit_q = start_q + jnp.where(clean_q, size_b, 0)

    def norm_stats(x):
        center = jnp.mean(x, axis=-1, keepdims=True)
        off = x - center
        inv = lax.rsqrt(jnp.mean(off * off, axis=-1, keepdims=True) + EPS)
        return off * inv, inv

    for row in range(up_bias_rows):
        bias_rows[row:row + 1, :] = bias_up_in[row * WIDE:(row + 1) * WIDE].reshape(1, WIDE)
    for row, vector in enumerate((gain_one_in, shift_one_in, gain_two_in, shift_two_in, bias_down_in)):
        vectors[row:row + 1, :] = vector[...].reshape(1, width)

    half_head = HD // 2
    lane = lax.broadcasted_iota(jnp.int32, (1, LANES), 1)
    frequency = jnp.exp((lane % half_head).astype(F32) * (-math.log(ROTARY_BASE) / half_head))
    sign = jnp.where(lane % HD < half_head, -1.0, 1.0)
    for index in range(groups):
        start = (index * inner + rank) * span
        position = lax.broadcasted_iota(jnp.int32, (span, LANES), 0) + start
        angle = position.astype(F32) * frequency
        cos_t[index] = jnp.cos(angle)
        sin_t[index] = jnp.sin(angle) * sign


    def project(index):
        x = xb[index].astype(F32)
        hat, _ = norm_stats(x)
        normed = (hat * gain_one[...] + shift_one[...]).astype(BF16)
        n1[pl.ds(pl.multiple_of(index * chunk, chunk), chunk), :] = normed
        slot = index * inner + rank
        cos = cos_t[index]
        sin = sin_t[index]
        cos2 = jnp.concatenate([cos, cos], axis=0)
        sin2 = jnp.concatenate([sin, sin], axis=0)
        at_q = pl.ds(pl.multiple_of(index * stack, stack), stack)
        for kind in range(3):
            out = nn(normed, wh[kind])
            for p in range(pairs):
                part = out[:, p * LANES:(p + 1) * LANES]
                if kind < 2:
                    part = part * cos2 + lane_swap(part) * sin2
                if kind == 0:
                    part = part * scale
                low = part.astype(BF16)
                if kind == 0:
                    qs[p, at_q, :] = stack_heads(low)
                else:
                    where = (kind - 1) * pairs + p
                    kvn[index, where] = low[:span]
                    kv[slot, where] = low[span:]

    for step in range(groups):
        index = group_peer(groups - step) if step else group
        if step == 0:
            own_x.wait()
            weight_copies[0].wait()
        else:
            x_passes[step - 1].wait()
        project(index)
        if step == 0:
            for copy, onward in zip(x_copies, x_passes):
                copy.wait_recv()
                onward.start()
            for copy in c_copies:
                copy.start()
        slot = index * inner + rank
        for near in range(1, inner):
            copy = remote(
                kv.at[slot], kv.at[slot], kv_send.at[index, near], kv_recv.at[index, near],
                peer(group * inner + plane_peer(near)),
            )
            copy.start()

    def kv_wait(index):
        for near in range(1, inner):
            source = index * inner + plane_peer(inner - near)
            remote(
                kv.at[source], kv.at[source], kv_send.at[index, near], kv_recv.at[index, near],
                peer(group * inner + plane_peer(near)),
            ).wait()

    def clean_mask(index, first_rank, count, shape):
        key = lax.broadcasted_iota(jnp.int32, shape, 0) + first_rank * span
        return key < limit_q + rank * span

    def noisy_mask(shape):
        key = lax.broadcasted_iota(jnp.int32, shape, 0) & (-size_b)
        return (key == start_q) & jnp.logical_not(clean_q)

    own_c.wait()
    for copy, onward in zip(c_copies, c_passes):
        copy.wait_recv()
        onward.start()
    weight_copies[2].wait()
    weight_copies[3].wait()
    for copy in c_passes:
        copy.wait()

    def feed_back(i, carry):
        cols = pl.ds(pl.multiple_of(i * WIDE, WIDE), WIDE)
        gpre[:, cols] = nt(dyb[...].reshape(rows, width), wd[cols, :]).astype(BF16)
        return carry

    lax.fori_loop(0, up_bias_rows, feed_back, 0)

    def head_send(piece, value, which):
        send_h[which % 3, piece * half_rows:(piece + 1) * half_rows, :] = value.astype(BF16)
        copy = head_copy(piece, which)
        copy.start()

    def head_copy(piece, which):
        at = pl.ds(piece * half_rows, half_rows)
        return remote(
            send_h.at[which % 3, at], recv_h.at[which % 3, at], h_send.at[which, piece], h_recv.at[which, piece], sibling
        )

    for index in range(groups):
        kv_wait(index)

        def attend(p, carry, index=index):
            q = qs[p, index * stack:(index + 1) * stack, :]
            pieces = []
            top = None
            for g in range(index + 1):
                keys = kv[g * inner:(g + 1) * inner, p].reshape(inner * span, LANES)
                s = nt(keys, q)
                if g == index:
                    s = jnp.where(clean_mask(index, 0, inner, s.shape), s, NEG)
                pieces.append(s)
                best = jnp.max(s, axis=0, keepdims=True)
                top = best if top is None else jnp.maximum(top, best)
            s = nt(kvn[index, p], q)
            s = jnp.where(noisy_mask(s.shape), s, NEG)
            top = jnp.maximum(top, jnp.max(s, axis=0, keepdims=True))
            e = jnp.exp(s - top)
            total = jnp.sum(e, axis=0, keepdims=True)
            out = tn(kvn[index, pairs + p], e.astype(BF16))
            for g in range(index + 1):
                e = jnp.exp(pieces[g] - top)
                total = total + jnp.sum(e, axis=0, keepdims=True)
                vals = kv[g * inner:(g + 1) * inner, pairs + p].reshape(inner * span, LANES)
                out = out + tn(vals, e.astype(BF16))
            lses[p, :, index * stack:(index + 1) * stack] = top + jnp.log(total)
            rows_out = jnp.transpose(merge_heads(out / total))
            att_f[p, index * chunk:(index + 1) * chunk, :] = rows_out
            at = pl.ds(pl.multiple_of(p * LANES, LANES), LANES)
            att[index * chunk:(index + 1) * chunk, at] = rows_out.astype(BF16)
            return carry

        lax.fori_loop(0, pairs, attend, 0)
        if index == 0:
            weight_copies[1].wait()
        if index % (groups // 2) == groups // 2 - 1:
            piece = index // (groups // 2)
            head_send(piece, nn(att[piece * half_rows:(piece + 1) * half_rows, :], wo[...]), 0)

    def chunk_rows(z):
        return pl.ds(pl.multiple_of(z * chunk, chunk), chunk)

    def second_norm(z, carry):
        at = chunk_rows(z)
        mid = xb[z].astype(F32) + (send_h[0, at, :].astype(F32) + recv_h[0, at, :].astype(F32))
        middle[at, :] = mid
        hat, _ = norm_stats(mid)
        n2[at, :] = (hat * gain_two[...] + shift_two[...]).astype(BF16)
        return carry

    for piece in range(2):
        head_copy(piece, 0).wait()
        lax.fori_loop(piece * groups // 2, (piece + 1) * groups // 2, second_norm, 0)

    small[...] = jnp.zeros_like(small)

    def feed(i, carry):
        cols = pl.ds(pl.multiple_of(i * WIDE, WIDE), WIDE)
        bias = bias_rows[pl.ds(i, 1), :]
        dy = dyb[...].reshape(rows, width)
        sums = jnp.zeros((1, WIDE), F32)
        for part in range(2):
            lo = part * half_rows
            v = nn(n2[lo:lo + half_rows, :], wu[:, cols]) + bias
            back = gpre[lo:lo + half_rows, cols].astype(F32)
            sq = v * v
            t = jnp.tanh(GELU_A * v * (1.0 + GELU_B * sq))
            half = 0.5 * (1.0 + t)
            hid[lo:lo + half_rows, cols] = (v * half).astype(BF16)
            slope = half + 0.5 * v * (1.0 - t * t) * (GELU_A * (1.0 + 3.0 * GELU_B * sq))
            low = (back * slope).astype(BF16)
            gpre[lo:lo + half_rows, cols] = low
            sums = sums + jnp.sum(low.astype(F32), axis=0, keepdims=True)
        small[pl.ds(i, 1), :] = sums
        down = tn(hid[:, cols], dy)
        for c in range(col_tiles):
            at = pl.ds(pl.multiple_of(c * hidden + i * WIDE, WIDE), WIDE)
            acc[at, :] = down[:, c * LANES:(c + 1) * LANES].astype(BF16)
        return carry

    def feed_up(i, carry):
        cols = pl.ds(pl.multiple_of(i * WIDE, WIDE), WIDE)
        up = tn(n2[...], gpre[:, cols])
        for c in range(WIDE // LANES):
            at = pl.ds(pl.multiple_of(bases[1] + (i * (WIDE // LANES) + c) * width, LANES), width)
            acc[at, :] = up[:, c * LANES:(c + 1) * LANES].astype(BF16)
        return carry

    low_bits = int(math.log2(inner))
    orders = [
        list(range(bits)),
        [1, 0] + list(range(2, bits)),
        list(range(low_bits, bits)) + list(range(low_bits)),
    ]

    def bit_of(bit):
        return (me // (1 << bit)) % 2

    def partner(bit):
        return peer(me + (1 - 2 * bit_of(bit)) * (1 << bit))

    def sum_steps(job, part):
        seg = job_rows[job] // n
        first = max(16, int(seg * 0.4 / 16 + 0.5) * 16)
        sizes = [first, first, seg - 2 * first]
        base = bases[job] + n * sum(sizes[:part])
        s = sizes[part]
        order = orders[part]
        lo = 0
        size = n

        def at(ref, first, count):
            return ref.at[pl.ds(pl.multiple_of(base + first * s, 16), count * s)]

        for k, bit in enumerate(order):
            half = size // 2
            mine = lo + bit_of(bit) * half
            other = lo + (1 - bit_of(bit)) * half
            copy = remote(
                at(acc, other, half), at(arr, n - size, half),
                ar_send.at[job, part, k], ar_recv.at[job, part, k], partner(bit),
            )
            copy.start()
            yield
            copy.wait()
            pl.semaphore_signal(ar_free.at[job, part, k], inc=1, device_id=partner(bit), device_id_type=MESH)

            def add(i, carry, mine=mine, size=size):
                to = pl.ds(pl.multiple_of(base + mine * s + i * s, 16), s)
                frm = pl.ds(pl.multiple_of(base + (n - size) * s + i * s, 16), s)
                acc[to, :] = (acc[to, :].astype(F32) + arr[frm, :].astype(F32)).astype(BF16)
                return carry

            lax.fori_loop(0, half, add, 0)
            lo, size = mine, half
        for k, bit in reversed(list(enumerate(order))):
            pl.semaphore_wait(ar_free.at[job, part, k], 1)
            copy = remote(
                at(acc, lo, size), at(acc, lo, size),
                ar_send.at[job, part, bits + k], ar_recv.at[job, part, bits + k], partner(bit),
            )
            copy.start()
            yield
            copy.wait()
            lo = lo - bit_of(bit) * size
            size = size * 2

    jobs = [[sum_steps(job, part) for part in range(3)] for job in range(len(job_rows))]

    def tick(*which):
        for job in which:
            for steps in jobs[job]:
                next(steps, None)

    lax.fori_loop(0, up_bias_rows, feed, 0)
    tick(0)
    lax.fori_loop(0, up_bias_rows, feed_up, 0)
    tick(1)

    for piece in range(2):
        lo = piece * half_rows
        head_send(piece, nt(gpre[lo:lo + half_rows, :], wu[...]), 1)
    for piece in range(2):
        lo = piece * half_rows
        head_send(piece, nn(hid[lo:lo + half_rows, :], wd[...]), 2)

    def norm_back(hat, inv, gain, upstream):
        scaled = upstream * gain
        first = jnp.mean(scaled, axis=-1, keepdims=True)
        second = jnp.mean(scaled * hat, axis=-1, keepdims=True)
        return inv * (scaled - first - hat * second)

    def second_back(z, carry):
        gain_sum, shift_sum, bias_sum = carry
        at = chunk_rows(z)
        upstream = send_h[1, at, :].astype(F32) + recv_h[1, at, :].astype(F32)
        hat, inv = norm_stats(middle[at, :])
        dy = dyb[z].astype(F32)
        total = dy + norm_back(hat, inv, gain_two[...], upstream)
        grad_mid[at, :] = total
        n2[at, :] = total.astype(BF16)
        gain_sum = gain_sum + jnp.sum(upstream * hat, axis=0, keepdims=True)
        shift_sum = shift_sum + jnp.sum(upstream, axis=0, keepdims=True)
        bias_sum = bias_sum + jnp.sum(dy, axis=0, keepdims=True)
        return gain_sum, shift_sum, bias_sum

    zero_row = jnp.zeros((1, width), F32)
    sums = (zero_row, zero_row, zero_row)
    for piece in range(2):
        head_copy(piece, 1).wait()
        sums = lax.fori_loop(piece * groups // 2, (piece + 1) * groups // 2, second_back, sums)

    def keep_small(which, row):
        for c in range(width // WIDE):
            at = up_bias_rows + which * (width // WIDE) + c
            small[at:at + 1, :] = row[:, c * WIDE:(c + 1) * WIDE]

    keep_small(0, sums[2])
    keep_small(3, sums[0])
    keep_small(4, sums[1])

    def attended_back(z, carry):
        at = chunk_rows(z)
        back = nt(n2[at, :], wo[...])
        at_q = pl.ds(pl.multiple_of(z * stack, stack), stack)
        for p in range(pairs):
            low = back[:, p * LANES:(p + 1) * LANES].astype(BF16)
            dos[p, at_q, :] = stack_heads(low)
            prod = jnp.transpose(low.astype(F32) * att_f[p, at, :])
            d0 = jnp.sum(prod[:HD], axis=0, keepdims=True)
            d1 = jnp.sum(prod[HD:], axis=0, keepdims=True)
            deltas[p, :, at_q] = jnp.concatenate([d0, d1], axis=1)
        return carry

    lax.fori_loop(0, groups, attended_back, 0)
    tick(0, 1)

    wout = tn(att[...], n2[...])
    for c in range(col_tiles):
        at = bases[2] + c * head_width
        acc[at:at + head_width, :] = wout[:, c * LANES:(c + 1) * LANES].astype(BF16)

    def noisy_back(p, carry):
        for index in range(groups):
            at = slice(index * stack, (index + 1) * stack)
            q = qs[p, at, :]
            do = dos[p, at, :]
            keys = kvn[index, p]
            s = nt(keys, q)
            s = jnp.where(noisy_mask(s.shape), s, NEG)
            e = jnp.exp(s - lses[p, :, at])
            dp = nt(kvn[index, pairs + p], do)
            ds = (e * (dp - deltas[p, :, at])).astype(BF16)
            dkvn[index, pairs + p] = nn(e.astype(BF16), do)
            dkvn[index, p] = nn(ds, q)
            dq_t[p, :, at] = tn(keys, ds)
        return carry

    lax.fori_loop(0, pairs, noisy_back, 0)

    def grad_copy(index, near):
        dest = plane_peer(near)
        return remote(
            dkv.at[index * inner + dest], rkv.at[index, near - 1], g_send.at[index, near], g_recv.at[index, near],
            peer(group * inner + dest),
        )

    for index in range(groups):
        for block in range(key_blocks):
            first = index * inner + block * key_ranks

            def clean_back(p, carry, index=index, block=block, first=first):
                at = slice(index * stack, groups * stack)
                q = qs[p, at, :]
                do = dos[p, at, :]
                keys = kv[first:first + key_ranks, p].reshape(key_ranks * span, LANES)
                vals = kv[first:first + key_ranks, pairs + p].reshape(key_ranks * span, LANES)
                s = nt(keys, q)
                own = s[:, :stack]
                own = jnp.where(clean_mask(index, block * key_ranks, key_ranks, own.shape), own, NEG)
                if index < groups - 1:
                    s = jnp.concatenate([own, s[:, stack:]], axis=1)
                else:
                    s = own
                e = jnp.exp(s - lses[p, :, at])
                dp = nt(vals, do)
                ds = (e * (dp - deltas[p, :, at])).astype(BF16)
                dv = nn(e.astype(BF16), do).astype(BF16)
                dk = nn(ds, q).astype(BF16)
                dkv[first:first + key_ranks, p] = dk.reshape(key_ranks, span, LANES)
                dkv[first:first + key_ranks, pairs + p] = dv.reshape(key_ranks, span, LANES)
                dq_t[p, :, at] += tn(keys, ds)
                return carry

            lax.fori_loop(0, pairs, clean_back, 0)
        for near in range(1, inner):
            grad_copy(index, near).start()
        tick(0, 1)

    def feed_out(z, carry):
        at = chunk_rows(z)
        fed = send_h[2, at, :].astype(F32) + recv_h[2, at, :].astype(F32)
        dyb[z] = (middle[at, :] + fed + bias_down[...]).astype(BF16)
        return carry

    for piece in range(2):
        head_copy(piece, 2).wait()
    lax.fori_loop(0, groups, feed_out, 0)

    def spread(buf, out, ssem, rsem, psend, precv):
        copies, passes = [], []
        own = pltpu.make_async_copy(buf.at[group], out.at[group], ssem.at[0])
        own.start()
        for step in range(1, groups):
            to = group_peer(step)
            source = group_peer(groups - step)
            copies.append(
                remote(buf.at[to, share], out.at[group, share], ssem.at[step], rsem.at[step], peer(to * inner + rank))
            )
            passes.append(remote(out.at[source, share], out.at[source, share], psend.at[step], precv.at[step], sibling))
        for copy in copies:
            copy.start()
        return own, copies, passes

    def pass_on(spread_out):
        own, copies, passes = spread_out
        own.wait()
        for copy, onward in zip(copies, passes):
            copy.wait()
            onward.start()

    y_spread = spread(dyb, y_out, y_send, y_recv, yf_send, yf_recv)

    def turned(index, grad):
        cos = cos_t[index]
        sin = sin_t[index]
        cos2 = jnp.concatenate([cos, cos], axis=0)
        sin2 = jnp.concatenate([sin, sin], axis=0)
        return grad * cos2 - lane_swap(grad) * sin2

    def query_grads(index, carry):
        at = chunk_rows(index)
        at_q = pl.ds(pl.multiple_of(index * stack, stack), stack)
        for p in range(pairs):
            gq = jnp.transpose(merge_heads(dq_t[p, :, at_q])) * scale
            gpre[at, p * LANES:(p + 1) * LANES] = turned(index, gq).astype(BF16)
        return carry

    def key_grads(index, carry):
        at = chunk_rows(index)
        slot = index * inner + rank
        for p in range(pairs):
            for kind in range(2):
                which = kind * pairs + p
                total = dkv[slot, which].astype(F32)
                for near in range(inner - 1):
                    total = total + rkv[index, near, which].astype(F32)
                g = jnp.concatenate([dkvn[index, which], total], axis=0)
                if kind == 0:
                    g = turned(index, g)
                col = (kind + 1) * head_width + p * LANES
                gpre[at, col:col + LANES] = g.astype(BF16)
        return carry

    def head_grads(kind, base):
        part = tn(n1[...], gpre[:, kind * head_width:(kind + 1) * head_width])
        for p in range(pairs):
            at = base + p * width
            acc[at:at + width, :] = part[:, p * LANES:(p + 1) * LANES].astype(BF16)

    lax.fori_loop(0, groups, query_grads, 0)
    query_base = bases[2] + col_tiles * head_width
    head_grads(0, query_base)
    tick(2)
    for index in range(groups):
        for near in range(1, inner):
            grad_copy(index, near).wait()
    lax.fori_loop(0, groups, key_grads, 0)
    head_grads(1, bases[3])
    head_grads(2, bases[3] + pairs * width)
    tick(3)

    for piece in range(2):
        lo = piece * half_rows
        back = nt(gpre[lo:lo + half_rows, :head_width], wh[0])
        back = back + nt(gpre[lo:lo + half_rows, head_width:2 * head_width], wh[1])
        back = back + nt(gpre[lo:lo + half_rows, 2 * head_width:3 * head_width], wh[2])
        head_send(piece, back, 3)

    tick(0, 1)

    def first_back(z, carry):
        gain_sum, shift_sum = carry
        at = chunk_rows(z)
        upstream = send_h[0, at, :].astype(F32) + recv_h[0, at, :].astype(F32)
        hat, inv = norm_stats(xb[z].astype(F32))
        dyb[z] = (grad_mid[at, :] + norm_back(hat, inv, gain_one[...], upstream)).astype(BF16)
        gain_sum = gain_sum + jnp.sum(upstream * hat, axis=0, keepdims=True)
        shift_sum = shift_sum + jnp.sum(upstream, axis=0, keepdims=True)
        return gain_sum, shift_sum

    pass_on(y_spread)
    sums = (zero_row, zero_row)
    for piece in range(2):
        head_copy(piece, 3).wait()
        sums = lax.fori_loop(piece * groups // 2, (piece + 1) * groups // 2, first_back, sums)
    ig_spread = spread(dyb, ig_out, i_send, i_recv, if_send, if_recv)
    keep_small(1, sums[0])
    keep_small(2, sums[1])

    def small_job():
        for bit in range(bits):
            copy = remote(small.at[...], small_r.at[bit], sm_send.at[bit], sm_recv.at[bit], partner(bit))
            copy.start()
            yield
            copy.wait()
            small[...] = small[...] + small_r[bit]

    jobs.append([small_job()])
    outs = [[], [], [], []]
    for c in range(col_tiles):
        at = slice(c * LANES, (c + 1) * LANES)
        outs[0].append((acc.at[pl.ds(bases[0] + c * hidden, hidden)], down_out.at[:, at]))
        outs[2].append((acc.at[pl.ds(bases[2] + c * head_width, head_width)], wout_out.at[:, at]))
    for c in range(hidden // LANES):
        at = slice(c * LANES, (c + 1) * LANES)
        outs[1].append((acc.at[pl.ds(bases[1] + c * width, width)], up_out.at[:, at]))
    for p in range(pairs):
        at = slice(p * LANES, (p + 1) * LANES)
        outs[2].append((acc.at[pl.ds(query_base + p * width, width)], heads_out.at[0, :, at]))
        for kind in range(2):
            outs[3].append(
                (acc.at[pl.ds(bases[3] + (kind * pairs + p) * width, width)], heads_out.at[kind + 1, :, at])
            )
    sem_at = 0
    copies = []

    def finish(job):
        nonlocal sem_at
        for src, dst in outs[job]:
            copy = pltpu.make_async_copy(src, dst, out_sem.at[sem_at])
            copy.start()
            copies.append(copy)
            sem_at += 1

    order = [0, 1, 2, 3, 4]
    done = set()
    for turn in range(2 * bits + 1):
        tick(*order)
        if turn == bits:
            pass_on(ig_spread)
        for job in range(4):
            if job not in done and all(steps.gi_frame is None for steps in jobs[job]):
                finish(job)
                done.add(job)
    small_out[...] = small[...]
    for copy in x_copies + c_copies:
        copy.wait_send()
    for onward in y_spread[2] + ig_spread[2]:
        onward.wait()
    for copy in copies:
        copy.wait()


def widen(count, *refs):
    sources, small, targets = refs[:count], refs[count], refs[count + 1:]
    for source, target in zip(sources, targets):
        target[...] = source[...].astype(target.dtype)
    row = 0
    for target in targets[count:]:
        for i in range(target.shape[0] // WIDE):
            target[i * WIDE:(i + 1) * WIDE] = small[row]
            row += 1


def local(
    layer_input, block_sizes, mixing_gain, mixing_shift, w_heads, w_output, feed_gain, feed_shift,
    w_up, bias_up, w_down, bias_down, cotangent,
):
    groups, _, span, width = layer_input.shape
    n = lax.axis_size("seq")
    head_width = w_heads.shape[2]
    hidden = w_up.shape[1]
    inner = n // groups
    pairs = head_width // LANES
    chunk = 2 * span
    rows = groups * chunk
    stack = 2 * chunk
    bits = int(math.log2(n))
    job_rows, bases = job_layout(n, width, head_width, hidden)
    small_rows = (hidden // WIDE + 5 * (width // WIDE) + 7) // 8 * 8
    out_copies = width // LANES + hidden // LANES + 3 * pairs + width // LANES
    anywhere = pl.BlockSpec(memory_space=pl.ANY)
    vmem = pl.BlockSpec(memory_space=pltpu.VMEM)
    dma = pltpu.SemaphoreType.DMA
    scratch = [
        pltpu.VMEM((3, width, head_width), BF16),
        pltpu.VMEM((head_width, width), BF16),
        pltpu.VMEM((width, hidden), BF16),
        pltpu.VMEM((hidden, width), BF16),
        pltpu.VMEM((groups, chunk, width), BF16),
        pltpu.VMEM((groups, chunk, width), BF16),
        pltpu.VMEM((rows, width), BF16),
        pltpu.VMEM((rows, width), BF16),
        pltpu.VMEM((pairs, groups * stack, LANES), BF16),
        pltpu.VMEM((pairs, groups * stack, LANES), BF16),
        pltpu.VMEM((n, 2 * pairs, span, LANES), BF16),
        pltpu.VMEM((groups, 2 * pairs, span, LANES), BF16),
        pltpu.VMEM((n, 2 * pairs, span, LANES), BF16),
        pltpu.VMEM((groups, inner - 1, 2 * pairs, span, LANES), BF16),
        pltpu.VMEM((groups, 2 * pairs, span, LANES), F32),
        pltpu.VMEM((pairs, 1, groups * stack), F32),
        pltpu.VMEM((pairs, 1, groups * stack), F32),
        pltpu.VMEM((rows, head_width), BF16),
        pltpu.VMEM((pairs, rows, LANES), F32),
        pltpu.VMEM((rows, width), F32),
        pltpu.VMEM((rows, hidden), BF16),
        pltpu.VMEM((rows, hidden), BF16),
        pltpu.VMEM((3, rows, width), BF16),
        pltpu.VMEM((3, rows, width), BF16),
        pltpu.VMEM((rows, width), F32),
        pltpu.VMEM((pairs, LANES, groups * stack), F32),
        pltpu.VMEM((bases[-1], LANES), BF16),
        pltpu.VMEM((bases[-1], LANES), BF16),
        pltpu.VMEM((small_rows, WIDE), F32),
        pltpu.VMEM((bits, small_rows, WIDE), F32),
        pltpu.VMEM((groups, span, LANES), F32),
        pltpu.VMEM((groups, span, LANES), F32),
        pltpu.VMEM((-(-hidden // WIDE // 8) * 8, WIDE), F32),
        pltpu.VMEM((8, width), F32),
        dma((6,)),
        *[dma((groups,))] * 8,
        dma((groups, inner)), dma((groups, inner)),
        dma((4, 2)), dma((4, 2)),
        dma((groups, inner)), dma((groups, inner)),
        *[dma((groups,))] * 8,
        dma((4, 3, 2 * bits)), dma((4, 3, 2 * bits)), pltpu.SemaphoreType.REGULAR((4, 3, bits)),
        dma((bits,)), dma((bits,)),
        dma((out_copies,)),
    ]
    out_shape = (
        jax.ShapeDtypeStruct((groups, chunk, width), BF16),
        jax.ShapeDtypeStruct((groups, chunk, width), BF16),
        jax.ShapeDtypeStruct((hidden, width), BF16),
        jax.ShapeDtypeStruct((width, hidden), BF16),
        jax.ShapeDtypeStruct((3, width, head_width), BF16),
        jax.ShapeDtypeStruct((head_width, width), BF16),
        jax.ShapeDtypeStruct((small_rows, WIDE), F32),
    )
    y, ig, down, up, heads, wout, small = pl.pallas_call(
        functools.partial(fused, (n, groups, span, width, head_width, hidden)),
        out_shape=out_shape,
        in_specs=[anywhere] * 6 + [pl.BlockSpec(memory_space=pltpu.SMEM)] + [vmem] * 6,
        out_specs=(anywhere,) * 6 + (vmem,),
        scratch_shapes=scratch,
        compiler_params=pltpu.CompilerParams(
            collective_id=0, has_side_effects=True, vmem_limit_bytes=VMEM_BYTES
        ),
    )(
        layer_input.reshape(groups, chunk, width),
        cotangent.reshape(groups, chunk, width),
        w_heads, w_output, w_up, w_down, block_sizes,
        mixing_gain, mixing_shift, feed_gain, feed_shift, bias_up, bias_down,
    )
    full = (groups, 2, span, width)
    steps = 8
    sources = (y.reshape(rows, width), ig.reshape(rows, width), heads, wout, up, down)
    kinds = (BF16,) + (F32,) * 5
    specs = []
    for source in sources:
        shape = source.shape
        block = shape[:-2] + (shape[-2] // steps, shape[-1])
        specs.append(pl.BlockSpec(block, lambda i, lead=len(shape) - 2: (0,) * lead + (i, 0)))
    vector_sizes = (hidden,) + (width,) * 5
    y, ig, heads, wout, up, down, *vectors = pl.pallas_call(
        functools.partial(widen, len(sources)),
        grid=(steps,),
        out_shape=tuple(jax.ShapeDtypeStruct(a.shape, kind) for a, kind in zip(sources, kinds))
        + tuple(jax.ShapeDtypeStruct((size,), F32) for size in vector_sizes),
        in_specs=specs + [pl.BlockSpec(small.shape, lambda i: (0, 0))],
        out_specs=tuple(specs) + tuple(pl.BlockSpec((size,), lambda i: (0,)) for size in vector_sizes),
        compiler_params=pltpu.CompilerParams(vmem_limit_bytes=VMEM_BYTES),
    )(*sources, small)
    return (y.reshape(full), ig.reshape(full), heads, wout, up, vectors[0], down, *vectors[1:])


def solution(mesh):
    in_specs = (
        P(None, None, "seq", None), P(), P(), P(), P(None, None, "head"), P("head", None), P(), P(),
        P(None, "head"), P("head"), P("head", None), P(), P(None, None, "seq", None),
    )
    out_specs = (
        P(None, None, "seq", None), P(None, None, "seq", None), P(None, None, "head"), P("head", None),
        P(None, "head"), P("head"), P("head", None), P(), P(), P(), P(), P(),
    )
    return jax.shard_map(local, mesh=mesh, in_specs=in_specs, out_specs=out_specs, check_vma=False)
```

```python
import functools
import math

import jax
import jax.numpy as jnp
from jax import lax
from jax.experimental import pallas as pl
from jax.experimental.pallas import tpu as pltpu
from jax.sharding import PartitionSpec as P

HD = 64
LANES = 128
NEG = -1e30
EPS = 1e-05
ROTARY_BASE = 10000.0
GELU_A = math.sqrt(2.0 / math.pi)
GELU_B = 0.044715
MESH = pl.DeviceIdType.MESH
F32 = jnp.float32
BF16 = jnp.bfloat16
WIDE = 256
VMEM_BYTES = 66_900_000


PART_UNITS = ((7, 7, 4, 7, 7, 4), (7, 7, 4, 7, 7, 4), (7, 7, 4), (7, 7, 4))
PART_ORDERS = ((0, 1, 2, 1, 0, 3), (0, 1, 2, 1, 0, 3), (0, 1, 2), (0, 1, 2))
TURNS = ((0, (0, 1, 2)), (0, (3, 4, 5)), (1, (0, 1, 2)), (1, (3, 4, 5)), (2, (0, 1, 2)), (3, (0, 1, 2)), (4, (0,)))
ROUNDS = {
    "feed_up": 1, "noisy": 1, "g3": 1, "hq": 1, "hk": 1, "plane": 3, "first_back": 2,
}


def nn(a, b):
    return lax.dot_general(a, b, (((1,), (0,)), ((), ())), preferred_element_type=F32)


def nt(a, b):
    return lax.dot_general(a, b, (((1,), (1,)), ((), ())), preferred_element_type=F32)


def tn(a, b):
    return lax.dot_general(a, b, (((0,), (0,)), ((), ())), preferred_element_type=F32)


def lane_swap(a):
    lane = lax.broadcasted_iota(jnp.int32, a.shape, 1)
    ahead = pltpu.roll(a, LANES - HD // 2, 1)
    behind = pltpu.roll(a, HD // 2, 1)
    return jnp.where(lane % HD < HD // 2, ahead, behind)


def stack_heads(a):
    lane = lax.broadcasted_iota(jnp.int32, a.shape, 1)
    zero = jnp.zeros_like(a)
    return jnp.concatenate([jnp.where(lane < HD, a, zero), jnp.where(lane >= HD, a, zero)], axis=0)


def merge_heads(a):
    half = a.shape[1] // 2
    sub = lax.broadcasted_iota(jnp.int32, (a.shape[0], half), 0)
    return jnp.where(sub < HD, a[:, :half], a[:, half:])


def job_layout(n, width, head_width, hidden):
    whole = [hidden * width // LANES] * 2 + [2 * head_width * width // LANES] * 2
    padded = [-(-count // (16 * n)) * 16 * n for count in whole]
    return padded, [sum(padded[:i]) for i in range(len(padded) + 1)]


def fused(dims, *refs):
    n, groups, span, width, head_width, hidden = dims
    (
        x_in, c_in, wh_in, wo_in, wu_in, wd_in, blocks,
        gain_one_in, shift_one_in, gain_two_in, shift_two_in, bias_up_in, bias_down_in,
        y_out, ig_out, down_out, up_out, heads_out, wout_out, small_out,
        wh, wo, wu, wd, xb, dyb, n1, n2, nc, qs, dos, kv, kvn, lses, deltas, att,
        middle, hid, gpre, send_h, recv_h, grad_mid, dq_t, core_part, plane_part, clean_sum,
        acc, arr, small, small_r, cos_a, sin_a, cos_b, sin_b, bias_rows, vectors,
        w_sem, xc_send, xc_recv, xn_send, xn_recv, c_send, c_recv, xcf_send, xcf_recv, xnf_send, xnf_recv, cf_send, cf_recv,
        kv_send, kv_recv, loc_sem, ncf_send, ncf_recv, h_send, h_recv, g_send, g_recv, k_send, k_recv,
        y_send, y_recv, i_send, i_recv, yf_send, yf_recv, if_send, if_recv, ar_send, ar_recv, ar_free, sm_send, sm_recv, out_sem,
    ) = refs
    inner = n // groups
    job_rows, bases = job_layout(n, width, head_width, hidden)
    pairs = head_width // LANES
    chunk = 2 * span
    rows = groups * chunk
    stack = 2 * chunk
    key_ranks = min(inner, max(1, WIDE // span))
    key_blocks = inner // key_ranks
    half_rows = rows // 2
    col_tiles = width // LANES
    bits = int(math.log2(n))
    scale = 1.0 / math.sqrt(HD)
    up_bias_rows = hidden // WIDE
    gain_one, shift_one, gain_two, shift_two, bias_down = (vectors.at[i:i + 1, :] for i in range(5))

    me = lax.axis_index("seq")
    core = lax.axis_index("head")
    group = me // inner
    rank = me % inner

    def peer(seq_index):
        return (seq_index, core)

    sibling = (me, 1 - core)

    def group_peer(step):
        return (group + step) % groups

    def plane_peer(step):
        return (rank + step) % inner

    def remote(src, dst, ssem, rsem, where):
        return pltpu.make_async_remote_copy(
            src_ref=src, dst_ref=dst, send_sem=ssem, recv_sem=rsem, device_id=where, device_id_type=MESH
        )

    barrier = pltpu.get_barrier_semaphore()
    for step in range(1, groups):
        pl.semaphore_signal(barrier, inc=1, device_id=peer(group_peer(step) * inner + rank), device_id_type=MESH)
    for step in range(1, inner):
        pl.semaphore_signal(barrier, inc=1, device_id=peer(group * inner + plane_peer(step)), device_id_type=MESH)
    pl.semaphore_signal(barrier, inc=1, device_id=sibling, device_id_type=MESH)
    weight_copies = [
        pltpu.make_async_copy(wh_in, wh, w_sem.at[0]),
        pltpu.make_async_copy(wo_in, wo, w_sem.at[1]),
        pltpu.make_async_copy(wu_in, wu, w_sem.at[2]),
        pltpu.make_async_copy(wd_in, wd, w_sem.at[3]),
    ]
    own_x = pltpu.make_async_copy(x_in.at[group], xb.at[group], w_sem.at[4])
    own_c = pltpu.make_async_copy(c_in.at[group], dyb.at[group], w_sem.at[5])
    own_x.start()
    weight_copies[0].start()
    pl.semaphore_wait(barrier, groups + inner - 1)

    clean_copies, noisy_copies, c_copies = [], [], []
    clean_passes, noisy_passes, c_passes = [], [], []
    share_rows = span // 2
    share = pl.ds(pl.multiple_of(core * share_rows, share_rows), share_rows)
    other_share = pl.ds(pl.multiple_of((1 - core) * share_rows, share_rows), share_rows)
    for step in range(1, groups):
        to = group_peer(step)
        source = group_peer(groups - step)
        where = peer(to * inner + rank)
        clean_copies.append(
            remote(x_in.at[to, 1, share], xb.at[group, 1, share], xc_send.at[step], xc_recv.at[step], where)
        )
        noisy_copies.append(
            remote(x_in.at[to, 0, share], xb.at[group, 0, share], xn_send.at[step], xn_recv.at[step], where)
        )
        c_copies.append(
            remote(c_in.at[to, :, share], dyb.at[group, :, share], c_send.at[step], c_recv.at[step], where)
        )
        clean_passes.append(
            remote(xb.at[source, 1, share], xb.at[source, 1, share], xcf_send.at[step], xcf_recv.at[step], sibling)
        )
        noisy_passes.append(
            remote(xb.at[source, 0, share], xb.at[source, 0, share], xnf_send.at[step], xnf_recv.at[step], sibling)
        )
        c_passes.append(
            remote(dyb.at[source, :, share], dyb.at[source, :, share], cf_send.at[step], cf_recv.at[step], sibling)
        )
    for copy in clean_copies + noisy_copies:
        copy.start()

    def plane_copy(index, near):
        slot = index * inner + rank
        return remote(
            xb.at[index, 1, share], nc.at[slot, share], kv_send.at[index, near], kv_recv.at[index, near],
            peer(group * inner + plane_peer(near)),
        )

    def own_clean(index):
        return pltpu.make_async_copy(xb.at[index, 1, share], nc.at[index * inner + rank, share], loc_sem.at[index])

    def plane_send(index):
        for near in range(1, inner):
            plane_copy(index, near).start()
        own_clean(index).start()

    def plane_pass(index):
        at = pl.ds(index * inner, inner)
        return remote(nc.at[at, share], nc.at[at, share], ncf_send.at[index], ncf_recv.at[index], sibling)

    def plane_done(index):
        own_clean(index).wait()
        for near in range(1, inner):
            plane_copy(index, near).wait()
        plane_pass(index).start()

    own_x.wait()
    plane_send(group)
    for copy in weight_copies[1:]:
        copy.start()
    own_c.start()

    size_b = blocks[group]
    lane_q = lax.broadcasted_iota(jnp.int32, (1, stack), 1)
    in_chunk = lane_q % chunk
    clean_q = in_chunk >= span
    start_q = (in_chunk % span) & (-size_b)
    limit_q = start_q + jnp.where(clean_q, size_b, 0)

    def norm_stats(x):
        center = jnp.mean(x, axis=-1, keepdims=True)
        off = x - center
        inv = lax.rsqrt(jnp.mean(off * off, axis=-1, keepdims=True) + EPS)
        return off * inv, inv

    for row in range(up_bias_rows):
        bias_rows[row:row + 1, :] = bias_up_in[row * WIDE:(row + 1) * WIDE].reshape(1, WIDE)
    for row, vector in enumerate((gain_one_in, shift_one_in, gain_two_in, shift_two_in, bias_down_in)):
        vectors[row:row + 1, :] = vector[...].reshape(1, width)

    half_head = HD // 2
    lane = lax.broadcasted_iota(jnp.int32, (1, LANES), 1)
    frequency = jnp.exp((lane % half_head).astype(F32) * (-math.log(ROTARY_BASE) / half_head))
    sign = jnp.where(lane % HD < half_head, -1.0, 1.0)
    start = lax.broadcasted_iota(jnp.int32, (n, LANES), 0) * span
    angle = start.astype(F32) * frequency
    cos_a[...] = jnp.cos(angle)
    sin_a[...] = jnp.sin(angle) * sign
    angle = lax.broadcasted_iota(jnp.int32, (span, LANES), 0).astype(F32) * frequency
    cos_b[...] = jnp.cos(angle)
    sin_b[...] = jnp.sin(angle) * sign

    def tables(slot):
        cos = cos_a[pl.ds(slot, 1), :]
        sin = sin_a[pl.ds(slot, 1), :]
        return cos * cos_b[...] - sin * sin_b[...], sin * cos_b[...] + cos * sin_b[...]

    def turn(value, table):
        return value * table[0] + lane_swap(value) * table[1]

    def turn_back(value, table):
        return value * table[0] - lane_swap(value) * table[1]

    def twice(table):
        return tuple(jnp.concatenate([part, part], axis=0) for part in table)

    def many(first, count):
        parts = [tables(first + i) for i in range(count)]
        return tuple(jnp.concatenate([part[i] for part in parts], axis=0) for i in range(2))

    weight_copies[0].wait()
    for step in range(1, groups):
        clean_copies[step - 1].wait_recv()
        plane_send(group_peer(groups - step))
        clean_passes[step - 1].start()
    for step in range(1, groups):
        noisy_copies[step - 1].wait_recv()
        noisy_passes[step - 1].start()
    for copy in c_copies:
        copy.start()
    plane_done(group)
    for copy in clean_passes + noisy_passes:
        copy.wait()

    def first_norm(z, carry):
        hat, _ = norm_stats(xb[z].reshape(chunk, width).astype(F32))
        n1[z] = (hat * gain_one[...] + shift_one[...]).astype(BF16).reshape(2, span, width)
        return carry

    lax.fori_loop(0, groups, first_norm, 0)

    def queries(z, carry):
        out = nn(n1[z].reshape(chunk, width), wh[0])
        table = twice(tables(z * inner + rank))
        at_q = pl.ds(pl.multiple_of(z * stack, stack), stack)
        for p in range(pairs):
            low = (turn(out[:, p * LANES:(p + 1) * LANES], table) * scale).astype(BF16)
            qs[p, at_q, :] = stack_heads(low)
        return carry

    lax.fori_loop(0, groups, queries, 0)
    noisy_rows = n1[:, 0].reshape(groups * span, width)
    for kind in range(2):
        out = nn(noisy_rows, wh[kind + 1])
        for z in range(groups):
            table = tables(z * inner + rank)
            for p in range(pairs):
                part = out[z * span:(z + 1) * span, p * LANES:(p + 1) * LANES]
                kvn[z, kind * pairs + p] = (part if kind else turn(part, table)).astype(BF16)
    for step in range(1, groups):
        plane_done(group_peer(groups - step))

    def clean_rows(first):
        x = nc[first:first + key_ranks].reshape(key_ranks * span, width).astype(F32)
        hat, _ = norm_stats(x)
        normed = (hat * gain_one[...] + shift_one[...]).astype(BF16)
        nc[first:first + key_ranks] = normed.reshape(key_ranks, span, width)
        table = many(first, key_ranks)
        for kind in range(2):
            out = nn(normed, wh[kind + 1])
            for p in range(pairs):
                part = out[:, p * LANES:(p + 1) * LANES]
                low = (part if kind else turn(part, table)).astype(BF16)
                kv[first:first + key_ranks, kind * pairs + p] = low.reshape(key_ranks, span, LANES)

    def clean_mask(index, first_rank, count, shape):
        key = lax.broadcasted_iota(jnp.int32, shape, 0) + first_rank * span
        return key < limit_q + rank * span

    def noisy_mask(shape):
        key = lax.broadcasted_iota(jnp.int32, shape, 0) & (-size_b)
        return (key == start_q) & jnp.logical_not(clean_q)

    def feed_back(i, carry):
        cols = pl.ds(pl.multiple_of(i * WIDE, WIDE), WIDE)
        gpre[:, cols] = nt(dyb[...].reshape(rows, width), wd[cols, :]).astype(BF16)
        return carry

    def head_send(piece, value, which):
        at = slice(piece * groups // 2, (piece + 1) * groups // 2)
        send_h[which % 2, at] = value.astype(BF16).reshape(groups // 2, 2, span, width)
        if which != 2:
            head_copy(piece, which).start()

    def head_copy(piece, which):
        at = pl.ds(piece * groups // 2, groups // 2)
        return remote(
            send_h.at[which % 2, at], recv_h.at[which % 2, at], h_send.at[which, piece], h_recv.at[which, piece], sibling
        )

    for index in range(groups):
        plane_pass(index).wait()
        for block in range(key_blocks):
            clean_rows(index * inner + block * key_ranks)

        def attend(p, carry, index=index):
            q = qs[p, index * stack:(index + 1) * stack, :]
            pieces = []
            top = None
            for g in range(index + 1):
                keys = kv[g * inner:(g + 1) * inner, p].reshape(inner * span, LANES)
                s = nt(keys, q)
                if g == index:
                    s = jnp.where(clean_mask(index, 0, inner, s.shape), s, NEG)
                pieces.append(s)
                best = jnp.max(s, axis=0, keepdims=True)
                top = best if top is None else jnp.maximum(top, best)
            s = nt(kvn[index, p], q)
            s = jnp.where(noisy_mask(s.shape), s, NEG)
            top = jnp.maximum(top, jnp.max(s, axis=0, keepdims=True))
            e = jnp.exp(s - top)
            total = jnp.sum(e, axis=0, keepdims=True)
            out = tn(kvn[index, pairs + p], e.astype(BF16))
            for g in range(index + 1):
                e = jnp.exp(pieces[g] - top)
                total = total + jnp.sum(e, axis=0, keepdims=True)
                vals = kv[g * inner:(g + 1) * inner, pairs + p].reshape(inner * span, LANES)
                out = out + tn(vals, e.astype(BF16))
            lses[p, :, index * stack:(index + 1) * stack] = top + jnp.log(total)
            merged = merge_heads(out / total)
            rows_out = jnp.transpose(merged)
            dq_t[p, :, index * stack:index * stack + chunk] = merged
            at = pl.ds(pl.multiple_of(p * LANES, LANES), LANES)
            att[index * chunk:(index + 1) * chunk, at] = rows_out.astype(BF16)
            return carry

        lax.fori_loop(0, pairs, attend, 0)
        if index == 0:
            weight_copies[1].wait()
        if index % (groups // 2) == groups // 2 - 1:
            piece = index // (groups // 2)
            head_send(piece, nn(att[piece * half_rows:(piece + 1) * half_rows, :], wo[...]), 0)
        if index == groups // 2:
            own_c.wait()
            for copy, onward in zip(c_copies, c_passes):
                copy.wait_recv()
                onward.start()

    weight_copies[2].wait()
    weight_copies[3].wait()
    for copy in c_passes:
        copy.wait()
    lax.fori_loop(0, up_bias_rows, feed_back, 0)

    def chunk_rows(z):
        return pl.ds(pl.multiple_of(z * chunk, chunk), chunk)

    def second_norm(z, carry):
        at = chunk_rows(z)
        mixed = send_h[0, z].astype(F32) + recv_h[0, z].astype(F32)
        mid = (xb[z].astype(F32) + mixed).reshape(chunk, width)
        middle[at, :] = mid
        hat, _ = norm_stats(mid)
        n2[at, :] = (hat * gain_two[...] + shift_two[...]).astype(BF16)
        return carry

    for piece in range(2):
        head_copy(piece, 0).wait()
        lax.fori_loop(piece * groups // 2, (piece + 1) * groups // 2, second_norm, 0)

    small[...] = jnp.zeros_like(small)

    def feed(i, carry):
        cols = pl.ds(pl.multiple_of(i * WIDE, WIDE), WIDE)
        bias = bias_rows[pl.ds(i, 1), :]
        dy = dyb[...].reshape(rows, width)
        sums = jnp.zeros((1, WIDE), F32)
        for part in range(2):
            lo = part * half_rows
            v = nn(n2[lo:lo + half_rows, :], wu[:, cols]) + bias
            back = gpre[lo:lo + half_rows, cols].astype(F32)
            sq = v * v
            t = jnp.tanh(GELU_A * v * (1.0 + GELU_B * sq))
            half = 0.5 * (1.0 + t)
            hid[lo:lo + half_rows, cols] = (v * half).astype(BF16)
            slope = half + 0.5 * v * (1.0 - t * t) * (GELU_A * (1.0 + 3.0 * GELU_B * sq))
            low = (back * slope).astype(BF16)
            gpre[lo:lo + half_rows, cols] = low
            sums = sums + jnp.sum(low.astype(F32), axis=0, keepdims=True)
        small[pl.ds(i, 1), :] = sums
        down = tn(hid[:, cols], dy)
        for c in range(col_tiles):
            at = pl.ds(pl.multiple_of(c * hidden + i * WIDE, WIDE), WIDE)
            acc[at, :] = down[:, c * LANES:(c + 1) * LANES].astype(BF16)
        return carry

    def feed_up(i, carry):
        cols = pl.ds(pl.multiple_of(i * WIDE, WIDE), WIDE)
        up = tn(n2[...], gpre[:, cols])
        for c in range(WIDE // LANES):
            at = pl.ds(pl.multiple_of(bases[1] + (i * (WIDE // LANES) + c) * width, LANES), width)
            acc[at, :] = up[:, c * LANES:(c + 1) * LANES].astype(BF16)
        return carry

    low_bits = int(math.log2(inner))
    plane_bits, group_bits = list(range(low_bits)), list(range(low_bits, bits))
    turned_bits = plane_bits[1::-1] + plane_bits[2:]
    orders = [
        plane_bits + group_bits,
        turned_bits + group_bits,
        group_bits + plane_bits,
        group_bits + turned_bits,
        turned_bits[:1] + group_bits + turned_bits[1:],
        plane_bits[:1] + group_bits + plane_bits[1:],
    ]

    def bit_of(bit):
        return (me // (1 << bit)) % 2

    def partner(bit):
        return peer(me + (1 - 2 * bit_of(bit)) * (1 << bit))

    def sum_steps(job, part):
        weights = PART_UNITS[job]
        units = job_rows[job] // n // 16
        edges = [(2 * sum(weights[:i]) * units + sum(weights)) // (2 * sum(weights)) for i in range(len(weights) + 1)]
        base = bases[job] + n * 16 * edges[part]
        s = 16 * (edges[part + 1] - edges[part])
        order = orders[PART_ORDERS[job][part]]
        if s == 0:
            return
        lo = 0
        size = n

        def at(ref, first, count):
            return ref.at[pl.ds(pl.multiple_of(base + first * s, 16), count * s)]

        for k, bit in enumerate(order):
            half = size // 2
            mine = lo + bit_of(bit) * half
            other = lo + (1 - bit_of(bit)) * half
            copy = remote(
                at(acc, other, half), at(arr, n - size, half),
                ar_send.at[job, part, k], ar_recv.at[job, part, k], partner(bit),
            )
            copy.start()
            yield
            copy.wait()
            pl.semaphore_signal(ar_free.at[job, part, k], inc=1, device_id=partner(bit), device_id_type=MESH)

            def add(i, carry, mine=mine, size=size):
                to = pl.ds(pl.multiple_of(base + mine * s + i * s, 16), s)
                frm = pl.ds(pl.multiple_of(base + (n - size) * s + i * s, 16), s)
                acc[to, :] = (acc[to, :].astype(F32) + arr[frm, :].astype(F32)).astype(BF16)
                return carry

            lax.fori_loop(0, half, add, 0)
            lo, size = mine, half
        for k, bit in reversed(list(enumerate(order))):
            pl.semaphore_wait(ar_free.at[job, part, k], 1)
            copy = remote(
                at(acc, lo, size), at(acc, lo, size),
                ar_send.at[job, part, bits + k], ar_recv.at[job, part, bits + k], partner(bit),
            )
            copy.start()
            yield
            copy.wait()
            lo = lo - bit_of(bit) * size
            size = size * 2

    jobs = [[sum_steps(job, part) for part in range(len(PART_UNITS[job]))] for job in range(len(job_rows))]
    query_base = bases[2] + col_tiles * head_width
    copies = []
    finished = set()
    outs = [[], [], [], []]
    for c in range(col_tiles):
        at = slice(c * LANES, (c + 1) * LANES)
        outs[0].append((acc.at[pl.ds(bases[0] + c * hidden, hidden)], down_out.at[:, at]))
        outs[2].append((acc.at[pl.ds(bases[2] + c * head_width, head_width)], wout_out.at[:, at]))
    for c in range(hidden // LANES):
        at = slice(c * LANES, (c + 1) * LANES)
        outs[1].append((acc.at[pl.ds(bases[1] + c * width, width)], up_out.at[:, at]))
    for p in range(pairs):
        at = slice(p * LANES, (p + 1) * LANES)
        outs[2].append((acc.at[pl.ds(query_base + p * width, width)], heads_out.at[0, :, at]))
        for kind in range(2):
            outs[3].append(
                (acc.at[pl.ds(bases[3] + (kind * pairs + p) * width, width)], heads_out.at[kind + 1, :, at])
            )
    sem_at = 0

    def finish(job):
        nonlocal sem_at
        for src, dst in outs[job]:
            copy = pltpu.make_async_copy(src, dst, out_sem.at[sem_at])
            copy.start()
            copies.append(copy)
            sem_at += 1


    def advance(job, part):
        next(jobs[job][part], None)
        if job < 4 and job not in finished and all(steps.gi_frame is None for steps in jobs[job]):
            finish(job)
            finished.add(job)


    released = set()
    running, waiting = [], list(TURNS)

    def take_round():
        for job, parts in running:
            for part in parts:
                advance(job, part)
        if waiting and waiting[0][0] in released:
            job, parts = waiting.pop(0)
            running.append((job, parts))
            for part in parts:
                advance(job, part)

    def point(name):
        for _ in range(ROUNDS.get(name, 0)):
            take_round()

    def begin(job):
        released.add(job)

    lax.fori_loop(0, up_bias_rows, feed, 0)
    begin(0)
    take_round()
    lax.fori_loop(0, up_bias_rows, feed_up, 0)
    begin(1)
    point("feed_up")

    for piece in range(2):
        lo = piece * half_rows
        head_send(piece, nt(gpre[lo:lo + half_rows, :], wu[...]), 1)
    point("back2")
    for piece in range(2):
        lo = piece * half_rows
        head_send(piece, nn(hid[lo:lo + half_rows, :], wd[...]), 2)
    point("fed")

    def norm_back(hat, inv, gain, upstream):
        scaled = upstream * gain
        first = jnp.mean(scaled, axis=-1, keepdims=True)
        second = jnp.mean(scaled * hat, axis=-1, keepdims=True)
        return inv * (scaled - first - hat * second)

    def second_back(z, carry):
        gain_sum, shift_sum, bias_sum = carry
        at = chunk_rows(z)
        upstream = (send_h[1, z].astype(F32) + recv_h[1, z].astype(F32)).reshape(chunk, width)
        hat, inv = norm_stats(middle[at, :])
        dy = dyb[z].astype(F32).reshape(chunk, width)
        total = dy + norm_back(hat, inv, gain_two[...], upstream)
        grad_mid[at, :] = total
        n2[at, :] = total.astype(BF16)
        gain_sum = gain_sum + jnp.sum(upstream * hat, axis=0, keepdims=True)
        shift_sum = shift_sum + jnp.sum(upstream, axis=0, keepdims=True)
        bias_sum = bias_sum + jnp.sum(dy, axis=0, keepdims=True)
        return gain_sum, shift_sum, bias_sum

    zero_row = jnp.zeros((1, width), F32)
    sums = (zero_row, zero_row, zero_row)
    for piece in range(2):
        head_copy(piece, 1).wait()
        sums = lax.fori_loop(piece * groups // 2, (piece + 1) * groups // 2, second_back, sums)

    def keep_small(which, row):
        for c in range(width // WIDE):
            at = up_bias_rows + which * (width // WIDE) + c
            small[at:at + 1, :] = row[:, c * WIDE:(c + 1) * WIDE]

    keep_small(0, sums[2])
    keep_small(3, sums[0])
    keep_small(4, sums[1])
    for piece in range(2):
        head_copy(piece, 2).start()
    point("second_back")

    def attended_back(z, carry):
        at = chunk_rows(z)
        back = nt(n2[at, :], wo[...])
        at_q = pl.ds(pl.multiple_of(z * stack, stack), stack)
        for p in range(pairs):
            low = back[:, p * LANES:(p + 1) * LANES].astype(BF16)
            dos[p, at_q, :] = stack_heads(low)
            at_o = pl.ds(pl.multiple_of(z * stack, stack), chunk)
            prod = jnp.transpose(low.astype(F32)) * dq_t[p, :, at_o]
            d0 = jnp.sum(prod[:HD], axis=0, keepdims=True)
            d1 = jnp.sum(prod[HD:], axis=0, keepdims=True)
            deltas[p, :, at_q] = jnp.concatenate([d0, d1], axis=1)
        return carry

    lax.fori_loop(0, groups, attended_back, 0)
    point("att_back")

    wout = tn(att[...], n2[...])
    for c in range(col_tiles):
        at = bases[2] + c * head_width
        acc[at:at + head_width, :] = wout[:, c * LANES:(c + 1) * LANES].astype(BF16)
    point("wout")

    def noisy_back(p, carry):
        for index in range(groups):
            at = slice(index * stack, (index + 1) * stack)
            q = qs[p, at, :]
            do = dos[p, at, :]
            keys = kvn[index, p]
            s = nt(keys, q)
            s = jnp.where(noisy_mask(s.shape), s, NEG)
            e = jnp.exp(s - lses[p, :, at])
            dp = nt(kvn[index, pairs + p], do)
            ds = (e * (dp - deltas[p, :, at])).astype(BF16)
            at_n = slice(index * span, (index + 1) * span)
            cols = pl.multiple_of(head_width + p * LANES, LANES)
            gpre[at_n, pl.ds(cols, LANES)] = turn_back(nn(ds, q), tables(index * inner + rank)).astype(BF16)
            cols = pl.multiple_of(2 * head_width + p * LANES, LANES)
            gpre[at_n, pl.ds(cols, LANES)] = nn(e.astype(BF16), do).astype(BF16)
            dq_t[p, :, at] = tn(keys, ds)
        return carry

    lax.fori_loop(0, pairs, noisy_back, 0)
    point("noisy")

    for index in range(groups):
        for block in range(key_blocks):
            first = index * inner + block * key_ranks

            def clean_back(p, carry, index=index, block=block, first=first):
                at = slice(index * stack, groups * stack)
                q = qs[p, at, :]
                do = dos[p, at, :]
                keys = kv[first:first + key_ranks, p].reshape(key_ranks * span, LANES)
                vals = kv[first:first + key_ranks, pairs + p].reshape(key_ranks * span, LANES)
                s = nt(keys, q)
                own = s[:, :stack]
                own = jnp.where(clean_mask(index, block * key_ranks, key_ranks, own.shape), own, NEG)
                if index < groups - 1:
                    s = jnp.concatenate([own, s[:, stack:]], axis=1)
                else:
                    s = own
                e = jnp.exp(s - lses[p, :, at])
                dp = nt(vals, do)
                ds = (e * (dp - deltas[p, :, at])).astype(BF16)
                dv = nn(e.astype(BF16), do).astype(BF16)
                dk = turn_back(nn(ds, q), many(first, key_ranks)).astype(BF16)
                dq_t[p, :, at] += tn(keys, ds)
                kv[first:first + key_ranks, p] = dk.reshape(key_ranks, span, LANES)
                kv[first:first + key_ranks, pairs + p] = dv.reshape(key_ranks, span, LANES)
                return carry

            if index < groups // 2:
                for p in range(pairs):
                    clean_back(p, 0)
                    point(f"g{index}p{p}")
            else:
                lax.fori_loop(0, pairs, clean_back, 0)
                point(f"g{index}")

    def query_grads(index, carry):
        at = chunk_rows(index)
        at_q = pl.ds(pl.multiple_of(index * stack, stack), stack)
        table = twice(tables(index * inner + rank))
        for p in range(pairs):
            gq = jnp.transpose(merge_heads(dq_t[p, :, at_q])) * scale
            gpre[at, p * LANES:(p + 1) * LANES] = turn_back(gq, table).astype(BF16)
        return carry

    def keep_heads(part, base):
        for p in range(part.shape[1] // LANES):
            at = base + p * width
            acc[at:at + width, :] = part[:, p * LANES:(p + 1) * LANES].astype(BF16)

    lax.fori_loop(0, groups, query_grads, 0)
    point("qg")
    keep_heads(tn(n1[...].reshape(rows, width), gpre[:, :head_width]), query_base)
    begin(2)
    point("hq")
    sweep = min(n, 16)
    many_rows = sweep * span
    widths = 2 * pairs if n <= 16 else pairs
    for lead in range(0, 2 * pairs, widths):
        at = head_width + lead * LANES
        part = tn(n1[:, 0].reshape(groups * span, width), gpre[:groups * span, at:at + widths * LANES])
        for first in range(0, n, sweep):
            gates = jnp.concatenate(
                [kv[first:first + sweep, lead + i].reshape(many_rows, LANES) for i in range(widths)], axis=1
            )
            part = part + tn(nc[first:first + sweep].reshape(many_rows, width), gates)
        keep_heads(part, bases[3] + lead * width)
    begin(3)
    point("hk")

    def clean_input(block, carry):
        at = pl.ds(block * key_ranks, key_ranks)
        total = None
        for kind in range(2):
            gates = jnp.concatenate(
                [kv[at, kind * pairs + p].reshape(key_ranks * span, LANES) for p in range(pairs)], axis=1
            )
            back = nt(gates, wh[kind + 1])
            total = back if total is None else total + back
        nc[at] = total.astype(BF16).reshape(key_ranks, span, width)
        return carry

    lax.fori_loop(0, n // key_ranks, clean_input, 0)
    core_copy = remote(nc.at[:, other_share], core_part, k_send.at[0], k_recv.at[0], sibling)
    core_copy.start()
    point("clean_in")

    def feed_out(z, carry):
        at = chunk_rows(z)
        fed = (send_h[0, z].astype(F32) + recv_h[0, z].astype(F32)).reshape(chunk, width)
        dyb[z] = (middle[at, :] + fed + bias_down[...]).astype(BF16).reshape(2, span, width)
        return carry

    for piece in range(2):
        head_copy(piece, 2).wait()
    lax.fori_loop(0, groups, feed_out, 0)

    point("feed_out")
    def spread(buf, out, ssem, rsem, psend, precv):
        copies, passes = [], []
        own = pltpu.make_async_copy(buf.at[group], out.at[group], ssem.at[0])
        own.start()
        for step in range(1, groups):
            to = group_peer(step)
            source = group_peer(groups - step)
            copies.append(
                remote(buf.at[to, :, share], out.at[group, :, share], ssem.at[step], rsem.at[step], peer(to * inner + rank))
            )
            passes.append(remote(out.at[source, :, share], out.at[source, :, share], psend.at[step], precv.at[step], sibling))
        for copy in copies:
            copy.start()
        return own, copies, passes

    def pass_on(spread_out):
        own, copies, passes = spread_out
        own.wait()
        for copy, onward in zip(copies, passes):
            copy.wait()
            onward.start()

    y_spread = spread(dyb, y_out, y_send, y_recv, yf_send, yf_recv)

    for piece in range(2):
        lo = piece * half_rows
        back = nt(gpre[lo:lo + half_rows, :head_width], wh[0]).reshape(groups // 2, 2, span, width)
        lo = lo // 2
        extra = nt(gpre[lo:lo + half_rows // 2, head_width:2 * head_width], wh[1])
        extra = extra + nt(gpre[lo:lo + half_rows // 2, 2 * head_width:3 * head_width], wh[2])
        extra = extra.reshape(groups // 2, span, width)
        at = slice(piece * groups // 2, (piece + 1) * groups // 2)
        send_h[1, at, 0] = (back[:, 0] + extra).astype(BF16)
        send_h[1, at, 1] = back[:, 1].astype(BF16)
        head_copy(piece, 3).start()
    point("back1")
    core_copy.wait()

    def core_add(slot, carry):
        nc[slot, share] = (nc[slot, share].astype(F32) + core_part[slot].astype(F32)).astype(BF16)
        return carry

    lax.fori_loop(0, n, core_add, 0)
    point("core_add")

    def part_copy(index, near):
        dest = plane_peer(near)
        return remote(
            nc.at[index * inner + dest, share], plane_part.at[index, near - 1], g_send.at[index, near],
            g_recv.at[index, near], peer(group * inner + dest),
        )

    for index in range(groups):
        for near in range(1, inner):
            part_copy(index, near).start()
    point("plane")
    for index in range(groups):
        for near in range(1, inner):
            part_copy(index, near).wait()

    def clean_add(index, carry):
        total = nc[index * inner + rank, share].astype(F32)
        for near in range(inner - 1):
            total = total + plane_part[index, near].astype(F32)
        clean_sum[index, share] = total.astype(BF16)
        return carry

    lax.fori_loop(0, groups, clean_add, 0)
    sum_copy = remote(clean_sum.at[:, share], clean_sum.at[:, share], k_send.at[1], k_recv.at[1], sibling)
    sum_copy.start()
    point("clean_add")
    sum_copy.wait()
    point("sum")

    def first_back(z, carry):
        gain_sum, shift_sum = carry
        at = chunk_rows(z)
        clean = clean_sum[z].astype(F32)
        upstream = (send_h[1, z].astype(F32) + recv_h[1, z].astype(F32)).reshape(chunk, width)
        upstream = upstream + jnp.concatenate([jnp.zeros_like(clean), clean], axis=0)
        hat, inv = norm_stats(xb[z].astype(F32).reshape(chunk, width))
        total = grad_mid[at, :] + norm_back(hat, inv, gain_one[...], upstream)
        dyb[z] = total.astype(BF16).reshape(2, span, width)
        gain_sum = gain_sum + jnp.sum(upstream * hat, axis=0, keepdims=True)
        shift_sum = shift_sum + jnp.sum(upstream, axis=0, keepdims=True)
        return gain_sum, shift_sum

    pass_on(y_spread)
    sums = (zero_row, zero_row)
    for piece in range(2):
        head_copy(piece, 3).wait()
        sums = lax.fori_loop(piece * groups // 2, (piece + 1) * groups // 2, first_back, sums)
    ig_spread = spread(dyb, ig_out, i_send, i_recv, if_send, if_recv)
    keep_small(1, sums[0])
    keep_small(2, sums[1])

    def small_job():
        for bit in range(bits):
            copy = remote(small.at[...], small_r.at[bit], sm_send.at[bit], sm_recv.at[bit], partner(bit))
            copy.start()
            yield
            copy.wait()
            small[...] = small[...] + small_r[bit]

    jobs.append([small_job()])
    begin(4)
    point("first_back")
    pass_on(ig_spread)
    point("ig")
    while any(steps.gi_frame is not None for job in jobs for steps in job):
        take_round()
    small_out[...] = small[...]
    for copy in clean_copies + noisy_copies + c_copies:
        copy.wait_send()
    for onward in y_spread[2] + ig_spread[2]:
        onward.wait()
    for copy in copies:
        copy.wait()


def widen(count, *refs):
    sources, small, targets = refs[:count], refs[count], refs[count + 1:]
    for source, target in zip(sources, targets):
        target[...] = source[...].astype(target.dtype)
    row = 0
    for target in targets[count:]:
        for i in range(target.shape[0] // WIDE):
            target[i * WIDE:(i + 1) * WIDE] = small[row]
            row += 1


def local(
    layer_input, block_sizes, mixing_gain, mixing_shift, w_heads, w_output, feed_gain, feed_shift,
    w_up, bias_up, w_down, bias_down, cotangent,
):
    groups, _, span, width = layer_input.shape
    n = lax.axis_size("seq")
    head_width = w_heads.shape[2]
    hidden = w_up.shape[1]
    inner = n // groups
    pairs = head_width // LANES
    chunk = 2 * span
    rows = groups * chunk
    stack = 2 * chunk
    bits = int(math.log2(n))
    job_rows, bases = job_layout(n, width, head_width, hidden)
    small_rows = (hidden // WIDE + 5 * (width // WIDE) + 7) // 8 * 8
    out_copies = width // LANES + hidden // LANES + 3 * pairs + width // LANES
    anywhere = pl.BlockSpec(memory_space=pl.ANY)
    vmem = pl.BlockSpec(memory_space=pltpu.VMEM)
    dma = pltpu.SemaphoreType.DMA
    own = pltpu.VMEM((groups, 2, span, width), BF16)
    scratch = [
        pltpu.VMEM((3, width, head_width), BF16),
        pltpu.VMEM((head_width, width), BF16),
        pltpu.VMEM((width, hidden), BF16),
        pltpu.VMEM((hidden, width), BF16),
        own,
        own,
        own,
        pltpu.VMEM((rows, width), BF16),
        pltpu.VMEM((n, span, width), BF16),
        pltpu.VMEM((pairs, groups * stack, LANES), BF16),
        pltpu.VMEM((pairs, groups * stack, LANES), BF16),
        pltpu.VMEM((n, 2 * pairs, span, LANES), BF16),
        pltpu.VMEM((groups, 2 * pairs, span, LANES), BF16),
        pltpu.VMEM((pairs, 1, groups * stack), F32),
        pltpu.VMEM((pairs, 1, groups * stack), F32),
        pltpu.VMEM((rows, head_width), BF16),
        pltpu.VMEM((rows, width), F32),
        pltpu.VMEM((rows, hidden), BF16),
        pltpu.VMEM((rows, hidden), BF16),
        pltpu.VMEM((2, groups, 2, span, width), BF16),
        pltpu.VMEM((2, groups, 2, span, width), BF16),
        pltpu.VMEM((rows, width), F32),
        pltpu.VMEM((pairs, LANES, groups * stack), F32),
        pltpu.VMEM((n, span // 2, width), BF16),
        pltpu.VMEM((groups, inner - 1, span // 2, width), BF16),
        pltpu.VMEM((groups, span, width), BF16),
        pltpu.VMEM((bases[-1], LANES), BF16),
        pltpu.VMEM((bases[-1], LANES), BF16),
        pltpu.VMEM((small_rows, WIDE), F32),
        pltpu.VMEM((bits, small_rows, WIDE), F32),
        pltpu.VMEM((n, LANES), F32),
        pltpu.VMEM((n, LANES), F32),
        pltpu.VMEM((span, LANES), F32),
        pltpu.VMEM((span, LANES), F32),
        pltpu.VMEM((-(-hidden // WIDE // 8) * 8, WIDE), F32),
        pltpu.VMEM((8, width), F32),
        dma((6,)),
        *[dma((groups,))] * 12,
        dma((groups, inner)), dma((groups, inner)), dma((groups,)), dma((groups,)), dma((groups,)),
        dma((4, 2)), dma((4, 2)),
        dma((groups, inner)), dma((groups, inner)), dma((2,)), dma((2,)),
        *[dma((groups,))] * 8,
        dma((4, 8, 2 * bits)), dma((4, 8, 2 * bits)), pltpu.SemaphoreType.REGULAR((4, 8, bits)),
        dma((bits,)), dma((bits,)),
        dma((out_copies,)),
    ]
    out_shape = (
        jax.ShapeDtypeStruct((groups, 2, span, width), BF16),
        jax.ShapeDtypeStruct((groups, 2, span, width), BF16),
        jax.ShapeDtypeStruct((hidden, width), BF16),
        jax.ShapeDtypeStruct((width, hidden), BF16),
        jax.ShapeDtypeStruct((3, width, head_width), BF16),
        jax.ShapeDtypeStruct((head_width, width), BF16),
        jax.ShapeDtypeStruct((small_rows, WIDE), F32),
    )
    y, ig, down, up, heads, wout, small = pl.pallas_call(
        functools.partial(fused, (n, groups, span, width, head_width, hidden)),
        out_shape=out_shape,
        in_specs=[anywhere] * 6 + [pl.BlockSpec(memory_space=pltpu.SMEM)] + [vmem] * 6,
        out_specs=(anywhere,) * 6 + (vmem,),
        scratch_shapes=scratch,
        compiler_params=pltpu.CompilerParams(
            collective_id=0, has_side_effects=True, vmem_limit_bytes=VMEM_BYTES
        ),
    )(
        layer_input,
        cotangent,
        w_heads, w_output, w_up, w_down, block_sizes,
        mixing_gain, mixing_shift, feed_gain, feed_shift, bias_up, bias_down,
    )
    full = (groups, 2, span, width)
    steps = 8
    sources = (y.reshape(rows, width), ig.reshape(rows, width), heads, wout, up, down)
    kinds = (BF16,) + (F32,) * 5
    specs = []
    for source in sources:
        shape = source.shape
        block = shape[:-2] + (shape[-2] // steps, shape[-1])
        specs.append(pl.BlockSpec(block, lambda i, lead=len(shape) - 2: (0,) * lead + (i, 0)))
    vector_sizes = (hidden,) + (width,) * 5
    y, ig, heads, wout, up, down, *vectors = pl.pallas_call(
        functools.partial(widen, len(sources)),
        grid=(steps,),
        out_shape=tuple(jax.ShapeDtypeStruct(a.shape, kind) for a, kind in zip(sources, kinds))
        + tuple(jax.ShapeDtypeStruct((size,), F32) for size in vector_sizes),
        in_specs=specs + [pl.BlockSpec(small.shape, lambda i: (0, 0))],
        out_specs=tuple(specs) + tuple(pl.BlockSpec((size,), lambda i: (0,)) for size in vector_sizes),
        compiler_params=pltpu.CompilerParams(vmem_limit_bytes=VMEM_BYTES),
    )(*sources, small)
    return (y.reshape(full), ig.reshape(full), heads, wout, up, vectors[0], down, *vectors[1:])


def solution(mesh):
    in_specs = (
        P(None, None, "seq", None), P(), P(), P(), P(None, None, "head"), P("head", None), P(), P(),
        P(None, "head"), P("head"), P("head", None), P(), P(None, None, "seq", None),
    )
    out_specs = (
        P(None, None, "seq", None), P(None, None, "seq", None), P(None, None, "head"), P("head", None),
        P(None, "head"), P("head"), P("head", None), P(), P(), P(), P(), P(),
    )
    return jax.shard_map(local, mesh=mesh, in_specs=in_specs, out_specs=out_specs, check_vma=False)
```

```python
import functools
import math

import jax
import jax.numpy as jnp
from jax import lax
from jax.experimental import pallas as pl
from jax.experimental.pallas import tpu as pltpu
from jax.sharding import PartitionSpec as P

HD = 64
LANES = 128
NEG = -1e30
EPS = 1e-05
ROTARY_BASE = 10000.0
GELU_A = math.sqrt(2.0 / math.pi)
GELU_B = 0.044715
MESH = pl.DeviceIdType.MESH
F32 = jnp.float32
BF16 = jnp.bfloat16
WIDE = 256
VMEM_BYTES = 66_900_000


PART_UNITS = ((7, 7, 4, 7, 7, 4), (7, 7, 4, 7, 7, 4), (7, 7, 4), (7, 7, 4))
PART_ORDERS = ((0, 1, 2, 1, 0, 3), (0, 1, 2, 1, 0, 3), (0, 1, 2), (0, 1, 2))
TURNS = ((0, (0, 1, 2)), (0, (3, 4, 5)), (1, (0, 1, 2)), (1, (3, 4, 5)), (2, (0, 1, 2)), (3, (0, 1, 2)), (4, (0,)))
ROUNDS = {
    "half0": 1, "half1": 1, "att_back": 1, "g1p2": 1, "hq": 1, "hk": 1, "plane": 3, "first_back": 2,
}


def nn(a, b):
    return lax.dot_general(a, b, (((1,), (0,)), ((), ())), preferred_element_type=F32)


def nt(a, b):
    return lax.dot_general(a, b, (((1,), (1,)), ((), ())), preferred_element_type=F32)


def tn(a, b):
    return lax.dot_general(a, b, (((0,), (0,)), ((), ())), preferred_element_type=F32)


def lane_swap(a):
    lane = lax.broadcasted_iota(jnp.int32, a.shape, 1)
    ahead = pltpu.roll(a, LANES - HD // 2, 1)
    behind = pltpu.roll(a, HD // 2, 1)
    return jnp.where(lane % HD < HD // 2, ahead, behind)


def stack_heads(a):
    lane = lax.broadcasted_iota(jnp.int32, a.shape, 1)
    zero = jnp.zeros_like(a)
    return jnp.concatenate([jnp.where(lane < HD, a, zero), jnp.where(lane >= HD, a, zero)], axis=0)


def merge_heads(a):
    half = a.shape[1] // 2
    sub = lax.broadcasted_iota(jnp.int32, (a.shape[0], half), 0)
    return jnp.where(sub < HD, a[:, :half], a[:, half:])


def job_layout(n, width, head_width, hidden):
    whole = [hidden * width // LANES] * 2 + [2 * head_width * width // LANES] * 2
    padded = [-(-count // (16 * n)) * 16 * n for count in whole]
    return padded, [sum(padded[:i]) for i in range(len(padded) + 1)]


def fused(dims, *refs):
    n, groups, span, width, head_width, hidden = dims
    (
        x_in, c_in, wh_in, wo_in, wu_in, wd_in, blocks,
        gain_one_in, shift_one_in, gain_two_in, shift_two_in, bias_up_in, bias_down_in,
        y_out, ig_out, down_out, up_out, heads_out, wout_out, small_out,
        wh, wo, wu, wd, xb, dyb, n1, n2, nc, qs, dos, kv, kvn, lses, deltas, att,
        middle, hid, gpre, send_h, recv_h, grad_mid, dq_t, core_part, plane_part, clean_sum,
        acc, arr, small, small_r, cos_a, sin_a, cos_b, sin_b, bias_rows, vectors,
        w_sem, xc_send, xc_recv, xn_send, xn_recv, c_send, c_recv, xcf_send, xcf_recv, xnf_send, xnf_recv, cf_send, cf_recv,
        kv_send, kv_recv, loc_sem, ncf_send, ncf_recv, h_send, h_recv, g_send, g_recv, k_send, k_recv,
        y_send, y_recv, i_send, i_recv, yf_send, yf_recv, if_send, if_recv, ar_send, ar_recv, ar_free, sm_send, sm_recv, out_sem,
    ) = refs
    inner = n // groups
    job_rows, bases = job_layout(n, width, head_width, hidden)
    pairs = head_width // LANES
    chunk = 2 * span
    rows = groups * chunk
    stack = 2 * chunk
    key_ranks = min(inner, max(1, WIDE // span))
    key_blocks = inner // key_ranks
    half_rows = rows // 2
    col_tiles = width // LANES
    bits = int(math.log2(n))
    scale = 1.0 / math.sqrt(HD)
    up_bias_rows = hidden // WIDE
    gain_one, shift_one, gain_two, shift_two, bias_down = (vectors.at[i:i + 1, :] for i in range(5))

    me = lax.axis_index("seq")
    core = lax.axis_index("head")
    group = me // inner
    rank = me % inner

    def peer(seq_index):
        return (seq_index, core)

    sibling = (me, 1 - core)

    def group_peer(step):
        return (group + step) % groups

    def plane_peer(step):
        return (rank + step) % inner

    def remote(src, dst, ssem, rsem, where):
        return pltpu.make_async_remote_copy(
            src_ref=src, dst_ref=dst, send_sem=ssem, recv_sem=rsem, device_id=where, device_id_type=MESH
        )

    barrier = pltpu.get_barrier_semaphore()
    for step in range(1, groups):
        pl.semaphore_signal(barrier, inc=1, device_id=peer(group_peer(step) * inner + rank), device_id_type=MESH)
    for step in range(1, inner):
        pl.semaphore_signal(barrier, inc=1, device_id=peer(group * inner + plane_peer(step)), device_id_type=MESH)
    pl.semaphore_signal(barrier, inc=1, device_id=sibling, device_id_type=MESH)
    weight_copies = [
        pltpu.make_async_copy(wh_in, wh, w_sem.at[0]),
        pltpu.make_async_copy(wo_in, wo, w_sem.at[1]),
        pltpu.make_async_copy(wu_in, wu, w_sem.at[2]),
        pltpu.make_async_copy(wd_in, wd, w_sem.at[3]),
    ]
    own_x = pltpu.make_async_copy(x_in.at[group], xb.at[group], w_sem.at[4])
    own_c = pltpu.make_async_copy(c_in.at[group], dyb.at[group], w_sem.at[5])
    own_x.start()
    weight_copies[0].start()
    pl.semaphore_wait(barrier, groups + inner - 1)

    clean_copies, noisy_copies, c_copies = [], [], []
    clean_passes, noisy_passes, c_passes = [], [], []
    share_rows = span // 2
    share = pl.ds(pl.multiple_of(core * share_rows, share_rows), share_rows)
    other_share = pl.ds(pl.multiple_of((1 - core) * share_rows, share_rows), share_rows)
    for step in range(1, groups):
        to = group_peer(step)
        source = group_peer(groups - step)
        where = peer(to * inner + rank)
        clean_copies.append(
            remote(x_in.at[to, 1, share], xb.at[group, 1, share], xc_send.at[step], xc_recv.at[step], where)
        )
        noisy_copies.append(
            remote(x_in.at[to, 0, share], xb.at[group, 0, share], xn_send.at[step], xn_recv.at[step], where)
        )
        c_copies.append(
            remote(c_in.at[to, :, share], dyb.at[group, :, share], c_send.at[step], c_recv.at[step], where)
        )
        clean_passes.append(
            remote(xb.at[source, 1, share], xb.at[source, 1, share], xcf_send.at[step], xcf_recv.at[step], sibling)
        )
        noisy_passes.append(
            remote(xb.at[source, 0, share], xb.at[source, 0, share], xnf_send.at[step], xnf_recv.at[step], sibling)
        )
        c_passes.append(
            remote(dyb.at[source, :, share], dyb.at[source, :, share], cf_send.at[step], cf_recv.at[step], sibling)
        )
    for copy in clean_copies + noisy_copies:
        copy.start()

    def plane_copy(index, near):
        slot = index * inner + rank
        return remote(
            xb.at[index, 1, share], nc.at[slot, share], kv_send.at[index, near], kv_recv.at[index, near],
            peer(group * inner + plane_peer(near)),
        )

    def own_clean(index):
        return pltpu.make_async_copy(xb.at[index, 1, share], nc.at[index * inner + rank, share], loc_sem.at[index])

    def plane_send(index):
        for near in range(1, inner):
            plane_copy(index, near).start()
        own_clean(index).start()

    def plane_pass(index):
        at = pl.ds(index * inner, inner)
        return remote(nc.at[at, share], nc.at[at, share], ncf_send.at[index], ncf_recv.at[index], sibling)

    def plane_done(index):
        own_clean(index).wait()
        for near in range(1, inner):
            plane_copy(index, near).wait()
        plane_pass(index).start()

    own_x.wait()
    plane_send(group)
    for copy in weight_copies[1:]:
        copy.start()
    own_c.start()

    size_b = blocks[group]
    lane_q = lax.broadcasted_iota(jnp.int32, (1, stack), 1)
    in_chunk = lane_q % chunk
    clean_q = in_chunk >= span
    start_q = (in_chunk % span) & (-size_b)
    limit_q = start_q + jnp.where(clean_q, size_b, 0)

    def norm_stats(x):
        center = jnp.mean(x, axis=-1, keepdims=True)
        off = x - center
        inv = lax.rsqrt(jnp.mean(off * off, axis=-1, keepdims=True) + EPS)
        return off * inv, inv

    for row in range(up_bias_rows):
        bias_rows[row:row + 1, :] = bias_up_in[row * WIDE:(row + 1) * WIDE].reshape(1, WIDE)
    for row, vector in enumerate((gain_one_in, shift_one_in, gain_two_in, shift_two_in, bias_down_in)):
        vectors[row:row + 1, :] = vector[...].reshape(1, width)

    half_head = HD // 2
    lane = lax.broadcasted_iota(jnp.int32, (1, LANES), 1)
    frequency = jnp.exp((lane % half_head).astype(F32) * (-math.log(ROTARY_BASE) / half_head))
    sign = jnp.where(lane % HD < half_head, -1.0, 1.0)
    start = lax.broadcasted_iota(jnp.int32, (n, LANES), 0) * span
    angle = start.astype(F32) * frequency
    cos_a[...] = jnp.cos(angle)
    sin_a[...] = jnp.sin(angle) * sign
    angle = lax.broadcasted_iota(jnp.int32, (span, LANES), 0).astype(F32) * frequency
    cos_b[...] = jnp.cos(angle)
    sin_b[...] = jnp.sin(angle) * sign

    def tables(slot):
        cos = cos_a[pl.ds(slot, 1), :]
        sin = sin_a[pl.ds(slot, 1), :]
        return cos * cos_b[...] - sin * sin_b[...], sin * cos_b[...] + cos * sin_b[...]

    def turn(value, table):
        return value * table[0] + lane_swap(value) * table[1]

    def turn_back(value, table):
        return value * table[0] - lane_swap(value) * table[1]

    def twice(table):
        return tuple(jnp.concatenate([part, part], axis=0) for part in table)

    def many(first, count):
        parts = [tables(first + i) for i in range(count)]
        return tuple(jnp.concatenate([part[i] for part in parts], axis=0) for i in range(2))

    weight_copies[0].wait()
    for step in range(1, groups):
        clean_copies[step - 1].wait_recv()
        plane_send(group_peer(groups - step))
        clean_passes[step - 1].start()
    for step in range(1, groups):
        noisy_copies[step - 1].wait_recv()
        noisy_passes[step - 1].start()
    for copy in c_copies:
        copy.start()

    def clean_rows(first):
        at = pl.ds(first, key_ranks)
        x = nc[at].reshape(key_ranks * span, width).astype(F32)
        hat, _ = norm_stats(x)
        normed = (hat * gain_one[...] + shift_one[...]).astype(BF16)
        nc[at] = normed.reshape(key_ranks, span, width)
        table = many(first, key_ranks)
        for kind in range(2):
            out = nn(normed, wh[kind + 1])
            for p in range(pairs):
                part = out[:, p * LANES:(p + 1) * LANES]
                low = (part if kind else turn(part, table)).astype(BF16)
                kv[at, kind * pairs + p] = low.reshape(key_ranks, span, LANES)

    def clean_group(index):
        plane_pass(index).wait()
        for block in range(key_blocks):
            clean_rows(index * inner + block * key_ranks)

    def first_norm(z, carry):
        hat, _ = norm_stats(xb[z].reshape(chunk, width).astype(F32))
        n1[z] = (hat * gain_one[...] + shift_one[...]).astype(BF16).reshape(2, span, width)
        return carry

    plane_done(group)
    for copy in clean_passes + noisy_passes:
        copy.wait()
    lax.fori_loop(0, groups, first_norm, 0)

    def queries(z, carry):
        out = nn(n1[z].reshape(chunk, width), wh[0])
        table = twice(tables(z * inner + rank))
        at_q = pl.ds(pl.multiple_of(z * stack, stack), stack)
        for p in range(pairs):
            low = (turn(out[:, p * LANES:(p + 1) * LANES], table) * scale).astype(BF16)
            qs[p, at_q, :] = stack_heads(low)
        return carry

    lax.fori_loop(0, groups, queries, 0)
    noisy_rows = n1[:, 0].reshape(groups * span, width)
    for kind in range(2):
        out = nn(noisy_rows, wh[kind + 1])
        for z in range(groups):
            table = tables(z * inner + rank)
            for p in range(pairs):
                part = out[z * span:(z + 1) * span, p * LANES:(p + 1) * LANES]
                kvn[z, kind * pairs + p] = (part if kind else turn(part, table)).astype(BF16)
    for step in range(1, groups):
        plane_done(group_peer(groups - step))

    def clean_mask(index, first_rank, count, shape):
        key = lax.broadcasted_iota(jnp.int32, shape, 0) + first_rank * span
        return key < limit_q + rank * span

    def noisy_mask(shape):
        key = lax.broadcasted_iota(jnp.int32, shape, 0) & (-size_b)
        return (key == start_q) & jnp.logical_not(clean_q)

    def feed_back(i, carry):
        cols = pl.ds(pl.multiple_of(i * WIDE, WIDE), WIDE)
        gpre[:, cols] = nt(dyb[...].reshape(rows, width), wd[cols, :]).astype(BF16)
        return carry

    def head_send(piece, value, which):
        at = slice(piece * groups // 2, (piece + 1) * groups // 2)
        send_h[which % 2, at] = value.astype(BF16).reshape(groups // 2, 2, span, width)
        if which != 2:
            head_copy(piece, which).start()

    def head_copy(piece, which):
        at = pl.ds(piece * groups // 2, groups // 2)
        return remote(
            send_h.at[which % 2, at], recv_h.at[which % 2, at], h_send.at[which, piece], h_recv.at[which, piece], sibling
        )

    for index in range(groups):
        clean_group(index)

        def attend(p, carry, index=index):
            q = qs[p, index * stack:(index + 1) * stack, :]
            pieces = []
            top = None
            for g in range(index + 1):
                keys = kv[g * inner:(g + 1) * inner, p].reshape(inner * span, LANES)
                s = nt(keys, q)
                if g == index:
                    s = jnp.where(clean_mask(index, 0, inner, s.shape), s, NEG)
                pieces.append(s)
                best = jnp.max(s, axis=0, keepdims=True)
                top = best if top is None else jnp.maximum(top, best)
            s = nt(kvn[index, p], q)
            s = jnp.where(noisy_mask(s.shape), s, NEG)
            top = jnp.maximum(top, jnp.max(s, axis=0, keepdims=True))
            e = jnp.exp(s - top)
            total = jnp.sum(e, axis=0, keepdims=True)
            out = tn(kvn[index, pairs + p], e.astype(BF16))
            for g in range(index + 1):
                e = jnp.exp(pieces[g] - top)
                total = total + jnp.sum(e, axis=0, keepdims=True)
                vals = kv[g * inner:(g + 1) * inner, pairs + p].reshape(inner * span, LANES)
                out = out + tn(vals, e.astype(BF16))
            lses[p, :, index * stack:(index + 1) * stack] = top + jnp.log(total)
            merged = merge_heads(out / total)
            rows_out = jnp.transpose(merged)
            dq_t[p, :, index * stack:index * stack + chunk] = merged
            at = pl.ds(pl.multiple_of(p * LANES, LANES), LANES)
            att[index * chunk:(index + 1) * chunk, at] = rows_out.astype(BF16)
            return carry

        lax.fori_loop(0, pairs, attend, 0)
        if index == 0:
            weight_copies[1].wait()
        if index % (groups // 2) == groups // 2 - 1:
            piece = index // (groups // 2)
            head_send(piece, nn(att[piece * half_rows:(piece + 1) * half_rows, :], wo[...]), 0)
        if index == groups // 2:
            own_c.wait()
            for copy, onward in zip(c_copies, c_passes):
                copy.wait_recv()
                onward.start()

    weight_copies[2].wait()
    weight_copies[3].wait()
    for copy in c_passes:
        copy.wait()
    lax.fori_loop(0, up_bias_rows, feed_back, 0)

    def chunk_rows(z):
        return pl.ds(pl.multiple_of(z * chunk, chunk), chunk)

    def second_norm(z, carry):
        at = chunk_rows(z)
        mixed = send_h[0, z].astype(F32) + recv_h[0, z].astype(F32)
        mid = (xb[z].astype(F32) + mixed).reshape(chunk, width)
        middle[at, :] = mid
        hat, _ = norm_stats(mid)
        n2[at, :] = (hat * gain_two[...] + shift_two[...]).astype(BF16)
        return carry

    for piece in range(2):
        head_copy(piece, 0).wait()
        lax.fori_loop(piece * groups // 2, (piece + 1) * groups // 2, second_norm, 0)

    small[...] = jnp.zeros_like(small)
    half_hidden = hidden // 2
    half_blocks = up_bias_rows // 2

    def feed(i, carry):
        cols = pl.ds(pl.multiple_of(i * WIDE, WIDE), WIDE)
        bias = bias_rows[pl.ds(i, 1), :]
        dy = dyb[...].reshape(rows, width)
        sums = jnp.zeros((1, WIDE), F32)
        for part in range(2):
            lo = part * half_rows
            v = nn(n2[lo:lo + half_rows, :], wu[:, cols]) + bias
            back = gpre[lo:lo + half_rows, cols].astype(F32)
            sq = v * v
            t = jnp.tanh(GELU_A * v * (1.0 + GELU_B * sq))
            half = 0.5 * (1.0 + t)
            hid[lo:lo + half_rows, cols] = (v * half).astype(BF16)
            slope = half + 0.5 * v * (1.0 - t * t) * (GELU_A * (1.0 + 3.0 * GELU_B * sq))
            low = (back * slope).astype(BF16)
            gpre[lo:lo + half_rows, cols] = low
            sums = sums + jnp.sum(low.astype(F32), axis=0, keepdims=True)
        small[pl.ds(i, 1), :] = sums
        down = tn(hid[:, cols], dy)
        for c in range(col_tiles):
            lead = (i // half_blocks) * (col_tiles * half_hidden) + c * half_hidden
            at = pl.ds(pl.multiple_of(lead + (i % half_blocks) * WIDE, WIDE), WIDE)
            acc[at, :] = down[:, c * LANES:(c + 1) * LANES].astype(BF16)
        return carry

    def feed_up(i, carry):
        cols = pl.ds(pl.multiple_of(i * WIDE, WIDE), WIDE)
        up = tn(n2[...], gpre[:, cols])
        for c in range(WIDE // LANES):
            at = pl.ds(pl.multiple_of(bases[1] + (i * (WIDE // LANES) + c) * width, LANES), width)
            acc[at, :] = up[:, c * LANES:(c + 1) * LANES].astype(BF16)
        return carry

    low_bits = int(math.log2(inner))
    plane_bits, group_bits = list(range(low_bits)), list(range(low_bits, bits))
    turned_bits = plane_bits[1::-1] + plane_bits[2:]
    orders = [
        plane_bits + group_bits,
        turned_bits + group_bits,
        group_bits + plane_bits,
        group_bits + turned_bits,
        turned_bits[:1] + group_bits + turned_bits[1:],
        plane_bits[:1] + group_bits + plane_bits[1:],
    ]

    def bit_of(bit):
        return (me // (1 << bit)) % 2

    def partner(bit):
        return peer(me + (1 - 2 * bit_of(bit)) * (1 << bit))

    def part_edges(job):
        weights = PART_UNITS[job]
        units = job_rows[job] // n // 16
        total = sum(weights)
        return [(2 * sum(weights[:i]) * units + total) // (2 * total) for i in range(len(weights) + 1)]

    def sum_steps(job, part):
        edges = part_edges(job)
        base = bases[job] + n * 16 * edges[part]
        s = 16 * (edges[part + 1] - edges[part])
        order = orders[PART_ORDERS[job][part]]
        if s == 0:
            return
        lo = 0
        size = n

        def at(ref, first, count):
            return ref.at[pl.ds(pl.multiple_of(base + first * s, 16), count * s)]

        for k, bit in enumerate(order):
            half = size // 2
            mine = lo + bit_of(bit) * half
            other = lo + (1 - bit_of(bit)) * half
            copy = remote(
                at(acc, other, half), at(arr, n - size, half),
                ar_send.at[job, part, k], ar_recv.at[job, part, k], partner(bit),
            )
            copy.start()
            yield
            copy.wait()
            pl.semaphore_signal(ar_free.at[job, part, k], inc=1, device_id=partner(bit), device_id_type=MESH)

            def add(i, carry, mine=mine, size=size):
                to = pl.ds(pl.multiple_of(base + mine * s + i * s, 16), s)
                frm = pl.ds(pl.multiple_of(base + (n - size) * s + i * s, 16), s)
                acc[to, :] = (acc[to, :].astype(F32) + arr[frm, :].astype(F32)).astype(BF16)
                return carry

            lax.fori_loop(0, half, add, 0)
            lo, size = mine, half
        for k, bit in reversed(list(enumerate(order))):
            pl.semaphore_wait(ar_free.at[job, part, k], 1)
            copy = remote(
                at(acc, lo, size), at(acc, lo, size),
                ar_send.at[job, part, bits + k], ar_recv.at[job, part, bits + k], partner(bit),
            )
            copy.start()
            yield
            copy.wait()
            lo = lo - bit_of(bit) * size
            size = size * 2

    jobs = [[sum_steps(job, part) for part in range(len(PART_UNITS[job]))] for job in range(len(job_rows))]
    query_base = bases[2] + col_tiles * head_width
    copies = []
    finished = set()
    outs = [[], [], [], []]
    for c in range(col_tiles):
        at = slice(c * LANES, (c + 1) * LANES)
        for part in range(2):
            lead = bases[0] + (part * col_tiles + c) * (hidden // 2)
            outs[0].append(
                (acc.at[pl.ds(lead, hidden // 2)], down_out.at[pl.ds(part * (hidden // 2), hidden // 2), at])
            )
        outs[2].append((acc.at[pl.ds(bases[2] + c * head_width, head_width)], wout_out.at[:, at]))
    for c in range(hidden // LANES):
        at = slice(c * LANES, (c + 1) * LANES)
        outs[1].append((acc.at[pl.ds(bases[1] + c * width, width)], up_out.at[:, at]))
    for p in range(pairs):
        at = slice(p * LANES, (p + 1) * LANES)
        outs[2].append((acc.at[pl.ds(query_base + p * width, width)], heads_out.at[0, :, at]))
        for kind in range(2):
            outs[3].append(
                (acc.at[pl.ds(bases[3] + (kind * pairs + p) * width, width)], heads_out.at[kind + 1, :, at])
            )
    sem_at = 0

    def finish(job):
        nonlocal sem_at
        for src, dst in outs[job]:
            copy = pltpu.make_async_copy(src, dst, out_sem.at[sem_at])
            copy.start()
            copies.append(copy)
            sem_at += 1


    def advance(job, part):
        next(jobs[job][part], None)
        if job < 4 and job not in finished and all(steps.gi_frame is None for steps in jobs[job]):
            finish(job)
            finished.add(job)


    released = set()
    running, waiting = [], list(TURNS)

    def take_round():
        for job, parts in running:
            for part in parts:
                advance(job, part)
        if waiting and waiting[0][0] in released:
            job, parts = waiting.pop(0)
            running.append((job, parts))
            for part in parts:
                advance(job, part)

    def point(name):
        for _ in range(ROUNDS.get(name, 0)):
            take_round()

    def begin(job):
        released.add(job)

    for job, work in enumerate((feed, feed_up)):
        lax.fori_loop(0, half_blocks, work, 0)
        if part_edges(job)[3] * 2 == part_edges(job)[-1]:
            begin(job)
        point(f"half{job}")
        lax.fori_loop(half_blocks, up_bias_rows, work, 0)
        begin(job)
        point(f"whole{job}")

    for piece in range(2):
        lo = piece * half_rows
        head_send(piece, nt(gpre[lo:lo + half_rows, :], wu[...]), 1)
    point("back2")
    for piece in range(2):
        lo = piece * half_rows
        head_send(piece, nn(hid[lo:lo + half_rows, :], wd[...]), 2)
    point("fed")

    def norm_back(hat, inv, gain, upstream):
        scaled = upstream * gain
        first = jnp.mean(scaled, axis=-1, keepdims=True)
        second = jnp.mean(scaled * hat, axis=-1, keepdims=True)
        return inv * (scaled - first - hat * second)

    def second_back(z, carry):
        gain_sum, shift_sum, bias_sum = carry
        at = chunk_rows(z)
        upstream = (send_h[1, z].astype(F32) + recv_h[1, z].astype(F32)).reshape(chunk, width)
        hat, inv = norm_stats(middle[at, :])
        dy = dyb[z].astype(F32).reshape(chunk, width)
        total = dy + norm_back(hat, inv, gain_two[...], upstream)
        grad_mid[at, :] = total
        n2[at, :] = total.astype(BF16)
        gain_sum = gain_sum + jnp.sum(upstream * hat, axis=0, keepdims=True)
        shift_sum = shift_sum + jnp.sum(upstream, axis=0, keepdims=True)
        bias_sum = bias_sum + jnp.sum(dy, axis=0, keepdims=True)
        return gain_sum, shift_sum, bias_sum

    zero_row = jnp.zeros((1, width), F32)
    sums = (zero_row, zero_row, zero_row)
    for piece in range(2):
        head_copy(piece, 1).wait()
        sums = lax.fori_loop(piece * groups // 2, (piece + 1) * groups // 2, second_back, sums)

    def keep_small(which, row):
        for c in range(width // WIDE):
            at = up_bias_rows + which * (width // WIDE) + c
            small[at:at + 1, :] = row[:, c * WIDE:(c + 1) * WIDE]

    keep_small(0, sums[2])
    keep_small(3, sums[0])
    keep_small(4, sums[1])
    for piece in range(2):
        head_copy(piece, 2).start()
    point("second_back")

    def attended_back(z, carry):
        at = chunk_rows(z)
        back = nt(n2[at, :], wo[...])
        at_q = pl.ds(pl.multiple_of(z * stack, stack), stack)
        for p in range(pairs):
            low = back[:, p * LANES:(p + 1) * LANES].astype(BF16)
            dos[p, at_q, :] = stack_heads(low)
            at_o = pl.ds(pl.multiple_of(z * stack, stack), chunk)
            prod = jnp.transpose(low.astype(F32)) * dq_t[p, :, at_o]
            d0 = jnp.sum(prod[:HD], axis=0, keepdims=True)
            d1 = jnp.sum(prod[HD:], axis=0, keepdims=True)
            deltas[p, :, at_q] = jnp.concatenate([d0, d1], axis=1)
        return carry

    lax.fori_loop(0, groups, attended_back, 0)
    point("att_back")

    def feed_out(z, carry):
        at = chunk_rows(z)
        fed = (send_h[0, z].astype(F32) + recv_h[0, z].astype(F32)).reshape(chunk, width)
        dyb[z] = (middle[at, :] + fed + bias_down[...]).astype(BF16).reshape(2, span, width)
        return carry

    for piece in range(2):
        head_copy(piece, 2).wait()
    lax.fori_loop(0, groups, feed_out, 0)

    point("feed_out")
    def spread(buf, out, ssem, rsem, psend, precv):
        copies, passes = [], []
        own = pltpu.make_async_copy(buf.at[group], out.at[group], ssem.at[0])
        own.start()
        for step in range(1, groups):
            to = group_peer(step)
            source = group_peer(groups - step)
            copies.append(
                remote(buf.at[to, :, share], out.at[group, :, share], ssem.at[step], rsem.at[step], peer(to * inner + rank))
            )
            passes.append(remote(out.at[source, :, share], out.at[source, :, share], psend.at[step], precv.at[step], sibling))
        for copy in copies:
            copy.start()
        return own, copies, passes

    def pass_on(spread_out):
        own, copies, passes = spread_out
        own.wait()
        for copy, onward in zip(copies, passes):
            copy.wait()
            onward.start()

    y_spread = spread(dyb, y_out, y_send, y_recv, yf_send, yf_recv)


    wout = tn(att[...], n2[...])
    for c in range(col_tiles):
        at = bases[2] + c * head_width
        acc[at:at + head_width, :] = wout[:, c * LANES:(c + 1) * LANES].astype(BF16)
    point("wout")

    def noisy_back(p, carry):
        for index in range(groups):
            at = slice(index * stack, (index + 1) * stack)
            q = qs[p, at, :]
            do = dos[p, at, :]
            keys = kvn[index, p]
            s = nt(keys, q)
            s = jnp.where(noisy_mask(s.shape), s, NEG)
            e = jnp.exp(s - lses[p, :, at])
            dp = nt(kvn[index, pairs + p], do)
            ds = (e * (dp - deltas[p, :, at])).astype(BF16)
            at_n = slice(index * span, (index + 1) * span)
            cols = pl.multiple_of(head_width + p * LANES, LANES)
            gpre[at_n, pl.ds(cols, LANES)] = turn_back(nn(ds, q), tables(index * inner + rank)).astype(BF16)
            cols = pl.multiple_of(2 * head_width + p * LANES, LANES)
            gpre[at_n, pl.ds(cols, LANES)] = nn(e.astype(BF16), do).astype(BF16)
            dq_t[p, :, at] = tn(keys, ds)
        return carry

    lax.fori_loop(0, pairs, noisy_back, 0)
    point("noisy")

    for index in range(groups):
        for block in range(key_blocks):
            first = index * inner + block * key_ranks

            def clean_back(p, carry, index=index, block=block, first=first):
                at = slice(index * stack, groups * stack)
                q = qs[p, at, :]
                do = dos[p, at, :]
                keys = kv[first:first + key_ranks, p].reshape(key_ranks * span, LANES)
                vals = kv[first:first + key_ranks, pairs + p].reshape(key_ranks * span, LANES)
                s = nt(keys, q)
                own = s[:, :stack]
                own = jnp.where(clean_mask(index, block * key_ranks, key_ranks, own.shape), own, NEG)
                if index < groups - 1:
                    s = jnp.concatenate([own, s[:, stack:]], axis=1)
                else:
                    s = own
                e = jnp.exp(s - lses[p, :, at])
                dp = nt(vals, do)
                ds = (e * (dp - deltas[p, :, at])).astype(BF16)
                dv = nn(e.astype(BF16), do).astype(BF16)
                dk = turn_back(nn(ds, q), many(first, key_ranks)).astype(BF16)
                dq_t[p, :, at] += tn(keys, ds)
                kv[first:first + key_ranks, p] = dk.reshape(key_ranks, span, LANES)
                kv[first:first + key_ranks, pairs + p] = dv.reshape(key_ranks, span, LANES)
                return carry

            if index < groups // 2:
                for p in range(pairs):
                    clean_back(p, 0)
                    point(f"g{index}p{p}")
            else:
                lax.fori_loop(0, pairs, clean_back, 0)
                point(f"g{index}")

    def query_grads(index, carry):
        at = chunk_rows(index)
        at_q = pl.ds(pl.multiple_of(index * stack, stack), stack)
        table = twice(tables(index * inner + rank))
        for p in range(pairs):
            gq = jnp.transpose(merge_heads(dq_t[p, :, at_q])) * scale
            gpre[at, p * LANES:(p + 1) * LANES] = turn_back(gq, table).astype(BF16)
        return carry

    def keep_heads(part, base):
        for p in range(part.shape[1] // LANES):
            at = base + p * width
            acc[at:at + width, :] = part[:, p * LANES:(p + 1) * LANES].astype(BF16)

    lax.fori_loop(0, groups, query_grads, 0)
    point("qg")
    keep_heads(tn(n1[...].reshape(rows, width), gpre[:, :head_width]), query_base)
    begin(2)
    point("hq")
    sweep = min(n, 16)
    many_rows = sweep * span
    widths = 2 * pairs if n <= 16 else pairs
    for lead in range(0, 2 * pairs, widths):
        at = head_width + lead * LANES
        part = tn(n1[:, 0].reshape(groups * span, width), gpre[:groups * span, at:at + widths * LANES])
        for first in range(0, n, sweep):
            gates = jnp.concatenate(
                [kv[first:first + sweep, lead + i].reshape(many_rows, LANES) for i in range(widths)], axis=1
            )
            part = part + tn(nc[first:first + sweep].reshape(many_rows, width), gates)
        keep_heads(part, bases[3] + lead * width)
    begin(3)
    point("hk")

    def clean_input(block, carry):
        at = pl.ds(block * key_ranks, key_ranks)
        total = None
        for kind in range(2):
            gates = jnp.concatenate(
                [kv[at, kind * pairs + p].reshape(key_ranks * span, LANES) for p in range(pairs)], axis=1
            )
            back = nt(gates, wh[kind + 1])
            total = back if total is None else total + back
        nc[at] = total.astype(BF16).reshape(key_ranks, span, width)
        return carry

    lax.fori_loop(0, n // key_ranks, clean_input, 0)
    core_copy = remote(nc.at[:, other_share], core_part, k_send.at[0], k_recv.at[0], sibling)
    core_copy.start()
    point("clean_in")


    for piece in range(2):
        lo = piece * half_rows
        back = nt(gpre[lo:lo + half_rows, :head_width], wh[0]).reshape(groups // 2, 2, span, width)
        lo = lo // 2
        extra = nt(gpre[lo:lo + half_rows // 2, head_width:2 * head_width], wh[1])
        extra = extra + nt(gpre[lo:lo + half_rows // 2, 2 * head_width:3 * head_width], wh[2])
        extra = extra.reshape(groups // 2, span, width)
        at = slice(piece * groups // 2, (piece + 1) * groups // 2)
        send_h[1, at, 0] = (back[:, 0] + extra).astype(BF16)
        send_h[1, at, 1] = back[:, 1].astype(BF16)
        head_copy(piece, 3).start()
    point("back1")
    core_copy.wait()

    def core_add(slot, carry):
        nc[slot, share] = (nc[slot, share].astype(F32) + core_part[slot].astype(F32)).astype(BF16)
        return carry

    lax.fori_loop(0, n, core_add, 0)
    point("core_add")

    def part_copy(index, near):
        dest = plane_peer(near)
        return remote(
            nc.at[index * inner + dest, share], plane_part.at[index, near - 1], g_send.at[index, near],
            g_recv.at[index, near], peer(group * inner + dest),
        )

    for index in range(groups):
        for near in range(1, inner):
            part_copy(index, near).start()
    point("plane")
    for index in range(groups):
        for near in range(1, inner):
            part_copy(index, near).wait()

    def clean_add(index, carry):
        total = nc[index * inner + rank, share].astype(F32)
        for near in range(inner - 1):
            total = total + plane_part[index, near].astype(F32)
        clean_sum[index, share] = total.astype(BF16)
        return carry

    lax.fori_loop(0, groups, clean_add, 0)
    sum_copy = remote(clean_sum.at[:, share], clean_sum.at[:, share], k_send.at[1], k_recv.at[1], sibling)
    sum_copy.start()
    point("clean_add")
    sum_copy.wait()
    point("sum")

    def first_back(z, carry):
        gain_sum, shift_sum = carry
        at = chunk_rows(z)
        clean = clean_sum[z].astype(F32)
        upstream = (send_h[1, z].astype(F32) + recv_h[1, z].astype(F32)).reshape(chunk, width)
        upstream = upstream + jnp.concatenate([jnp.zeros_like(clean), clean], axis=0)
        hat, inv = norm_stats(xb[z].astype(F32).reshape(chunk, width))
        total = grad_mid[at, :] + norm_back(hat, inv, gain_one[...], upstream)
        dyb[z] = total.astype(BF16).reshape(2, span, width)
        gain_sum = gain_sum + jnp.sum(upstream * hat, axis=0, keepdims=True)
        shift_sum = shift_sum + jnp.sum(upstream, axis=0, keepdims=True)
        return gain_sum, shift_sum

    pass_on(y_spread)
    sums = (zero_row, zero_row)
    for piece in range(2):
        head_copy(piece, 3).wait()
        sums = lax.fori_loop(piece * groups // 2, (piece + 1) * groups // 2, first_back, sums)
    ig_spread = spread(dyb, ig_out, i_send, i_recv, if_send, if_recv)
    keep_small(1, sums[0])
    keep_small(2, sums[1])

    def small_job():
        for bit in range(bits):
            copy = remote(small.at[...], small_r.at[bit], sm_send.at[bit], sm_recv.at[bit], partner(bit))
            copy.start()
            yield
            copy.wait()
            small[...] = small[...] + small_r[bit]

    jobs.append([small_job()])
    begin(4)
    point("first_back")
    pass_on(ig_spread)
    point("ig")
    while any(steps.gi_frame is not None for job in jobs for steps in job):
        take_round()
    small_out[...] = small[...]
    for copy in clean_copies + noisy_copies + c_copies:
        copy.wait_send()
    for onward in y_spread[2] + ig_spread[2]:
        onward.wait()
    for copy in copies:
        copy.wait()


def widen(count, *refs):
    sources, small, targets = refs[:count], refs[count], refs[count + 1:]
    for source, target in zip(sources, targets):
        target[...] = source[...].astype(target.dtype)
    row = 0
    for target in targets[count:]:
        for i in range(target.shape[0] // WIDE):
            target[i * WIDE:(i + 1) * WIDE] = small[row]
            row += 1


def local(
    layer_input, block_sizes, mixing_gain, mixing_shift, w_heads, w_output, feed_gain, feed_shift,
    w_up, bias_up, w_down, bias_down, cotangent,
):
    groups, _, span, width = layer_input.shape
    n = lax.axis_size("seq")
    head_width = w_heads.shape[2]
    hidden = w_up.shape[1]
    inner = n // groups
    pairs = head_width // LANES
    chunk = 2 * span
    rows = groups * chunk
    stack = 2 * chunk
    bits = int(math.log2(n))
    job_rows, bases = job_layout(n, width, head_width, hidden)
    small_rows = (hidden // WIDE + 5 * (width // WIDE) + 7) // 8 * 8
    out_copies = 2 * (width // LANES) + hidden // LANES + 3 * pairs + width // LANES
    anywhere = pl.BlockSpec(memory_space=pl.ANY)
    vmem = pl.BlockSpec(memory_space=pltpu.VMEM)
    dma = pltpu.SemaphoreType.DMA
    own = pltpu.VMEM((groups, 2, span, width), BF16)
    scratch = [
        pltpu.VMEM((3, width, head_width), BF16),
        pltpu.VMEM((head_width, width), BF16),
        pltpu.VMEM((width, hidden), BF16),
        pltpu.VMEM((hidden, width), BF16),
        own,
        own,
        own,
        pltpu.VMEM((rows, width), BF16),
        pltpu.VMEM((n, span, width), BF16),
        pltpu.VMEM((pairs, groups * stack, LANES), BF16),
        pltpu.VMEM((pairs, groups * stack, LANES), BF16),
        pltpu.VMEM((n, 2 * pairs, span, LANES), BF16),
        pltpu.VMEM((groups, 2 * pairs, span, LANES), BF16),
        pltpu.VMEM((pairs, 1, groups * stack), F32),
        pltpu.VMEM((pairs, 1, groups * stack), F32),
        pltpu.VMEM((rows, head_width), BF16),
        pltpu.VMEM((rows, width), F32),
        pltpu.VMEM((rows, hidden), BF16),
        pltpu.VMEM((rows, hidden), BF16),
        pltpu.VMEM((2, groups, 2, span, width), BF16),
        pltpu.VMEM((2, groups, 2, span, width), BF16),
        pltpu.VMEM((rows, width), F32),
        pltpu.VMEM((pairs, LANES, groups * stack), F32),
        pltpu.VMEM((n, span // 2, width), BF16),
        pltpu.VMEM((groups, inner - 1, span // 2, width), BF16),
        pltpu.VMEM((groups, span, width), BF16),
        pltpu.VMEM((bases[-1], LANES), BF16),
        pltpu.VMEM((bases[-1], LANES), BF16),
        pltpu.VMEM((small_rows, WIDE), F32),
        pltpu.VMEM((bits, small_rows, WIDE), F32),
        pltpu.VMEM((n, LANES), F32),
        pltpu.VMEM((n, LANES), F32),
        pltpu.VMEM((span, LANES), F32),
        pltpu.VMEM((span, LANES), F32),
        pltpu.VMEM((-(-hidden // WIDE // 8) * 8, WIDE), F32),
        pltpu.VMEM((8, width), F32),
        dma((6,)),
        *[dma((groups,))] * 12,
        dma((groups, inner)), dma((groups, inner)), dma((groups,)), dma((groups,)), dma((groups,)),
        dma((4, 2)), dma((4, 2)),
        dma((groups, inner)), dma((groups, inner)), dma((2,)), dma((2,)),
        *[dma((groups,))] * 8,
        dma((4, 8, 2 * bits)), dma((4, 8, 2 * bits)), pltpu.SemaphoreType.REGULAR((4, 8, bits)),
        dma((bits,)), dma((bits,)),
        dma((out_copies,)),
    ]
    out_shape = (
        jax.ShapeDtypeStruct((groups, 2, span, width), BF16),
        jax.ShapeDtypeStruct((groups, 2, span, width), BF16),
        jax.ShapeDtypeStruct((hidden, width), BF16),
        jax.ShapeDtypeStruct((width, hidden), BF16),
        jax.ShapeDtypeStruct((3, width, head_width), BF16),
        jax.ShapeDtypeStruct((head_width, width), BF16),
        jax.ShapeDtypeStruct((small_rows, WIDE), F32),
    )
    y, ig, down, up, heads, wout, small = pl.pallas_call(
        functools.partial(fused, (n, groups, span, width, head_width, hidden)),
        out_shape=out_shape,
        in_specs=[anywhere] * 6 + [pl.BlockSpec(memory_space=pltpu.SMEM)] + [vmem] * 6,
        out_specs=(anywhere,) * 6 + (vmem,),
        scratch_shapes=scratch,
        compiler_params=pltpu.CompilerParams(
            collective_id=0, has_side_effects=True, vmem_limit_bytes=VMEM_BYTES
        ),
    )(
        layer_input,
        cotangent,
        w_heads, w_output, w_up, w_down, block_sizes,
        mixing_gain, mixing_shift, feed_gain, feed_shift, bias_up, bias_down,
    )
    full = (groups, 2, span, width)
    steps = 2
    sources = (y.reshape(rows, width), ig.reshape(rows, width), heads, wout, up, down)
    kinds = (BF16,) + (F32,) * 5
    specs = []
    for source in sources:
        shape = source.shape
        block = shape[:-2] + (shape[-2] // steps, shape[-1])
        specs.append(pl.BlockSpec(block, lambda i, lead=len(shape) - 2: (0,) * lead + (i, 0)))
    vector_sizes = (hidden,) + (width,) * 5
    y, ig, heads, wout, up, down, *vectors = pl.pallas_call(
        functools.partial(widen, len(sources)),
        grid=(steps,),
        out_shape=tuple(jax.ShapeDtypeStruct(a.shape, kind) for a, kind in zip(sources, kinds))
        + tuple(jax.ShapeDtypeStruct((size,), F32) for size in vector_sizes),
        in_specs=specs + [pl.BlockSpec(small.shape, lambda i: (0, 0))],
        out_specs=tuple(specs) + tuple(pl.BlockSpec((size,), lambda i: (0,)) for size in vector_sizes),
        compiler_params=pltpu.CompilerParams(vmem_limit_bytes=VMEM_BYTES),
    )(*sources, small)
    return (y.reshape(full), ig.reshape(full), heads, wout, up, vectors[0], down, *vectors[1:])


def solution(mesh):
    in_specs = (
        P(None, None, "seq", None), P(), P(), P(), P(None, None, "head"), P("head", None), P(), P(),
        P(None, "head"), P("head"), P("head", None), P(), P(None, None, "seq", None),
    )
    out_specs = (
        P(None, None, "seq", None), P(None, None, "seq", None), P(None, None, "head"), P("head", None),
        P(None, "head"), P("head"), P("head", None), P(), P(), P(), P(), P(),
    )
    return jax.shard_map(local, mesh=mesh, in_specs=in_specs, out_specs=out_specs, check_vma=False)
```

```python
import functools
import math

import jax
import jax.numpy as jnp
from jax import lax
from jax.experimental import pallas as pl
from jax.experimental.pallas import tpu as pltpu
from jax.sharding import PartitionSpec as P

HD = 64
LANES = 128
NEG = -1e30
EPS = 1e-05
ROTARY_BASE = 10000.0
GELU_A = math.sqrt(2.0 / math.pi)
GELU_B = 0.044715
MESH = pl.DeviceIdType.MESH
F32 = jnp.float32
BF16 = jnp.bfloat16
WIDE = 256
VMEM_BYTES = 66_900_000


PART_UNITS = ((6, 6, 6, 8, 7, 3), (7, 8, 3, 8, 7, 3), (7, 8, 3), (7, 7, 4))
PART_ORDERS = ((0, 1, 2, 1, 0, 3), (0, 1, 2, 1, 0, 3), (0, 1, 2), (0, 1, 2))
TURNS = ((0, (0, 1, 2)), (0, (3, 4, 5)), (1, (0, 1, 2)), (1, (3, 4, 5)), (2, (0, 1, 2)), (3, (0, 1, 2)), (4, (0,)))
ROUNDS = {
    "half0": 1, "half1": 1, "att_back": 1, "g1p2": 1, "hq": 1, "hk": 1, "plane": 3, "first_back": 2,
}


def nn(a, b):
    return lax.dot_general(a, b, (((1,), (0,)), ((), ())), preferred_element_type=F32)


def nt(a, b):
    return lax.dot_general(a, b, (((1,), (1,)), ((), ())), preferred_element_type=F32)


def tn(a, b):
    return lax.dot_general(a, b, (((0,), (0,)), ((), ())), preferred_element_type=F32)


def lane_swap(a):
    lane = lax.broadcasted_iota(jnp.int32, a.shape, 1)
    ahead = pltpu.roll(a, LANES - HD // 2, 1)
    behind = pltpu.roll(a, HD // 2, 1)
    return jnp.where(lane % HD < HD // 2, ahead, behind)


def stack_heads(a):
    lane = lax.broadcasted_iota(jnp.int32, a.shape, 1)
    zero = jnp.zeros_like(a)
    return jnp.concatenate([jnp.where(lane < HD, a, zero), jnp.where(lane >= HD, a, zero)], axis=0)


def merge_heads(a):
    half = a.shape[1] // 2
    sub = lax.broadcasted_iota(jnp.int32, (a.shape[0], half), 0)
    return jnp.where(sub < HD, a[:, :half], a[:, half:])


def job_layout(n, width, head_width, hidden):
    whole = [hidden * width // LANES] * 2 + [2 * head_width * width // LANES] * 2
    padded = [-(-count // (16 * n)) * 16 * n for count in whole]
    return padded, [sum(padded[:i]) for i in range(len(padded) + 1)]


def fused(dims, *refs):
    n, groups, span, width, head_width, hidden = dims
    (
        x_in, c_in, wh_in, wo_in, wu_in, wd_in, blocks,
        gain_one_in, shift_one_in, gain_two_in, shift_two_in, bias_up_in, bias_down_in,
        y_out, ig_out, down_out, up_out, heads_out, wout_out, small_out,
        wh, wo, wu, wd, xb, dyb, n1, n2, nc, qs, dos, kv, kvn, lses, deltas, att,
        middle, hid, gpre, send_h, recv_h, grad_mid, dq_t, core_part, plane_part, clean_sum,
        acc, arr, small, small_r, cos_a, sin_a, cos_b, sin_b, bias_rows, vectors,
        w_sem, xc_send, xc_recv, xn_send, xn_recv, c_send, c_recv, xcf_send, xcf_recv, xnf_send, xnf_recv, cf_send, cf_recv,
        kv_send, kv_recv, loc_sem, ncf_send, ncf_recv, h_send, h_recv, g_send, g_recv, k_send, k_recv,
        y_send, y_recv, i_send, i_recv, yf_send, yf_recv, if_send, if_recv, ar_send, ar_recv, ar_free, sm_send, sm_recv, out_sem,
    ) = refs
    inner = n // groups
    job_rows, bases = job_layout(n, width, head_width, hidden)
    pairs = head_width // LANES
    chunk = 2 * span
    rows = groups * chunk
    stack = 2 * chunk
    key_ranks = min(inner, max(1, WIDE // span))
    key_blocks = inner // key_ranks
    half_rows = rows // 2
    col_tiles = width // LANES
    bits = int(math.log2(n))
    scale = 1.0 / math.sqrt(HD)
    up_bias_rows = hidden // WIDE
    gain_one, shift_one, gain_two, shift_two, bias_down = (vectors.at[i:i + 1, :] for i in range(5))

    me = lax.axis_index("seq")
    core = lax.axis_index("head")
    group = me // inner
    rank = me % inner

    def peer(seq_index):
        return (seq_index, core)

    sibling = (me, 1 - core)

    def group_peer(step):
        return (group + step) % groups

    def plane_peer(step):
        return (rank + step) % inner

    def remote(src, dst, ssem, rsem, where):
        return pltpu.make_async_remote_copy(
            src_ref=src, dst_ref=dst, send_sem=ssem, recv_sem=rsem, device_id=where, device_id_type=MESH
        )

    barrier = pltpu.get_barrier_semaphore()
    for step in range(1, groups):
        pl.semaphore_signal(barrier, inc=1, device_id=peer(group_peer(step) * inner + rank), device_id_type=MESH)
    for step in range(1, inner):
        pl.semaphore_signal(barrier, inc=1, device_id=peer(group * inner + plane_peer(step)), device_id_type=MESH)
    pl.semaphore_signal(barrier, inc=1, device_id=sibling, device_id_type=MESH)
    weight_copies = [
        pltpu.make_async_copy(wh_in, wh, w_sem.at[0]),
        pltpu.make_async_copy(wo_in, wo, w_sem.at[1]),
        pltpu.make_async_copy(wu_in, wu, w_sem.at[2]),
        pltpu.make_async_copy(wd_in, wd, w_sem.at[3]),
    ]
    own_x = pltpu.make_async_copy(x_in.at[group], xb.at[group], w_sem.at[4])
    own_c = pltpu.make_async_copy(c_in.at[group], dyb.at[group], w_sem.at[5])
    own_x.start()
    weight_copies[0].start()
    pl.semaphore_wait(barrier, groups + inner - 1)

    clean_copies, noisy_copies, c_copies = [], [], []
    clean_passes, noisy_passes, c_passes = [], [], []
    share_rows = span // 2
    share = pl.ds(pl.multiple_of(core * share_rows, share_rows), share_rows)
    other_share = pl.ds(pl.multiple_of((1 - core) * share_rows, share_rows), share_rows)
    for step in range(1, groups):
        to = group_peer(step)
        source = group_peer(groups - step)
        where = peer(to * inner + rank)
        clean_copies.append(
            remote(x_in.at[to, 1, share], xb.at[group, 1, share], xc_send.at[step], xc_recv.at[step], where)
        )
        noisy_copies.append(
            remote(x_in.at[to, 0, share], xb.at[group, 0, share], xn_send.at[step], xn_recv.at[step], where)
        )
        c_copies.append(
            remote(c_in.at[to, :, share], dyb.at[group, :, share], c_send.at[step], c_recv.at[step], where)
        )
        clean_passes.append(
            remote(xb.at[source, 1, share], xb.at[source, 1, share], xcf_send.at[step], xcf_recv.at[step], sibling)
        )
        noisy_passes.append(
            remote(xb.at[source, 0, share], xb.at[source, 0, share], xnf_send.at[step], xnf_recv.at[step], sibling)
        )
        c_passes.append(
            remote(dyb.at[source, :, share], dyb.at[source, :, share], cf_send.at[step], cf_recv.at[step], sibling)
        )
    for copy in clean_copies + noisy_copies:
        copy.start()

    def plane_copy(index, near):
        slot = index * inner + rank
        return remote(
            xb.at[index, 1, share], nc.at[slot, share], kv_send.at[index, near], kv_recv.at[index, near],
            peer(group * inner + plane_peer(near)),
        )

    def own_clean(index):
        return pltpu.make_async_copy(xb.at[index, 1, share], nc.at[index * inner + rank, share], loc_sem.at[index])

    def plane_send(index):
        for near in range(1, inner):
            plane_copy(index, near).start()
        own_clean(index).start()

    def plane_pass(index):
        at = pl.ds(index * inner, inner)
        return remote(nc.at[at, share], nc.at[at, share], ncf_send.at[index], ncf_recv.at[index], sibling)

    def plane_done(index):
        own_clean(index).wait()
        for near in range(1, inner):
            plane_copy(index, near).wait()
        plane_pass(index).start()

    own_x.wait()
    plane_send(group)
    for copy in weight_copies[1:]:
        copy.start()
    own_c.start()

    size_b = blocks[group]
    lane_q = lax.broadcasted_iota(jnp.int32, (1, stack), 1)
    in_chunk = lane_q % chunk
    clean_q = in_chunk >= span
    start_q = (in_chunk % span) & (-size_b)
    limit_q = start_q + jnp.where(clean_q, size_b, 0)

    def norm_stats(x):
        center = jnp.mean(x, axis=-1, keepdims=True)
        off = x - center
        inv = lax.rsqrt(jnp.mean(off * off, axis=-1, keepdims=True) + EPS)
        return off * inv, inv

    for row in range(up_bias_rows):
        bias_rows[row:row + 1, :] = bias_up_in[row * WIDE:(row + 1) * WIDE].reshape(1, WIDE)
    for row, vector in enumerate((gain_one_in, shift_one_in, gain_two_in, shift_two_in, bias_down_in)):
        vectors[row:row + 1, :] = vector[...].reshape(1, width)

    half_head = HD // 2
    lane = lax.broadcasted_iota(jnp.int32, (1, LANES), 1)
    frequency = jnp.exp((lane % half_head).astype(F32) * (-math.log(ROTARY_BASE) / half_head))
    sign = jnp.where(lane % HD < half_head, -1.0, 1.0)
    start = lax.broadcasted_iota(jnp.int32, (n, LANES), 0) * span
    angle = start.astype(F32) * frequency
    cos_a[...] = jnp.cos(angle)
    sin_a[...] = jnp.sin(angle) * sign
    angle = lax.broadcasted_iota(jnp.int32, (span, LANES), 0).astype(F32) * frequency
    cos_b[...] = jnp.cos(angle)
    sin_b[...] = jnp.sin(angle) * sign

    def tables(slot):
        cos = cos_a[pl.ds(slot, 1), :]
        sin = sin_a[pl.ds(slot, 1), :]
        return cos * cos_b[...] - sin * sin_b[...], sin * cos_b[...] + cos * sin_b[...]

    def turn(value, table):
        return value * table[0] + lane_swap(value) * table[1]

    def turn_back(value, table):
        return value * table[0] - lane_swap(value) * table[1]

    def twice(table):
        return tuple(jnp.concatenate([part, part], axis=0) for part in table)

    def many(first, count):
        parts = [tables(first + i) for i in range(count)]
        return tuple(jnp.concatenate([part[i] for part in parts], axis=0) for i in range(2))

    weight_copies[0].wait()
    for step in range(1, groups):
        clean_copies[step - 1].wait_recv()
        plane_send(group_peer(groups - step))
        clean_passes[step - 1].start()
    for step in range(1, groups):
        noisy_copies[step - 1].wait_recv()
        noisy_passes[step - 1].start()
    for copy in c_copies:
        copy.start()

    def clean_rows(first):
        at = pl.ds(first, key_ranks)
        x = nc[at].reshape(key_ranks * span, width).astype(F32)
        hat, _ = norm_stats(x)
        normed = (hat * gain_one[...] + shift_one[...]).astype(BF16)
        nc[at] = normed.reshape(key_ranks, span, width)
        table = many(first, key_ranks)
        for kind in range(2):
            out = nn(normed, wh[kind + 1])
            for p in range(pairs):
                part = out[:, p * LANES:(p + 1) * LANES]
                low = (part if kind else turn(part, table)).astype(BF16)
                kv[at, kind * pairs + p] = low.reshape(key_ranks, span, LANES)

    def clean_group(index):
        plane_pass(index).wait()
        for block in range(key_blocks):
            clean_rows(index * inner + block * key_ranks)

    def first_norm(z, carry):
        hat, _ = norm_stats(xb[z].reshape(chunk, width).astype(F32))
        n1[z] = (hat * gain_one[...] + shift_one[...]).astype(BF16).reshape(2, span, width)
        return carry

    plane_done(group)
    for copy in clean_passes + noisy_passes:
        copy.wait()
    lax.fori_loop(0, groups, first_norm, 0)

    def queries(z, carry):
        out = nn(n1[z].reshape(chunk, width), wh[0])
        table = twice(tables(z * inner + rank))
        at_q = pl.ds(pl.multiple_of(z * stack, stack), stack)
        for p in range(pairs):
            low = (turn(out[:, p * LANES:(p + 1) * LANES], table) * scale).astype(BF16)
            qs[p, at_q, :] = stack_heads(low)
        return carry

    lax.fori_loop(0, groups, queries, 0)
    noisy_rows = n1[:, 0].reshape(groups * span, width)
    for kind in range(2):
        out = nn(noisy_rows, wh[kind + 1])
        for z in range(groups):
            table = tables(z * inner + rank)
            for p in range(pairs):
                part = out[z * span:(z + 1) * span, p * LANES:(p + 1) * LANES]
                kvn[z, kind * pairs + p] = (part if kind else turn(part, table)).astype(BF16)
    for step in range(1, groups):
        plane_done(group_peer(groups - step))

    def clean_mask(index, first_rank, count, shape):
        key = lax.broadcasted_iota(jnp.int32, shape, 0) + first_rank * span
        return key < limit_q + rank * span

    def noisy_mask(shape):
        key = lax.broadcasted_iota(jnp.int32, shape, 0) & (-size_b)
        return (key == start_q) & jnp.logical_not(clean_q)

    def feed_back(i, carry):
        cols = pl.ds(pl.multiple_of(i * WIDE, WIDE), WIDE)
        gpre[:, cols] = nt(dyb[...].reshape(rows, width), wd[cols, :]).astype(BF16)
        return carry

    def head_send(piece, value, which):
        at = slice(piece * groups // 2, (piece + 1) * groups // 2)
        send_h[which % 2, at] = value.astype(BF16).reshape(groups // 2, 2, span, width)
        if which != 2:
            head_copy(piece, which).start()

    def head_copy(piece, which):
        at = pl.ds(piece * groups // 2, groups // 2)
        return remote(
            send_h.at[which % 2, at], recv_h.at[which % 2, at], h_send.at[which, piece], h_recv.at[which, piece], sibling
        )

    for index in range(groups):
        clean_group(index)

        def attend(p, carry, index=index):
            q = qs[p, index * stack:(index + 1) * stack, :]
            pieces = []
            top = None
            for g in range(index + 1):
                keys = kv[g * inner:(g + 1) * inner, p].reshape(inner * span, LANES)
                s = nt(keys, q)
                if g == index:
                    s = jnp.where(clean_mask(index, 0, inner, s.shape), s, NEG)
                pieces.append(s)
                best = jnp.max(s, axis=0, keepdims=True)
                top = best if top is None else jnp.maximum(top, best)
            s = nt(kvn[index, p], q)
            s = jnp.where(noisy_mask(s.shape), s, NEG)
            top = jnp.maximum(top, jnp.max(s, axis=0, keepdims=True))
            e = jnp.exp(s - top)
            total = jnp.sum(e, axis=0, keepdims=True)
            out = tn(kvn[index, pairs + p], e.astype(BF16))
            for g in range(index + 1):
                e = jnp.exp(pieces[g] - top)
                total = total + jnp.sum(e, axis=0, keepdims=True)
                vals = kv[g * inner:(g + 1) * inner, pairs + p].reshape(inner * span, LANES)
                out = out + tn(vals, e.astype(BF16))
            lses[p, :, index * stack:(index + 1) * stack] = top + jnp.log(total)
            merged = merge_heads(out / total)
            rows_out = jnp.transpose(merged)
            dq_t[p, :, index * stack:index * stack + chunk] = merged
            at = pl.ds(pl.multiple_of(p * LANES, LANES), LANES)
            att[index * chunk:(index + 1) * chunk, at] = rows_out.astype(BF16)
            return carry

        lax.fori_loop(0, pairs, attend, 0)
        if index == 0:
            weight_copies[1].wait()
        if index % (groups // 2) == groups // 2 - 1:
            piece = index // (groups // 2)
            head_send(piece, nn(att[piece * half_rows:(piece + 1) * half_rows, :], wo[...]), 0)
        if index == groups // 2:
            own_c.wait()
            for copy, onward in zip(c_copies, c_passes):
                copy.wait_recv()
                onward.start()

    weight_copies[2].wait()
    weight_copies[3].wait()
    for copy in c_passes:
        copy.wait()
    lax.fori_loop(0, up_bias_rows, feed_back, 0)

    def chunk_rows(z):
        return pl.ds(pl.multiple_of(z * chunk, chunk), chunk)

    def second_norm(z, carry):
        at = chunk_rows(z)
        mixed = send_h[0, z].astype(F32) + recv_h[0, z].astype(F32)
        mid = (xb[z].astype(F32) + mixed).reshape(chunk, width)
        middle[at, :] = mid
        hat, _ = norm_stats(mid)
        n2[at, :] = (hat * gain_two[...] + shift_two[...]).astype(BF16)
        return carry

    for piece in range(2):
        head_copy(piece, 0).wait()
        lax.fori_loop(piece * groups // 2, (piece + 1) * groups // 2, second_norm, 0)

    small[...] = jnp.zeros_like(small)
    half_hidden = hidden // 2
    half_blocks = up_bias_rows // 2

    def feed(i, carry):
        cols = pl.ds(pl.multiple_of(i * WIDE, WIDE), WIDE)
        bias = bias_rows[pl.ds(i, 1), :]
        dy = dyb[...].reshape(rows, width)
        sums = jnp.zeros((1, WIDE), F32)
        for part in range(2):
            lo = part * half_rows
            v = nn(n2[lo:lo + half_rows, :], wu[:, cols]) + bias
            back = gpre[lo:lo + half_rows, cols].astype(F32)
            sq = v * v
            t = jnp.tanh(GELU_A * v * (1.0 + GELU_B * sq))
            half = 0.5 * (1.0 + t)
            hid[lo:lo + half_rows, cols] = (v * half).astype(BF16)
            slope = half + 0.5 * v * (1.0 - t * t) * (GELU_A * (1.0 + 3.0 * GELU_B * sq))
            low = (back * slope).astype(BF16)
            gpre[lo:lo + half_rows, cols] = low
            sums = sums + jnp.sum(low.astype(F32), axis=0, keepdims=True)
        small[pl.ds(i, 1), :] = sums
        down = tn(hid[:, cols], dy)
        for c in range(col_tiles):
            lead = (i // half_blocks) * (col_tiles * half_hidden) + c * half_hidden
            at = pl.ds(pl.multiple_of(lead + (i % half_blocks) * WIDE, WIDE), WIDE)
            acc[at, :] = down[:, c * LANES:(c + 1) * LANES].astype(BF16)
        return carry

    def feed_up(i, carry):
        cols = pl.ds(pl.multiple_of(i * WIDE, WIDE), WIDE)
        up = tn(n2[...], gpre[:, cols])
        for c in range(WIDE // LANES):
            at = pl.ds(pl.multiple_of(bases[1] + (i * (WIDE // LANES) + c) * width, LANES), width)
            acc[at, :] = up[:, c * LANES:(c + 1) * LANES].astype(BF16)
        return carry

    low_bits = int(math.log2(inner))
    plane_bits, group_bits = list(range(low_bits)), list(range(low_bits, bits))
    turned_bits = plane_bits[1::-1] + plane_bits[2:]
    orders = [
        plane_bits + group_bits,
        turned_bits + group_bits,
        group_bits + plane_bits,
        group_bits + turned_bits,
        turned_bits[:1] + group_bits + turned_bits[1:],
        plane_bits[:1] + group_bits + plane_bits[1:],
    ]

    def bit_of(bit):
        return (me // (1 << bit)) % 2

    def partner(bit):
        return peer(me + (1 - 2 * bit_of(bit)) * (1 << bit))

    def part_edges(job):
        weights = PART_UNITS[job]
        units = job_rows[job] // n // 16
        total = sum(weights)
        return [(2 * sum(weights[:i]) * units + total) // (2 * total) for i in range(len(weights) + 1)]

    def sum_steps(job, part):
        edges = part_edges(job)
        base = bases[job] + n * 16 * edges[part]
        s = 16 * (edges[part + 1] - edges[part])
        order = orders[PART_ORDERS[job][part]]
        if s == 0:
            return
        lo = 0
        size = n

        def at(ref, first, count):
            return ref.at[pl.ds(pl.multiple_of(base + first * s, 16), count * s)]

        for k, bit in enumerate(order):
            half = size // 2
            mine = lo + bit_of(bit) * half
            other = lo + (1 - bit_of(bit)) * half
            copy = remote(
                at(acc, other, half), at(arr, n - size, half),
                ar_send.at[job, part, k], ar_recv.at[job, part, k], partner(bit),
            )
            copy.start()
            yield
            copy.wait()
            pl.semaphore_signal(ar_free.at[job, part, k], inc=1, device_id=partner(bit), device_id_type=MESH)

            def add(i, carry, mine=mine, size=size):
                to = pl.ds(pl.multiple_of(base + mine * s + i * s, 16), s)
                frm = pl.ds(pl.multiple_of(base + (n - size) * s + i * s, 16), s)
                acc[to, :] = (acc[to, :].astype(F32) + arr[frm, :].astype(F32)).astype(BF16)
                return carry

            lax.fori_loop(0, half, add, 0)
            lo, size = mine, half
        for k, bit in reversed(list(enumerate(order))):
            pl.semaphore_wait(ar_free.at[job, part, k], 1)
            copy = remote(
                at(acc, lo, size), at(acc, lo, size),
                ar_send.at[job, part, bits + k], ar_recv.at[job, part, bits + k], partner(bit),
            )
            copy.start()
            yield
            copy.wait()
            lo = lo - bit_of(bit) * size
            size = size * 2

    jobs = [[sum_steps(job, part) for part in range(len(PART_UNITS[job]))] for job in range(len(job_rows))]
    query_base = bases[2] + col_tiles * head_width
    copies = []
    finished = set()
    outs = [[], [], [], []]
    for c in range(col_tiles):
        at = slice(c * LANES, (c + 1) * LANES)
        for part in range(2):
            lead = bases[0] + (part * col_tiles + c) * (hidden // 2)
            outs[0].append(
                (acc.at[pl.ds(lead, hidden // 2)], down_out.at[pl.ds(part * (hidden // 2), hidden // 2), at])
            )
        outs[2].append((acc.at[pl.ds(bases[2] + c * head_width, head_width)], wout_out.at[:, at]))
    for c in range(hidden // LANES):
        at = slice(c * LANES, (c + 1) * LANES)
        outs[1].append((acc.at[pl.ds(bases[1] + c * width, width)], up_out.at[:, at]))
    for p in range(pairs):
        at = slice(p * LANES, (p + 1) * LANES)
        outs[2].append((acc.at[pl.ds(query_base + p * width, width)], heads_out.at[0, :, at]))
        for kind in range(2):
            outs[3].append(
                (acc.at[pl.ds(bases[3] + (kind * pairs + p) * width, width)], heads_out.at[kind + 1, :, at])
            )
    sem_at = 0

    def finish(job):
        nonlocal sem_at
        for src, dst in outs[job]:
            copy = pltpu.make_async_copy(src, dst, out_sem.at[sem_at])
            copy.start()
            copies.append(copy)
            sem_at += 1


    def advance(job, part):
        next(jobs[job][part], None)
        if job < 4 and job not in finished and all(steps.gi_frame is None for steps in jobs[job]):
            finish(job)
            finished.add(job)


    released = set()
    running, waiting = [], list(TURNS)

    def take_round():
        for job, parts in running:
            for part in parts:
                advance(job, part)
        if waiting and waiting[0][0] in released:
            job, parts = waiting.pop(0)
            running.append((job, parts))
            for part in parts:
                advance(job, part)

    def point(name):
        for _ in range(ROUNDS.get(name, 0)):
            take_round()

    def begin(job):
        released.add(job)

    for job, work in enumerate((feed, feed_up)):
        lax.fori_loop(0, half_blocks, work, 0)
        if part_edges(job)[3] * 2 == part_edges(job)[-1]:
            begin(job)
        point(f"half{job}")
        lax.fori_loop(half_blocks, up_bias_rows, work, 0)
        begin(job)
        point(f"whole{job}")

    for piece in range(2):
        lo = piece * half_rows
        head_send(piece, nt(gpre[lo:lo + half_rows, :], wu[...]), 1)
    point("back2")
    for piece in range(2):
        lo = piece * half_rows
        head_send(piece, nn(hid[lo:lo + half_rows, :], wd[...]), 2)
    point("fed")

    def norm_back(hat, inv, gain, upstream):
        scaled = upstream * gain
        first = jnp.mean(scaled, axis=-1, keepdims=True)
        second = jnp.mean(scaled * hat, axis=-1, keepdims=True)
        return inv * (scaled - first - hat * second)

    def second_back(z, carry):
        gain_sum, shift_sum, bias_sum = carry
        at = chunk_rows(z)
        upstream = (send_h[1, z].astype(F32) + recv_h[1, z].astype(F32)).reshape(chunk, width)
        hat, inv = norm_stats(middle[at, :])
        dy = dyb[z].astype(F32).reshape(chunk, width)
        total = dy + norm_back(hat, inv, gain_two[...], upstream)
        grad_mid[at, :] = total
        n2[at, :] = total.astype(BF16)
        gain_sum = gain_sum + jnp.sum(upstream * hat, axis=0, keepdims=True)
        shift_sum = shift_sum + jnp.sum(upstream, axis=0, keepdims=True)
        bias_sum = bias_sum + jnp.sum(dy, axis=0, keepdims=True)
        return gain_sum, shift_sum, bias_sum

    zero_row = jnp.zeros((1, width), F32)
    sums = (zero_row, zero_row, zero_row)
    for piece in range(2):
        head_copy(piece, 1).wait()
        sums = lax.fori_loop(piece * groups // 2, (piece + 1) * groups // 2, second_back, sums)

    def keep_small(which, row):
        for c in range(width // WIDE):
            at = up_bias_rows + which * (width // WIDE) + c
            small[at:at + 1, :] = row[:, c * WIDE:(c + 1) * WIDE]

    keep_small(0, sums[2])
    keep_small(3, sums[0])
    keep_small(4, sums[1])
    for piece in range(2):
        head_copy(piece, 2).start()
    point("second_back")

    def attended_back(z, carry):
        at = chunk_rows(z)
        back = nt(n2[at, :], wo[...])
        at_q = pl.ds(pl.multiple_of(z * stack, stack), stack)
        for p in range(pairs):
            low = back[:, p * LANES:(p + 1) * LANES].astype(BF16)
            dos[p, at_q, :] = stack_heads(low)
            at_o = pl.ds(pl.multiple_of(z * stack, stack), chunk)
            prod = jnp.transpose(low.astype(F32)) * dq_t[p, :, at_o]
            d0 = jnp.sum(prod[:HD], axis=0, keepdims=True)
            d1 = jnp.sum(prod[HD:], axis=0, keepdims=True)
            deltas[p, :, at_q] = jnp.concatenate([d0, d1], axis=1)
        return carry

    lax.fori_loop(0, groups, attended_back, 0)
    point("att_back")

    def feed_out(z, carry):
        at = chunk_rows(z)
        fed = (send_h[0, z].astype(F32) + recv_h[0, z].astype(F32)).reshape(chunk, width)
        dyb[z] = (middle[at, :] + fed + bias_down[...]).astype(BF16).reshape(2, span, width)
        return carry

    for piece in range(2):
        head_copy(piece, 2).wait()
    lax.fori_loop(0, groups, feed_out, 0)

    point("feed_out")
    def spread(buf, out, ssem, rsem, psend, precv):
        copies, passes = [], []
        own = pltpu.make_async_copy(buf.at[group], out.at[group], ssem.at[0])
        own.start()
        for step in range(1, groups):
            to = group_peer(step)
            source = group_peer(groups - step)
            copies.append(
                remote(buf.at[to, :, share], out.at[group, :, share], ssem.at[step], rsem.at[step], peer(to * inner + rank))
            )
            passes.append(remote(out.at[source, :, share], out.at[source, :, share], psend.at[step], precv.at[step], sibling))
        for copy in copies:
            copy.start()
        return own, copies, passes

    def pass_on(spread_out):
        own, copies, passes = spread_out
        own.wait()
        for copy, onward in zip(copies, passes):
            copy.wait()
            onward.start()

    y_spread = spread(dyb, y_out, y_send, y_recv, yf_send, yf_recv)


    wout = tn(att[...], n2[...])
    for c in range(col_tiles):
        at = bases[2] + c * head_width
        acc[at:at + head_width, :] = wout[:, c * LANES:(c + 1) * LANES].astype(BF16)
    point("wout")

    def noisy_back(p, carry):
        for index in range(groups):
            at = slice(index * stack, (index + 1) * stack)
            q = qs[p, at, :]
            do = dos[p, at, :]
            keys = kvn[index, p]
            s = nt(keys, q)
            s = jnp.where(noisy_mask(s.shape), s, NEG)
            e = jnp.exp(s - lses[p, :, at])
            dp = nt(kvn[index, pairs + p], do)
            ds = (e * (dp - deltas[p, :, at])).astype(BF16)
            at_n = slice(index * span, (index + 1) * span)
            cols = pl.multiple_of(head_width + p * LANES, LANES)
            gpre[at_n, pl.ds(cols, LANES)] = turn_back(nn(ds, q), tables(index * inner + rank)).astype(BF16)
            cols = pl.multiple_of(2 * head_width + p * LANES, LANES)
            gpre[at_n, pl.ds(cols, LANES)] = nn(e.astype(BF16), do).astype(BF16)
            dq_t[p, :, at] = tn(keys, ds)
        return carry

    lax.fori_loop(0, pairs, noisy_back, 0)
    point("noisy")

    for index in range(groups):
        for block in range(key_blocks):
            first = index * inner + block * key_ranks

            def clean_back(p, carry, index=index, block=block, first=first):
                at = slice(index * stack, groups * stack)
                q = qs[p, at, :]
                do = dos[p, at, :]
                keys = kv[first:first + key_ranks, p].reshape(key_ranks * span, LANES)
                vals = kv[first:first + key_ranks, pairs + p].reshape(key_ranks * span, LANES)
                s = nt(keys, q)
                own = s[:, :stack]
                own = jnp.where(clean_mask(index, block * key_ranks, key_ranks, own.shape), own, NEG)
                if index < groups - 1:
                    s = jnp.concatenate([own, s[:, stack:]], axis=1)
                else:
                    s = own
                e = jnp.exp(s - lses[p, :, at])
                dp = nt(vals, do)
                ds = (e * (dp - deltas[p, :, at])).astype(BF16)
                dv = nn(e.astype(BF16), do).astype(BF16)
                dk = turn_back(nn(ds, q), many(first, key_ranks)).astype(BF16)
                dq_t[p, :, at] += tn(keys, ds)
                kv[first:first + key_ranks, p] = dk.reshape(key_ranks, span, LANES)
                kv[first:first + key_ranks, pairs + p] = dv.reshape(key_ranks, span, LANES)
                return carry

            if index < groups // 2:
                for p in range(pairs):
                    clean_back(p, 0)
                    point(f"g{index}p{p}")
            else:
                lax.fori_loop(0, pairs, clean_back, 0)
                point(f"g{index}")

    def query_grads(index, carry):
        at = chunk_rows(index)
        at_q = pl.ds(pl.multiple_of(index * stack, stack), stack)
        table = twice(tables(index * inner + rank))
        for p in range(pairs):
            gq = jnp.transpose(merge_heads(dq_t[p, :, at_q])) * scale
            gpre[at, p * LANES:(p + 1) * LANES] = turn_back(gq, table).astype(BF16)
        return carry

    def keep_heads(part, base):
        for p in range(part.shape[1] // LANES):
            at = base + p * width
            acc[at:at + width, :] = part[:, p * LANES:(p + 1) * LANES].astype(BF16)

    lax.fori_loop(0, groups, query_grads, 0)
    point("qg")
    keep_heads(tn(n1[...].reshape(rows, width), gpre[:, :head_width]), query_base)
    begin(2)
    point("hq")
    sweep = min(n, 16)
    many_rows = sweep * span
    widths = 2 * pairs if n <= 16 else pairs
    for lead in range(0, 2 * pairs, widths):
        at = head_width + lead * LANES
        part = tn(n1[:, 0].reshape(groups * span, width), gpre[:groups * span, at:at + widths * LANES])
        for first in range(0, n, sweep):
            gates = jnp.concatenate(
                [kv[first:first + sweep, lead + i].reshape(many_rows, LANES) for i in range(widths)], axis=1
            )
            part = part + tn(nc[first:first + sweep].reshape(many_rows, width), gates)
        keep_heads(part, bases[3] + lead * width)
    begin(3)
    point("hk")

    def clean_input(block, carry):
        at = pl.ds(block * key_ranks, key_ranks)
        total = None
        for kind in range(2):
            gates = jnp.concatenate(
                [kv[at, kind * pairs + p].reshape(key_ranks * span, LANES) for p in range(pairs)], axis=1
            )
            back = nt(gates, wh[kind + 1])
            total = back if total is None else total + back
        nc[at] = total.astype(BF16).reshape(key_ranks, span, width)
        return carry

    lax.fori_loop(0, n // key_ranks, clean_input, 0)
    core_copy = remote(nc.at[:, other_share], core_part, k_send.at[0], k_recv.at[0], sibling)
    core_copy.start()
    point("clean_in")


    for piece in range(2):
        lo = piece * half_rows
        back = nt(gpre[lo:lo + half_rows, :head_width], wh[0]).reshape(groups // 2, 2, span, width)
        lo = lo // 2
        extra = nt(gpre[lo:lo + half_rows // 2, head_width:2 * head_width], wh[1])
        extra = extra + nt(gpre[lo:lo + half_rows // 2, 2 * head_width:3 * head_width], wh[2])
        extra = extra.reshape(groups // 2, span, width)
        at = slice(piece * groups // 2, (piece + 1) * groups // 2)
        send_h[1, at, 0] = (back[:, 0] + extra).astype(BF16)
        send_h[1, at, 1] = back[:, 1].astype(BF16)
        head_copy(piece, 3).start()
    point("back1")
    core_copy.wait()

    def core_add(slot, carry):
        nc[slot, share] = (nc[slot, share].astype(F32) + core_part[slot].astype(F32)).astype(BF16)
        return carry

    lax.fori_loop(0, n, core_add, 0)
    point("core_add")

    def part_copy(index, near):
        dest = plane_peer(near)
        return remote(
            nc.at[index * inner + dest, share], plane_part.at[index, near - 1], g_send.at[index, near],
            g_recv.at[index, near], peer(group * inner + dest),
        )

    for index in range(groups):
        for near in range(1, inner):
            part_copy(index, near).start()
    point("plane")
    for index in range(groups):
        for near in range(1, inner):
            part_copy(index, near).wait()

    def clean_add(index, carry):
        total = nc[index * inner + rank, share].astype(F32)
        for near in range(inner - 1):
            total = total + plane_part[index, near].astype(F32)
        clean_sum[index, share] = total.astype(BF16)
        return carry

    lax.fori_loop(0, groups, clean_add, 0)
    sum_copy = remote(clean_sum.at[:, share], clean_sum.at[:, share], k_send.at[1], k_recv.at[1], sibling)
    sum_copy.start()
    point("clean_add")
    sum_copy.wait()
    point("sum")

    def first_back(z, carry):
        gain_sum, shift_sum = carry
        at = chunk_rows(z)
        clean = clean_sum[z].astype(F32)
        upstream = (send_h[1, z].astype(F32) + recv_h[1, z].astype(F32)).reshape(chunk, width)
        upstream = upstream + jnp.concatenate([jnp.zeros_like(clean), clean], axis=0)
        hat, inv = norm_stats(xb[z].astype(F32).reshape(chunk, width))
        total = grad_mid[at, :] + norm_back(hat, inv, gain_one[...], upstream)
        dyb[z] = total.astype(BF16).reshape(2, span, width)
        gain_sum = gain_sum + jnp.sum(upstream * hat, axis=0, keepdims=True)
        shift_sum = shift_sum + jnp.sum(upstream, axis=0, keepdims=True)
        return gain_sum, shift_sum

    pass_on(y_spread)
    sums = (zero_row, zero_row)
    for piece in range(2):
        head_copy(piece, 3).wait()
        sums = lax.fori_loop(piece * groups // 2, (piece + 1) * groups // 2, first_back, sums)
    ig_spread = spread(dyb, ig_out, i_send, i_recv, if_send, if_recv)
    keep_small(1, sums[0])
    keep_small(2, sums[1])

    def small_job():
        for bit in range(bits):
            copy = remote(small.at[...], small_r.at[bit], sm_send.at[bit], sm_recv.at[bit], partner(bit))
            copy.start()
            yield
            copy.wait()
            small[...] = small[...] + small_r[bit]

    jobs.append([small_job()])
    begin(4)
    point("first_back")
    pass_on(ig_spread)
    point("ig")
    while any(steps.gi_frame is not None for job in jobs for steps in job):
        take_round()
    small_out[...] = small[...]
    for copy in clean_copies + noisy_copies + c_copies:
        copy.wait_send()
    for onward in y_spread[2] + ig_spread[2]:
        onward.wait()
    for copy in copies:
        copy.wait()


def widen(count, *refs):
    sources, small, targets = refs[:count], refs[count], refs[count + 1:]
    for source, target in zip(sources, targets):
        target[...] = source[...].astype(target.dtype)
    row = 0
    for target in targets[count:]:
        for i in range(target.shape[0] // WIDE):
            target[i * WIDE:(i + 1) * WIDE] = small[row]
            row += 1


def local(
    layer_input, block_sizes, mixing_gain, mixing_shift, w_heads, w_output, feed_gain, feed_shift,
    w_up, bias_up, w_down, bias_down, cotangent,
):
    groups, _, span, width = layer_input.shape
    n = lax.axis_size("seq")
    head_width = w_heads.shape[2]
    hidden = w_up.shape[1]
    inner = n // groups
    pairs = head_width // LANES
    chunk = 2 * span
    rows = groups * chunk
    stack = 2 * chunk
    bits = int(math.log2(n))
    job_rows, bases = job_layout(n, width, head_width, hidden)
    small_rows = (hidden // WIDE + 5 * (width // WIDE) + 7) // 8 * 8
    out_copies = 2 * (width // LANES) + hidden // LANES + 3 * pairs + width // LANES
    anywhere = pl.BlockSpec(memory_space=pl.ANY)
    vmem = pl.BlockSpec(memory_space=pltpu.VMEM)
    dma = pltpu.SemaphoreType.DMA
    own = pltpu.VMEM((groups, 2, span, width), BF16)
    scratch = [
        pltpu.VMEM((3, width, head_width), BF16),
        pltpu.VMEM((head_width, width), BF16),
        pltpu.VMEM((width, hidden), BF16),
        pltpu.VMEM((hidden, width), BF16),
        own,
        own,
        own,
        pltpu.VMEM((rows, width), BF16),
        pltpu.VMEM((n, span, width), BF16),
        pltpu.VMEM((pairs, groups * stack, LANES), BF16),
        pltpu.VMEM((pairs, groups * stack, LANES), BF16),
        pltpu.VMEM((n, 2 * pairs, span, LANES), BF16),
        pltpu.VMEM((groups, 2 * pairs, span, LANES), BF16),
        pltpu.VMEM((pairs, 1, groups * stack), F32),
        pltpu.VMEM((pairs, 1, groups * stack), F32),
        pltpu.VMEM((rows, head_width), BF16),
        pltpu.VMEM((rows, width), F32),
        pltpu.VMEM((rows, hidden), BF16),
        pltpu.VMEM((rows, hidden), BF16),
        pltpu.VMEM((2, groups, 2, span, width), BF16),
        pltpu.VMEM((2, groups, 2, span, width), BF16),
        pltpu.VMEM((rows, width), F32),
        pltpu.VMEM((pairs, LANES, groups * stack), F32),
        pltpu.VMEM((n, span // 2, width), BF16),
        pltpu.VMEM((groups, inner - 1, span // 2, width), BF16),
        pltpu.VMEM((groups, span, width), BF16),
        pltpu.VMEM((bases[-1], LANES), BF16),
        pltpu.VMEM((bases[-1], LANES), BF16),
        pltpu.VMEM((small_rows, WIDE), F32),
        pltpu.VMEM((bits, small_rows, WIDE), F32),
        pltpu.VMEM((n, LANES), F32),
        pltpu.VMEM((n, LANES), F32),
        pltpu.VMEM((span, LANES), F32),
        pltpu.VMEM((span, LANES), F32),
        pltpu.VMEM((-(-hidden // WIDE // 8) * 8, WIDE), F32),
        pltpu.VMEM((8, width), F32),
        dma((6,)),
        *[dma((groups,))] * 12,
        dma((groups, inner)), dma((groups, inner)), dma((groups,)), dma((groups,)), dma((groups,)),
        dma((4, 2)), dma((4, 2)),
        dma((groups, inner)), dma((groups, inner)), dma((2,)), dma((2,)),
        *[dma((groups,))] * 8,
        dma((4, 8, 2 * bits)), dma((4, 8, 2 * bits)), pltpu.SemaphoreType.REGULAR((4, 8, bits)),
        dma((bits,)), dma((bits,)),
        dma((out_copies,)),
    ]
    out_shape = (
        jax.ShapeDtypeStruct((groups, 2, span, width), BF16),
        jax.ShapeDtypeStruct((groups, 2, span, width), BF16),
        jax.ShapeDtypeStruct((hidden, width), BF16),
        jax.ShapeDtypeStruct((width, hidden), BF16),
        jax.ShapeDtypeStruct((3, width, head_width), BF16),
        jax.ShapeDtypeStruct((head_width, width), BF16),
        jax.ShapeDtypeStruct((small_rows, WIDE), F32),
    )
    y, ig, down, up, heads, wout, small = pl.pallas_call(
        functools.partial(fused, (n, groups, span, width, head_width, hidden)),
        out_shape=out_shape,
        in_specs=[anywhere] * 6 + [pl.BlockSpec(memory_space=pltpu.SMEM)] + [vmem] * 6,
        out_specs=(anywhere,) * 6 + (vmem,),
        scratch_shapes=scratch,
        compiler_params=pltpu.CompilerParams(
            collective_id=0, has_side_effects=True, vmem_limit_bytes=VMEM_BYTES
        ),
    )(
        layer_input,
        cotangent,
        w_heads, w_output, w_up, w_down, block_sizes,
        mixing_gain, mixing_shift, feed_gain, feed_shift, bias_up, bias_down,
    )
    full = (groups, 2, span, width)
    steps = 2
    sources = (y.reshape(rows, width), ig.reshape(rows, width), heads, wout, up, down)
    kinds = (BF16,) + (F32,) * 5
    specs = []
    for source in sources:
        shape = source.shape
        block = shape[:-2] + (shape[-2] // steps, shape[-1])
        specs.append(pl.BlockSpec(block, lambda i, lead=len(shape) - 2: (0,) * lead + (i, 0)))
    vector_sizes = (hidden,) + (width,) * 5
    y, ig, heads, wout, up, down, *vectors = pl.pallas_call(
        functools.partial(widen, len(sources)),
        grid=(steps,),
        out_shape=tuple(jax.ShapeDtypeStruct(a.shape, kind) for a, kind in zip(sources, kinds))
        + tuple(jax.ShapeDtypeStruct((size,), F32) for size in vector_sizes),
        in_specs=specs + [pl.BlockSpec(small.shape, lambda i: (0, 0))],
        out_specs=tuple(specs) + tuple(pl.BlockSpec((size,), lambda i: (0,)) for size in vector_sizes),
        compiler_params=pltpu.CompilerParams(vmem_limit_bytes=VMEM_BYTES),
    )(*sources, small)
    return (y.reshape(full), ig.reshape(full), heads, wout, up, vectors[0], down, *vectors[1:])


def solution(mesh):
    in_specs = (
        P(None, None, "seq", None), P(), P(), P(), P(None, None, "head"), P("head", None), P(), P(),
        P(None, "head"), P("head"), P("head", None), P(), P(None, None, "seq", None),
    )
    out_specs = (
        P(None, None, "seq", None), P(None, None, "seq", None), P(None, None, "head"), P("head", None),
        P(None, "head"), P("head"), P("head", None), P(), P(), P(), P(), P(),
    )
    return jax.shard_map(local, mesh=mesh, in_specs=in_specs, out_specs=out_specs, check_vma=False)
```
